512 devices in a mesh: visit: 32 (over z, x_lo), patch: 16 (over x_hi, y, core).
Axes of the slice: x: 4 (x_hi: 2, x_lo: 2; x = x_hi * 2 + x_lo), y: 4, z: 16, core: 2. Of those that a mesh axis runs over, the one named last changes fastest.
Arguments:
- templates: float32 [32, 2, 256, 1024], P('visit', None, 'patch'), may hold values from -16 to 16, as said below
- owners: int32 [2], replicated, may hold values from 0 to 31, as said below
- science: float32 [2, 32, 256, 1024], P(None, 'visit', 'patch'), may hold values from -40 to 40
- sci_var: float32 [2, 32, 256, 1024], P(None, 'visit', 'patch'), may hold values from 0.03 to 0.3
- bad_pixels: int32 [2, 32, 256, 1024], P(None, 'visit', 'patch'), may hold values 0 or 1
Outputs:
- significance: float32 [2, 32, 256, 1024], P(None, 'visit', 'patch')
The draws below stay inside these ranges and needn't reach their ends.
Inputs may be any that keep to these rules, and one draw needn't show every extreme that they name: `owners`: the steps' entries are distinct indices of stored tiles, one of them always 32 - 1. `templates`: variances (index 1) lie in 0.01 to 0.1.
All inputs are finite; a program needn't handle non-finite values. No bound on the sum of `bad_pixels` on one device may be relied on, other than what follows from the above.
Results may differ from the reference program's by a relative error of at most 0.0003.
Values sent between devices are 32-bit elements; how exact they have to be, the bound alone decides.
A program may use at most 64 MiB of HBM per device.

```python
import math
import jax
import jax.numpy as jnp
import numpy as np
from jax import lax

COLS = 1024
NPROF = 5
RAD = 10
STEPS = 2
ROWS = 256
VISITS = 32
TEMPLATES = 32


def template_stack(key):
    image_key, var_key = jax.random.split(jax.random.fold_in(key, 11))
    position = jnp.arange(ROWS).astype(jnp.float32) / ROWS
    row_scale = jnp.exp(position * math.log(3.0))
    image = jax.random.truncated_normal(image_key, -4.0, 4.0, (TEMPLATES, ROWS, COLS), jnp.float32) * row_scale[None, :, None]
    variance = jnp.exp(jax.random.uniform(var_key, (TEMPLATES, ROWS, COLS), jnp.float32, math.log(0.01), math.log(0.1)))
    return jnp.stack([image, variance], axis=1)


def owner_list(key):
    first_key, order_key = jax.random.split(jax.random.fold_in(key, 23))
    chosen = jax.random.permutation(first_key, TEMPLATES - 1)[:STEPS - 1]
    listed = jnp.concatenate([chosen.astype(jnp.int32), jnp.full((1,), TEMPLATES - 1, jnp.int32)])
    order = jax.random.permutation(order_key, STEPS)
    return listed[order].astype(jnp.int32)


def draw_templates(key, part):
    return template_stack(key)


def draw_owners(key, part):
    return owner_list(key)


def draw_science(key, part):
    stored = template_stack(key)[:, 0]
    chosen = stored[owner_list(key)]
    keys = jax.random.split(jax.random.fold_in(key, 37), 3)
    level = jax.random.uniform(keys[0], (3, STEPS, VISITS), jnp.float32, -0.3, 0.3)
    level = level + jnp.array([0.8, 0.0, 0.0], jnp.float32)[:, None, None]
    slope = jax.random.uniform(keys[1], (3, STEPS, VISITS), jnp.float32, -0.4, 0.4)
    position = jnp.arange(ROWS).astype(jnp.float32) / ROWS - 0.5
    factor = level[..., None] + slope[..., None] * position
    col_shift = jnp.roll(chosen, 1, axis=2)
    row_shift = jnp.roll(chosen, 2, axis=1)
    mixed = factor[0][..., None] * chosen[:, None] + factor[1][..., None] * col_shift[:, None] + factor[2][..., None] * row_shift[:, None]
    noise = 0.3 * jax.random.truncated_normal(keys[2], -4.0, 4.0, (STEPS, VISITS, ROWS, COLS), jnp.float32)
    return mixed + noise


def set_ends(result, stream_key, least, high):
    longest = result.shape.index(max(result.shape))
    spots = []
    for shift in (0, 1):
        where = [jax.random.randint(jax.random.fold_in(stream_key, axis), (), 0, length) for axis, length in enumerate(result.shape)]
        where[longest] = (where[longest] + shift) % result.shape[longest]
        spots.append(tuple(where))
    return result.at[spots[0]].set(least).at[spots[1]].set(high)


def steps_of(own_key, extent, shards, smallest, largest):
    loudness, own = 1.0, jax.random.fold_in(own_key, 6)
    for axis_at, shards_of in shards:
        heights = jnp.exp(jax.random.uniform(jax.random.fold_in(own, axis_at), (shards_of,), jnp.float32, smallest / len(shards), largest / len(shards)))
        loudness = loudness * jnp.repeat(heights, extent[axis_at] // shards_of).reshape([-1 if axis == axis_at else 1 for axis in range(len(extent))])
    return loudness


def setup_inputs(seed: int = 0) -> dict:
    streams_of = jax.random.split(jax.random.key(seed), 6)
    return {
        "templates": draw_templates(jax.random.fold_in(streams_of[5], 71), 0),
        "owners": draw_owners(jax.random.fold_in(streams_of[5], 71), 0),
        "science": draw_science(jax.random.fold_in(streams_of[5], 71), 0),
        "sci_var": jnp.clip(jnp.exp(math.log(0.3) - 2.3025852 * jax.random.uniform(streams_of[3], (STEPS, VISITS, ROWS, COLS), jnp.float32) ** steps_of(streams_of[3], (STEPS, VISITS, ROWS, COLS), ((1, 32), (2, 16)), -0.2, 0.2)), 0.03, 0.3),
        "bad_pixels": set_ends((jax.random.randint(streams_of[4], (STEPS, VISITS, ROWS, COLS), 0, 16) < 1).astype(jnp.int32), jax.random.fold_in(streams_of[4], 1), 0, 1),
    }


ridge = 1.0

def profile_table():
    offsets = np.arange(-RAD, RAD + 1) * 1.0
    recipe = [(1.0, 0), (1.5, 1), (2.0, 2), (3.0, 0), (4.0, 1)]
    profiles = []
    for spread, degree in recipe[:NPROF]:
        profile = offsets ** degree * np.exp(-offsets * offsets / (2.0 * spread * spread))
        for earlier in profiles:
            profile = profile - np.dot(earlier, profile) * earlier
        profile = profile / np.sqrt(np.dot(profile, profile))
        profiles.append(profile)
    return np.stack(profiles)

def basis_images(extended):
    profiles = jnp.asarray(profile_table(), jnp.float32)
    height = extended.shape[0] - 2 * RAD
    across = extended.shape[1]
    widened = jnp.pad(extended, ((0, 0), (RAD, RAD)))
    columns = jnp.zeros((NPROF, extended.shape[0], across), jnp.float32)
    for offset in range(2 * RAD + 1):
        columns = columns + profiles[:, offset, None, None] * widened[None, :, offset:offset + across]
    images = jnp.zeros((NPROF, NPROF, height, across), jnp.float32)
    for offset in range(2 * RAD + 1):
        images = images + profiles[None, :, offset, None, None] * columns[:, None, offset:offset + height, :]
    return images.reshape(NPROF * NPROF, height, across)

def solve_kernel(normal_mat, normal_rhs):
    count = normal_mat.shape[0]
    factor = jnp.linalg.cholesky(normal_mat + ridge * jnp.eye(count, dtype=jnp.float32))
    return jax.scipy.linalg.cho_solve((factor, True), normal_rhs)

def reference(templates, owners, science, sci_var, bad_pixels):
    results = []
    for current in range(STEPS):
        arrived = templates[owners[current]]
        extended = jnp.pad(arrived[0], ((RAD, RAD), (0, 0)))
        images = basis_images(extended)
        flattened = images.reshape(NPROF * NPROF, -1)
        tile_var = arrived[1]

        def fit_visit(pieces):
            image_sci, var_sci, bad_one = pieces
            usable = (1 - bad_one).astype(jnp.float32)
            noise_var = var_sci + tile_var
            weight = usable / noise_var
            normal_mat = jnp.dot((images * weight[None]).reshape(NPROF * NPROF, -1), flattened.T, precision=lax.Precision.HIGHEST)
            normal_rhs = jnp.dot(flattened, (weight * image_sci).reshape(-1), precision=lax.Precision.HIGHEST)
            kernel_coef = solve_kernel(normal_mat, normal_rhs)
            fitted = jnp.dot(kernel_coef, flattened, precision=lax.Precision.HIGHEST).reshape(image_sci.shape)
            return usable * (image_sci - fitted) / jnp.sqrt(noise_var)
        results.append(lax.map(fit_visit, (science[current], sci_var[current], bad_pixels[current])))
    return jnp.stack(results)
```

```python
import functools

import jax
import jax.numpy as jnp
import ml_dtypes
import numpy as np
from jax import lax
from jax.experimental import pallas as pl
from jax.experimental.pallas import tpu as pltpu
from jax.sharding import PartitionSpec as P

NPROF = 5
RAD = 10
STEPS = 2
RIDGE = 1.0

GROUP = 8
NGROUPS = 4
NPATCH = 16
SLOT = 7
FIXED = 31
ROWS = 16
LANES = 128
NBLOCKS = 8
SCI = 5
MESH = pl.DeviceIdType.MESH

PARTS = (
    (0, 1, 6, 7, 0),
    (1, 1, 13, 3, 0),
    (1, 0, 0, 3, 3),
    (2, 0, 3, 7, 0),
    (3, 0, 10, 6, 0),
    (4, -1, 0, 7, 0),
    (5, -1, 7, 3, 0),
    (5, 0, 16, 3, 4),
    (6, 0, 19, 7, 0),
    (7, 0, 26, 6, 0),
)
VAR_AT = 39
POSITIONS = 40


def image_positions():
    return list(range(0, 13)) + list(range(14, 27)) + list(range(28, 38))


def profile_table():
    offsets = np.arange(-RAD, RAD + 1) * 1.0
    recipe = [(1.0, 0), (1.5, 1), (2.0, 2), (3.0, 0), (4.0, 1)]
    profiles = []
    for spread, degree in recipe[:NPROF]:
        profile = offsets**degree * np.exp(-offsets * offsets / (2.0 * spread * spread))
        for earlier in profiles:
            profile = profile - np.dot(earlier, profile) * earlier
        profile = profile / np.sqrt(np.dot(profile, profile))
        profiles.append(profile)
    return np.stack(profiles)


def column_table():
    prof = profile_table().astype(np.float32)
    table = np.zeros((2 * LANES, NPROF * LANES), np.float32)
    for k in range(NPROF):
        for n in range(LANES):
            first = n + LANES // 2 - RAD
            table[first : first + 2 * RAD + 1, k * LANES + n] = prof[k]
    return table


def split3(x):
    high = x.astype(ml_dtypes.bfloat16).astype(np.float32)
    mid = (x - high).astype(ml_dtypes.bfloat16).astype(np.float32)
    low = (x - high - mid).astype(ml_dtypes.bfloat16).astype(np.float32)
    return high, mid, low


def row_table():
    prof = profile_table().astype(np.float32)
    places = image_positions()
    table = np.zeros((ROWS * 8, POSITIONS), np.float32)
    for h in range(ROWS):
        for l in range(NPROF):
            for a in range(2 * RAD + 1):
                table[h * 8 + l, places[h + a]] = prof[l, a]
    high, mid, low = split3(table)
    return np.concatenate([high, high, high, mid, mid, low], axis=1).astype(ml_dtypes.bfloat16)


def rounded(x):
    return x.astype(jnp.bfloat16).astype(jnp.float32)


def normal_part(slot, step, ag, ag_flat, cols, basis, col_ref, row_ref, sci_ref, svar_ref, bad_ref):
    x = ag[slot, 0:POSITIONS]
    y = pltpu.roll(x, LANES // 2, 2)
    lane = lax.broadcasted_iota(jnp.int32, y.shape, 2)
    block = lax.broadcasted_iota(jnp.int32, y.shape, 1)
    before = jnp.where(block == 0, 0.0, pltpu.roll(y, 1, 1))
    after = jnp.where(block == NBLOCKS - 1, 0.0, pltpu.roll(y, NBLOCKS - 1, 1))
    low = lane < LANES // 2
    left = jnp.where(low, before, y).reshape(POSITIONS * NBLOCKS, LANES)
    right = jnp.where(low, y, after).reshape(POSITIONS * NBLOCKS, LANES)
    window = jnp.concatenate([left, right], axis=1)
    for k in range(NPROF):
        cols[k * POSITIONS * NBLOCKS : (k + 1) * POSITIONS * NBLOCKS, :] = jnp.dot(
            window,
            col_ref[:, k * LANES : (k + 1) * LANES],
            precision=lax.Precision.HIGHEST,
            preferred_element_type=jnp.float32,
        )

    def one_block(b, total):
        at = pl.multiple_of(b * LANES, LANES)
        c = jnp.concatenate(
            [
                cols[pl.ds(k * POSITIONS * NBLOCKS + b, POSITIONS, stride=NBLOCKS), :]
                for k in range(NPROF)
            ],
            axis=1,
        )
        high = rounded(c)
        rest = c - high
        mid = rounded(rest)
        low = rest - mid
        stacked = jnp.concatenate([high, mid, low, high, mid, high], axis=0).astype(jnp.bfloat16)
        d = jnp.dot(row_ref[...], stacked, preferred_element_type=jnp.float32)
        science = sci_ref[step, :, pl.ds(at, LANES)]
        usable = (1 - bad_ref[step, :, pl.ds(at, LANES)]).astype(jnp.float32)
        tile_var = ag_flat[pl.ds((slot * 56 + VAR_AT) * NBLOCKS + b, ROWS, stride=NBLOCKS), :]
        weight = usable / (svar_ref[step, :, pl.ds(at, LANES)] + tile_var)
        spread = jnp.broadcast_to(weight[:, None, :], (ROWS, 8, LANES)).reshape(ROWS * 8, LANES)
        sci_spread = jnp.broadcast_to(science[:, None, :], (ROWS, 8, LANES)).reshape(ROWS * 8, LANES)
        place = lax.broadcasted_iota(jnp.int32, (ROWS * 8, LANES), 0) & 7
        first = jnp.where(place == SCI, sci_spread, d[:, 0:LANES])
        parts = [first] + [d[:, k * LANES : (k + 1) * LANES] for k in range(1, NPROF)]
        for k in range(NPROF):
            basis[slot, b, :, k * LANES : (k + 1) * LANES] = parts[k]

        def arranged(pieces):
            return jnp.concatenate(
                [
                    jnp.concatenate([piece[h * 8 : h * 8 + 8] for piece in pieces], axis=0)
                    for h in range(ROWS)
                ],
                axis=1,
            )

        def two(pieces):
            highs = [rounded(piece) for piece in pieces]
            rests = [piece - h for piece, h in zip(pieces, highs)]
            return arranged(highs + rests).astype(jnp.bfloat16)

        right = two(parts)
        left = two([piece * spread for piece in parts])
        product = lax.dot_general(
            left, right, (((1,), (1,)), ((), ())), preferred_element_type=jnp.float32
        )
        return total + product

    total = lax.fori_loop(0, NBLOCKS, one_block, jnp.zeros((80, 80), jnp.float32))
    full = total[0:40, 0:40] + total[0:40, 40:80] + total[40:80, 0:40] + total[40:80, 40:80]
    return full


def solve(mats):
    row = lax.broadcasted_iota(jnp.int32, (40, LANES), 0)
    col = lax.broadcasted_iota(jnp.int32, (40, LANES), 1)
    mats = [m + jnp.where(row == col, RIDGE, 0.0) for m in mats]
    for k in range(NPROF):
        for l in range(NPROF):
            p = k * 8 + l
            for s in range(STEPS):
                m = mats[s]
                pivot = m[p : p + 1, :] / m[p : p + 1, p : p + 1]
                mats[s] = jnp.where(row == p, pivot, m - m[:, p : p + 1] * pivot)
    return [
        jnp.where(row == SCI, -1.0, jnp.broadcast_to(m[:, SCI : SCI + 1], (40, LANES)))
        for m in mats
    ]


def kernel(
    owners, temp_ref, sci_ref, svar_ref, bad_ref, col_ref, row_ref, out_ref,
    mine, recv1, send2, recv2, ag, red, cols, basis,
    ssem1, same_sem, cross_sem, ssem2, rsem2, static_send, static_recv, ssem3, rsem3, ssem4, rsem4,
):
    v = lax.axis_index("visit")
    p = lax.axis_index("patch")
    group = v // GROUP
    cls = v % GROUP

    def peer(t):
        return group * GROUP + t

    recv1[...] = jnp.zeros_like(recv1)
    flat = mine.reshape(2 * ROWS * NBLOCKS, LANES)
    for kind in range(2):
        for half in range(2):
            for b in range(NBLOCKS):
                flat[pl.ds((kind * ROWS + half * 8) * NBLOCKS + b, 8, stride=NBLOCKS), :] = temp_ref[
                    kind, half * 8 : half * 8 + 8, b * LANES : (b + 1) * LANES
                ]

    barrier = pltpu.get_barrier_semaphore()

    def greet(vv, pp):
        pl.semaphore_signal(barrier, inc=1, device_id=(vv, pp), device_id_type=MESH)

    for d in range(1, GROUP):
        greet(peer((cls + d) % GROUP), p)
    for d in range(1, NGROUPS):
        greet(((group + d) % NGROUPS) * GROUP + cls, p)
    for d in range(1, NPATCH):
        greet(v, (p + d) % NPATCH)

    @pl.when((cls < 2) & (p > 0))
    def _():
        for d in range(1, GROUP):
            greet(peer((cls + d) % GROUP), p - 1)

    @pl.when(((cls == 4) | (cls == 5)) & (p < NPATCH - 1))
    def _():
        for d in range(1, GROUP):
            greet(peer((cls + d) % GROUP), p + 1)

    below = jnp.where(p < NPATCH - 1, jnp.where(cls < 2, 1, 2), 0)
    above = jnp.where(p > 0, jnp.where((cls == 4) | (cls == 5), 1, 2), 0)
    pl.semaphore_wait(barrier, GROUP - 1 + NGROUPS - 1 + NPATCH - 1 + below + above)

    def first_copy(i):
        t, dp, at, n, to = PARTS[i]
        return pltpu.make_async_remote_copy(
            src_ref=mine.at[pl.ds(at, n)],
            dst_ref=recv1.at[pl.ds(cls * SLOT + to, n)],
            send_sem=ssem1.at[i],
            recv_sem=same_sem if dp == 0 else cross_sem,
            device_id=(peer(t), p + dp),
            device_id_type=MESH,
        )

    def sends(i):
        t, dp = PARTS[i][:2]
        if dp == 0:
            return cls != t
        return p < NPATCH - 1 if dp == 1 else p > 0

    for i in range(len(PARTS)):

        @pl.when(sends(i))
        def _(i=i):
            first_copy(i).start()

    for t, dp, at, n, to in PARTS:

        @pl.when(cls == t)
        def _(t=t, dp=dp, at=at, n=n, to=to):
            if dp == 0:
                recv1[pl.ds(t * SLOT + to, n)] = mine[pl.ds(at, n)]

    for t, dp, at, n, to in PARTS:
        if dp == 0:

            @pl.when(cls == t)
            def _(n=n):
                rows = recv1.at[pl.ds(0, (GROUP - 1) * n)]
                pltpu.make_async_copy(rows, rows, same_sem).wait()

        else:

            @pl.when((cls == t) & (p > 0 if dp == 1 else p < NPATCH - 1))
            def _(n=n):
                rows = recv1.at[pl.ds(0, GROUP * n)]
                pltpu.make_async_copy(rows, rows, cross_sem).wait()

    own = pl.ds(cls * SLOT, SLOT)
    fixed = pl.ds((FIXED % GROUP) * SLOT, SLOT)

    def static_copy(g):
        return pltpu.make_async_remote_copy(
            src_ref=recv1.at[fixed],
            dst_ref=ag.at[0, own],
            send_sem=static_send.at[g],
            recv_sem=static_recv,
            device_id=(g * GROUP + cls, p),
            device_id_type=MESH,
        )

    @pl.when(group == FIXED // GROUP)
    def _():
        for g in range(NGROUPS - 1):
            static_copy(g).start()
        ag[0, own] = recv1[fixed]

    other = owners[0] + owners[1] - FIXED
    chosen = recv1[pl.ds((other & 7) * SLOT, SLOT)]
    send2[...] = chosen
    recv2[pl.ds(group * SLOT, SLOT)] = chosen

    def second_copy(d):
        return pltpu.make_async_remote_copy(
            src_ref=send2,
            dst_ref=recv2.at[pl.ds(group * SLOT, SLOT)],
            send_sem=ssem2.at[d],
            recv_sem=rsem2.at[d],
            device_id=(((group + d) % NGROUPS) * GROUP + cls, p),
            device_id_type=MESH,
        )

    for d in (2, 1, 3):
        second_copy(d).start()

    def third_copy(slot, d):
        return pltpu.make_async_remote_copy(
            src_ref=ag.at[slot, own],
            dst_ref=ag.at[slot, own],
            send_sem=ssem3.at[slot, d],
            recv_sem=rsem3.at[slot],
            device_id=(peer((cls + d) % GROUP), p),
            device_id_type=MESH,
        )

    @pl.when(group != FIXED // GROUP)
    def _():
        pltpu.make_async_copy(ag.at[0, own], ag.at[0, own], static_recv).wait()

    for d in range(1, GROUP):
        third_copy(0, d).start()
    for d in range(1, NGROUPS):
        second_copy(d).wait_recv()
    ag[1, own] = recv2[pl.ds(((other >> 3) & 3) * SLOT, SLOT)]
    for d in range(1, GROUP):
        third_copy(1, d).start()

    ag_flat = ag.reshape(STEPS * 56 * NBLOCKS, LANES)
    fixed_step = jnp.where(owners[1] == FIXED, 1, 0)
    found = []
    for slot in range(STEPS):
        rows = ag.at[slot, pl.ds(0, (GROUP - 1) * SLOT)]
        pltpu.make_async_copy(rows, rows, rsem3.at[slot]).wait()
        step = fixed_step if slot == 0 else 1 - fixed_step
        found.append(
            normal_part(slot, step, ag, ag_flat, cols, basis, col_ref, row_ref, sci_ref, svar_ref, bad_ref)
        )
    wide = [jnp.concatenate([m, jnp.zeros((40, LANES - 40), jnp.float32)], axis=1) for m in found]
    red[p] = wide[0] + pltpu.roll(wide[1], 64, 1)

    def fourth_copy(d):
        return pltpu.make_async_remote_copy(
            src_ref=red.at[p],
            dst_ref=red.at[p],
            send_sem=ssem4.at[d],
            recv_sem=rsem4.at[d],
            device_id=(v, (p + d) % NPATCH),
            device_id_type=MESH,
        )

    for d in range(1, NPATCH):
        fourth_copy(d).start()
    for d in range(1, NPATCH):
        fourth_copy(d).wait_recv()
    total = red[0]
    for q in range(1, NPATCH):
        total = total + red[q]

    coefs = solve([total, pltpu.roll(total, 64, 1)])

    for step in range(STEPS):
        slot = jnp.where(fixed_step == step, 0, 1)
        coef = jnp.where(fixed_step == step, coefs[0], coefs[1])

        def one_block(b, carry, step=step, slot=slot, coef=coef):
            at = pl.multiple_of(b * LANES, LANES)
            sums = jnp.zeros((ROWS, 8, LANES), jnp.float32)
            for k in range(NPROF):
                d = basis[slot, b, :, k * LANES : (k + 1) * LANES].reshape(ROWS, 8, LANES)
                sums = sums + d * coef[k * 8 : k * 8 + 8][None]
            left = jnp.sum(sums, axis=1)
            usable = (1 - bad_ref[step, :, pl.ds(at, LANES)]).astype(jnp.float32)
            tile_var = ag_flat[pl.ds((slot * 56 + VAR_AT) * NBLOCKS + b, ROWS, stride=NBLOCKS), :]
            noise = svar_ref[step, :, pl.ds(at, LANES)] + tile_var
            out_ref[step, :, pl.ds(at, LANES)] = -(usable * left) / jnp.sqrt(noise)
            return carry

        lax.fori_loop(0, NBLOCKS, one_block, 0)

    for i in range(len(PARTS)):

        @pl.when(sends(i))
        def _(i=i):
            first_copy(i).wait_send()

    @pl.when(group == FIXED // GROUP)
    def _():
        for g in range(NGROUPS - 1):
            static_copy(g).wait_send()

    for d in range(1, NGROUPS):
        second_copy(d).wait_send()
    for slot in range(STEPS):
        for d in range(1, GROUP):
            third_copy(slot, d).wait_send()
    for d in range(1, NPATCH):
        fourth_copy(d).wait_send()


def shards(templates, owners, science, sci_var, bad_pixels):
    vmem = pl.BlockSpec(memory_space=pltpu.VMEM)
    row_shape = (NBLOCKS, LANES)
    dma = pltpu.SemaphoreType.DMA
    result = pl.pallas_call(
        kernel,
        out_shape=jax.ShapeDtypeStruct((STEPS, ROWS, NBLOCKS * LANES), jnp.float32),
        in_specs=[pl.BlockSpec(memory_space=pltpu.SMEM)] + [vmem] * 6,
        out_specs=vmem,
        scratch_shapes=[
            pltpu.VMEM((2 * ROWS, *row_shape), jnp.float32),
            pltpu.VMEM((GROUP * SLOT, *row_shape), jnp.float32),
            pltpu.VMEM((SLOT, *row_shape), jnp.float32),
            pltpu.VMEM((NGROUPS * SLOT, *row_shape), jnp.float32),
            pltpu.VMEM((STEPS, GROUP * SLOT, *row_shape), jnp.float32),
            pltpu.VMEM((NPATCH, 40, LANES), jnp.float32),
            pltpu.VMEM((NPROF * POSITIONS * NBLOCKS, LANES), jnp.float32),
            pltpu.VMEM((STEPS, NBLOCKS, ROWS * 8, NPROF * LANES), jnp.float32),
            dma((len(PARTS),)),
            dma,
            dma,
            dma((NGROUPS,)),
            dma((NGROUPS,)),
            dma((NGROUPS,)),
            dma,
            dma((STEPS, GROUP)),
            dma((STEPS,)),
            dma((NPATCH,)),
            dma((NPATCH,)),
        ],
        compiler_params=pltpu.CompilerParams(
            collective_id=0, has_side_effects=True, vmem_limit_bytes=32 * 1024 * 1024
        ),
        name="difference",
    )(
        owners,
        templates[0],
        science[:, 0],
        sci_var[:, 0],
        bad_pixels[:, 0],
        jnp.asarray(column_table()),
        jnp.asarray(row_table()),
    )
    return result[:, None]


def solution(mesh):
    return jax.shard_map(
        shards,
        mesh=mesh,
        in_specs=(
            P("visit", None, "patch", None),
            P(),
            P(None, "visit", "patch", None),
            P(None, "visit", "patch", None),
            P(None, "visit", "patch", None),
        ),
        out_specs=P(None, "visit", "patch", None),
        check_vma=False,
    )
```

```python
import functools

import jax
import jax.numpy as jnp
import ml_dtypes
import numpy as np
from jax import lax
from jax.experimental import pallas as pl
from jax.experimental.pallas import tpu as pltpu
from jax.sharding import PartitionSpec as P

NPROF = 5
RAD = 10
STEPS = 2
RIDGE = 1.0

GROUP = 8
NGROUPS = 4
NPATCH = 16
SLOT = 7
FIXED = 31
ROWS = 16
LANES = 128
NBLOCKS = 8
SCI = 5
MESH = pl.DeviceIdType.MESH

PARTS = (
    (0, 1, 6, 7, 0),
    (1, 1, 13, 3, 0),
    (1, 0, 0, 3, 3),
    (2, 0, 3, 7, 0),
    (3, 0, 10, 6, 0),
    (4, -1, 0, 7, 0),
    (5, -1, 7, 3, 0),
    (5, 0, 16, 3, 4),
    (6, 0, 19, 7, 0),
    (7, 0, 26, 6, 0),
)
VAR_AT = 39
POSITIONS = 40


def image_positions():
    return list(range(0, 13)) + list(range(14, 27)) + list(range(28, 38))


def profile_table():
    offsets = np.arange(-RAD, RAD + 1) * 1.0
    recipe = [(1.0, 0), (1.5, 1), (2.0, 2), (3.0, 0), (4.0, 1)]
    profiles = []
    for spread, degree in recipe[:NPROF]:
        profile = offsets**degree * np.exp(-offsets * offsets / (2.0 * spread * spread))
        for earlier in profiles:
            profile = profile - np.dot(earlier, profile) * earlier
        profile = profile / np.sqrt(np.dot(profile, profile))
        profiles.append(profile)
    return np.stack(profiles)


def column_table():
    prof = profile_table().astype(np.float32)
    table = np.zeros((2 * LANES, NPROF * LANES), np.float32)
    for k in range(NPROF):
        for n in range(LANES):
            first = n + LANES // 2 - RAD
            table[first : first + 2 * RAD + 1, k * LANES + n] = prof[k]
    high, mid, _ = split3(table)
    return np.concatenate([high, mid], axis=1).astype(ml_dtypes.bfloat16)


def split3(x):
    high = x.astype(ml_dtypes.bfloat16).astype(np.float32)
    mid = (x - high).astype(ml_dtypes.bfloat16).astype(np.float32)
    low = (x - high - mid).astype(ml_dtypes.bfloat16).astype(np.float32)
    return high, mid, low


def row_table():
    prof = profile_table().astype(np.float32)
    places = image_positions()
    table = np.zeros((ROWS * 8, POSITIONS), np.float32)
    for h in range(ROWS):
        for l in range(NPROF):
            for a in range(2 * RAD + 1):
                table[h * 8 + l, places[h + a]] = prof[l, a]
    high, mid, low = split3(table)
    return np.concatenate([high, high, high, mid, mid, low], axis=1).astype(ml_dtypes.bfloat16)


def rounded(x):
    return x.astype(jnp.bfloat16).astype(jnp.float32)


def normal_part(slot, step, ag, ag_flat, cols, basis, col_ref, row_ref, sci_ref, svar_ref, bad_ref):
    x = ag[slot, 0:POSITIONS]
    y = pltpu.roll(x, LANES // 2, 2)
    lane = lax.broadcasted_iota(jnp.int32, y.shape, 2)
    block = lax.broadcasted_iota(jnp.int32, y.shape, 1)
    before = jnp.where(block == 0, 0.0, pltpu.roll(y, 1, 1))
    after = jnp.where(block == NBLOCKS - 1, 0.0, pltpu.roll(y, NBLOCKS - 1, 1))
    low = lane < LANES // 2
    left = jnp.where(low, before, y).reshape(POSITIONS * NBLOCKS, LANES)
    right = jnp.where(low, y, after).reshape(POSITIONS * NBLOCKS, LANES)
    window = jnp.concatenate([left, right], axis=1)
    height = POSITIONS * NBLOCKS
    high = rounded(window)
    both = jnp.concatenate([high, window - high], axis=0).astype(jnp.bfloat16)
    for k in range(NPROF):
        table = col_ref[:, k * LANES : (k + 1) * LANES]
        rest = col_ref[:, (NPROF + k) * LANES : (NPROF + k + 1) * LANES]
        main = jnp.dot(both, table, preferred_element_type=jnp.float32)
        more = jnp.dot(both[0:height], rest, preferred_element_type=jnp.float32)
        cols[k * height : (k + 1) * height, :] = main[0:height] + (main[height:] + more)

    def one_block(b, total):
        at = pl.multiple_of(b * LANES, LANES)
        c = jnp.concatenate(
            [
                cols[pl.ds(k * height + b, POSITIONS, stride=NBLOCKS), :]
                for k in range(NPROF)
            ],
            axis=1,
        )
        high = rounded(c)
        rest = c - high
        mid = rounded(rest)
        low = rest - mid
        stacked = jnp.concatenate([high, mid, low, high, mid, high], axis=0).astype(jnp.bfloat16)
        d = jnp.dot(row_ref[...], stacked, preferred_element_type=jnp.float32)
        science = sci_ref[step, 0, :, pl.ds(at, LANES)]
        usable = (1 - bad_ref[step, 0, :, pl.ds(at, LANES)]).astype(jnp.float32)
        tile_var = ag_flat[pl.ds((slot * 56 + VAR_AT) * NBLOCKS + b, ROWS, stride=NBLOCKS), :]
        scale = usable / jnp.sqrt(svar_ref[step, 0, :, pl.ds(at, LANES)] + tile_var)
        spread = jnp.broadcast_to(scale[:, None, :], (ROWS, 8, LANES)).reshape(ROWS * 8, LANES)
        sci_spread = jnp.broadcast_to(science[:, None, :], (ROWS, 8, LANES)).reshape(ROWS * 8, LANES)
        place = lax.broadcasted_iota(jnp.int32, (ROWS * 8, LANES), 0) & 7
        parts = [d[:, k * LANES : (k + 1) * LANES] for k in range(NPROF)]
        parts[0] = jnp.where(place == SCI, sci_spread, parts[0])
        parts = [part * spread for part in parts]
        for k in range(NPROF):
            basis[slot, b, :, k * LANES : (k + 1) * LANES] = parts[k]

        def arranged(pieces):
            return jnp.concatenate(
                [
                    jnp.concatenate([piece[h * 8 : h * 8 + 8] for piece in pieces], axis=0)
                    for h in range(ROWS)
                ],
                axis=1,
            ).astype(jnp.bfloat16)

        highs = [rounded(part) for part in parts]
        rests = [part - h for part, h in zip(parts, highs)]
        return total + lax.dot_general(
            arranged(highs + rests),
            arranged(highs),
            (((1,), (1,)), ((), ())),
            preferred_element_type=jnp.float32,
        )

    total = lax.fori_loop(0, NBLOCKS, one_block, jnp.zeros((80, 40), jnp.float32), unroll=4)
    return total[0:40] + (total[40:80] + total[40:80].T)


def packed(mat):
    wide = jnp.concatenate([mat, jnp.zeros((40, LANES - 40), jnp.float32)], axis=1)
    first = wide[0:8] + pltpu.roll(wide[8:16], 40, 1) + pltpu.roll(wide[16:24], 80, 1)
    return jnp.concatenate([first, wide[24:32] + pltpu.roll(wide[32:40], 40, 1)], axis=0)


def unpacked(tiles):
    first, second = tiles[0:8], tiles[8:16]
    return jnp.concatenate(
        [
            first,
            pltpu.roll(first, LANES - 40, 1),
            pltpu.roll(first, LANES - 80, 1),
            second,
            pltpu.roll(second, LANES - 40, 1),
        ],
        axis=0,
    )


def solve(mats):
    row = lax.broadcasted_iota(jnp.int32, (40, LANES), 0)
    col = lax.broadcasted_iota(jnp.int32, (40, LANES), 1)
    mats = [m + jnp.where(row == col, RIDGE, 0.0) for m in mats]
    for k in range(NPROF):
        for l in range(NPROF):
            p = k * 8 + l
            for s in range(STEPS):
                m = mats[s]
                pivot = m[p : p + 1, :] / m[p : p + 1, p : p + 1]
                mats[s] = jnp.where(row == p, pivot, m - m[:, p : p + 1] * pivot)
    return [
        jnp.where(row == SCI, -1.0, jnp.broadcast_to(m[:, SCI : SCI + 1], (40, LANES)))
        for m in mats
    ]


def kernel(
    owners, temp_hbm, sci_hbm, svar_hbm, bad_hbm, col_hbm, row_hbm, out_ref,
    temp_ref, sci_ref, svar_ref, bad_ref, col_ref, row_ref, load_sem,
    mine, recv1, send2, recv2, ag, red, cols, basis,
    ssem1, same_sem, cross_sem, ssem2, rsem2, static_send, static_recv, ssem3, rsem3, ssem4, rsem4,
):
    v = lax.axis_index("visit")
    p = lax.axis_index("patch")
    group = v // GROUP
    cls = v % GROUP

    def peer(t):
        return group * GROUP + t

    loads = [
        pltpu.make_async_copy(src, dst, load_sem.at[i])
        for i, (src, dst) in enumerate(
            (
                (temp_hbm, temp_ref),
                (col_hbm, col_ref),
                (row_hbm, row_ref),
                (svar_hbm, svar_ref),
                (bad_hbm, bad_ref),
                (sci_hbm, sci_ref),
            )
        )
    ]
    for load in loads:
        load.start()

    recv1[...] = jnp.zeros_like(recv1)

    barrier = pltpu.get_barrier_semaphore()

    def greet(vv, pp):
        pl.semaphore_signal(barrier, inc=1, device_id=(vv, pp), device_id_type=MESH)

    for d in range(1, GROUP):
        greet(peer((cls + d) % GROUP), p)
    for d in range(1, NGROUPS):
        greet(((group + d) % NGROUPS) * GROUP + cls, p)
    for d in range(1, NPATCH):
        greet(v, (p + d) % NPATCH)

    @pl.when((cls < 2) & (p > 0))
    def _():
        for d in range(1, GROUP):
            greet(peer((cls + d) % GROUP), p - 1)

    @pl.when(((cls == 4) | (cls == 5)) & (p < NPATCH - 1))
    def _():
        for d in range(1, GROUP):
            greet(peer((cls + d) % GROUP), p + 1)

    below = jnp.where(p < NPATCH - 1, jnp.where(cls < 2, 1, 2), 0)
    above = jnp.where(p > 0, jnp.where((cls == 4) | (cls == 5), 1, 2), 0)
    loads[0].wait()
    flat = mine.reshape(2 * ROWS * NBLOCKS, LANES)
    for kind in range(2):
        for half in range(2):
            for b in range(NBLOCKS):
                flat[pl.ds((kind * ROWS + half * 8) * NBLOCKS + b, 8, stride=NBLOCKS), :] = temp_ref[
                    0, kind, half * 8 : half * 8 + 8, b * LANES : (b + 1) * LANES
                ]

    pl.semaphore_wait(barrier, GROUP - 1 + NGROUPS - 1 + NPATCH - 1 + below + above)

    def first_copy(i):
        t, dp, at, n, to = PARTS[i]
        return pltpu.make_async_remote_copy(
            src_ref=mine.at[pl.ds(at, n)],
            dst_ref=recv1.at[pl.ds(cls * SLOT + to, n)],
            send_sem=ssem1.at[i],
            recv_sem=same_sem if dp == 0 else cross_sem,
            device_id=(peer(t), p + dp),
            device_id_type=MESH,
        )

    def sends(i):
        t, dp = PARTS[i][:2]
        if dp == 0:
            return cls != t
        return p < NPATCH - 1 if dp == 1 else p > 0

    for i in range(len(PARTS)):

        @pl.when(sends(i))
        def _(i=i):
            first_copy(i).start()

    for t, dp, at, n, to in PARTS:

        @pl.when(cls == t)
        def _(t=t, dp=dp, at=at, n=n, to=to):
            if dp == 0:
                recv1[pl.ds(t * SLOT + to, n)] = mine[pl.ds(at, n)]

    for t, dp, at, n, to in PARTS:
        if dp == 0:

            @pl.when(cls == t)
            def _(n=n):
                rows = recv1.at[pl.ds(0, (GROUP - 1) * n)]
                pltpu.make_async_copy(rows, rows, same_sem).wait()

        else:

            @pl.when((cls == t) & (p > 0 if dp == 1 else p < NPATCH - 1))
            def _(n=n):
                rows = recv1.at[pl.ds(0, GROUP * n)]
                pltpu.make_async_copy(rows, rows, cross_sem).wait()

    own = pl.ds(cls * SLOT, SLOT)
    fixed = pl.ds((FIXED % GROUP) * SLOT, SLOT)

    def static_copy(g):
        return pltpu.make_async_remote_copy(
            src_ref=recv1.at[fixed],
            dst_ref=ag.at[0, own],
            send_sem=static_send.at[g],
            recv_sem=static_recv,
            device_id=(g * GROUP + cls, p),
            device_id_type=MESH,
        )

    @pl.when(group == FIXED // GROUP)
    def _():
        for g in range(NGROUPS - 1):
            static_copy(g).start()
        ag[0, own] = recv1[fixed]

    other = owners[0] + owners[1] - FIXED
    chosen = recv1[pl.ds((other & 7) * SLOT, SLOT)]
    send2[...] = chosen
    recv2[pl.ds(group * SLOT, SLOT)] = chosen

    def second_copy(d):
        return pltpu.make_async_remote_copy(
            src_ref=send2,
            dst_ref=recv2.at[pl.ds(group * SLOT, SLOT)],
            send_sem=ssem2.at[d],
            recv_sem=rsem2.at[d],
            device_id=(((group + d) % NGROUPS) * GROUP + cls, p),
            device_id_type=MESH,
        )

    for d in (2, 1, 3):
        second_copy(d).start()

    def third_copy(slot, d):
        return pltpu.make_async_remote_copy(
            src_ref=ag.at[slot, own],
            dst_ref=ag.at[slot, own],
            send_sem=ssem3.at[slot, d],
            recv_sem=rsem3.at[slot],
            device_id=(peer((cls + d) % GROUP), p),
            device_id_type=MESH,
        )

    @pl.when(group != FIXED // GROUP)
    def _():
        pltpu.make_async_copy(ag.at[0, own], ag.at[0, own], static_recv).wait()

    for d in range(1, GROUP):
        third_copy(0, d).start()
    for d in range(1, NGROUPS):
        second_copy(d).wait_recv()
    ag[1, own] = recv2[pl.ds(((other >> 3) & 3) * SLOT, SLOT)]
    for d in range(1, GROUP):
        third_copy(1, d).start()

    ag_flat = ag.reshape(STEPS * 56 * NBLOCKS, LANES)
    fixed_step = jnp.where(owners[1] == FIXED, 1, 0)
    for load in loads[1:]:
        load.wait()

    def fourth_copy(slot, d):
        return pltpu.make_async_remote_copy(
            src_ref=red.at[slot, p],
            dst_ref=red.at[slot, p],
            send_sem=ssem4.at[slot, d],
            recv_sem=rsem4.at[slot],
            device_id=(v, (p + d) % NPATCH),
            device_id_type=MESH,
        )

    for slot in range(STEPS):
        rows = ag.at[slot, pl.ds(0, (GROUP - 1) * SLOT)]
        pltpu.make_async_copy(rows, rows, rsem3.at[slot]).wait()
        step = fixed_step if slot == 0 else 1 - fixed_step
        red[slot, p] = packed(
            normal_part(slot, step, ag, ag_flat, cols, basis, col_ref, row_ref, sci_ref, svar_ref, bad_ref)
        )
        for d in range(1, NPATCH):
            fourth_copy(slot, d).start()

    mats = []
    for slot in range(STEPS):
        rows = red.at[slot, pl.ds(0, NPATCH - 1)]
        pltpu.make_async_copy(rows, rows, rsem4.at[slot]).wait()
        total = red[slot, 0]
        for q in range(1, NPATCH):
            total = total + red[slot, q]
        mats.append(unpacked(total))
    coefs = solve(mats)

    for step in range(STEPS):
        slot = jnp.where(fixed_step == step, 0, 1)
        coef = jnp.where(fixed_step == step, coefs[0], coefs[1])

        def one_block(b, carry, step=step, slot=slot, coef=coef):
            at = pl.multiple_of(b * LANES, LANES)
            sums = jnp.zeros((ROWS, 8, LANES), jnp.float32)
            for k in range(NPROF):
                d = basis[slot, b, :, k * LANES : (k + 1) * LANES].reshape(ROWS, 8, LANES)
                sums = sums + d * coef[k * 8 : k * 8 + 8][None]
            out_ref[step, 0, :, pl.ds(at, LANES)] = -jnp.sum(sums, axis=1)
            return carry

        lax.fori_loop(0, NBLOCKS, one_block, 0, unroll=4)

    for i in range(len(PARTS)):

        @pl.when(sends(i))
        def _(i=i):
            first_copy(i).wait_send()

    @pl.when(group == FIXED // GROUP)
    def _():
        for g in range(NGROUPS - 1):
            static_copy(g).wait_send()

    for d in range(1, NGROUPS):
        second_copy(d).wait_send()
    for slot in range(STEPS):
        for d in range(1, GROUP):
            third_copy(slot, d).wait_send()
        for d in range(1, NPATCH):
            fourth_copy(slot, d).wait_send()


def shards(templates, owners, science, sci_var, bad_pixels):
    hbm = pl.BlockSpec(memory_space=pltpu.HBM)
    row_shape = (NBLOCKS, LANES)
    dma = pltpu.SemaphoreType.DMA
    col_table, rows_table = jnp.asarray(column_table()), jnp.asarray(row_table())
    operands = (templates, science, sci_var, bad_pixels, col_table, rows_table)
    return pl.pallas_call(
        kernel,
        out_shape=jax.ShapeDtypeStruct(science.shape, jnp.float32),
        in_specs=[pl.BlockSpec(memory_space=pltpu.SMEM)] + [hbm] * len(operands),
        out_specs=pl.BlockSpec(memory_space=pltpu.VMEM),
        scratch_shapes=[pltpu.VMEM(x.shape, x.dtype) for x in operands]
        + [
            dma((len(operands),)),
            pltpu.VMEM((2 * ROWS, *row_shape), jnp.float32),
            pltpu.VMEM((GROUP * SLOT, *row_shape), jnp.float32),
            pltpu.VMEM((SLOT, *row_shape), jnp.float32),
            pltpu.VMEM((NGROUPS * SLOT, *row_shape), jnp.float32),
            pltpu.VMEM((STEPS, GROUP * SLOT, *row_shape), jnp.float32),
            pltpu.VMEM((STEPS, NPATCH, 16, LANES), jnp.float32),
            pltpu.VMEM((NPROF * POSITIONS * NBLOCKS, LANES), jnp.float32),
            pltpu.VMEM((STEPS, NBLOCKS, ROWS * 8, NPROF * LANES), jnp.float32),
            dma((len(PARTS),)),
            dma,
            dma,
            dma((NGROUPS,)),
            dma((NGROUPS,)),
            dma((NGROUPS,)),
            dma,
            dma((STEPS, GROUP)),
            dma((STEPS,)),
            dma((STEPS, NPATCH)),
            dma((STEPS,)),
        ],
        compiler_params=pltpu.CompilerParams(
            collective_id=0, has_side_effects=True, vmem_limit_bytes=32 * 1024 * 1024
        ),
        name="difference",
    )(owners, *operands)


def solution(mesh):
    return jax.shard_map(
        shards,
        mesh=mesh,
        in_specs=(
            P("visit", None, "patch", None),
            P(),
            P(None, "visit", "patch", None),
            P(None, "visit", "patch", None),
            P(None, "visit", "patch", None),
        ),
        out_specs=P(None, "visit", "patch", None),
        check_vma=False,
    )
```

```python
import functools

import jax
import jax.numpy as jnp
import ml_dtypes
import numpy as np
from jax import lax
from jax.experimental import pallas as pl
from jax.experimental.pallas import tpu as pltpu
from jax.sharding import PartitionSpec as P

NPROF = 5
RAD = 10
STEPS = 2
RIDGE = 1.0

GROUP = 8
NGROUPS = 4
NPATCH = 16
SLOT = 7
FIXED = 31
ROWS = 16
LANES = 128
NBLOCKS = 8
SCI = 5
MESH = pl.DeviceIdType.MESH

PARTS = (
    (0, 1, 6, 7, 0),
    (1, 1, 13, 3, 0),
    (1, 0, 0, 3, 3),
    (2, 0, 3, 7, 0),
    (3, 0, 10, 6, 0),
    (4, -1, 0, 7, 0),
    (5, -1, 7, 3, 0),
    (5, 0, 16, 3, 4),
    (6, 0, 19, 7, 0),
    (7, 0, 26, 6, 0),
)
VAR_AT = 39
POSITIONS = 40


def image_positions():
    return list(range(0, 13)) + list(range(14, 27)) + list(range(28, 38))


def profile_table():
    offsets = np.arange(-RAD, RAD + 1) * 1.0
    recipe = [(1.0, 0), (1.5, 1), (2.0, 2), (3.0, 0), (4.0, 1)]
    profiles = []
    for spread, degree in recipe[:NPROF]:
        profile = offsets**degree * np.exp(-offsets * offsets / (2.0 * spread * spread))
        for earlier in profiles:
            profile = profile - np.dot(earlier, profile) * earlier
        profile = profile / np.sqrt(np.dot(profile, profile))
        profiles.append(profile)
    return np.stack(profiles)


def column_table():
    prof = profile_table().astype(np.float32)
    table = np.zeros((2 * LANES, NPROF * LANES), np.float32)
    for k in range(NPROF):
        for n in range(LANES):
            first = n + LANES // 2 - RAD
            table[first : first + 2 * RAD + 1, k * LANES + n] = prof[k]
    high, mid, _ = split3(table)
    return np.concatenate([high, mid], axis=1).astype(ml_dtypes.bfloat16)


def split3(x):
    high = x.astype(ml_dtypes.bfloat16).astype(np.float32)
    mid = (x - high).astype(ml_dtypes.bfloat16).astype(np.float32)
    low = (x - high - mid).astype(ml_dtypes.bfloat16).astype(np.float32)
    return high, mid, low


def row_table():
    prof = profile_table().astype(np.float32)
    places = image_positions()
    table = np.zeros((ROWS * 8, POSITIONS), np.float32)
    for h in range(ROWS):
        for l in range(NPROF):
            for a in range(2 * RAD + 1):
                table[h * 8 + l, places[h + a]] = prof[l, a]
    high, mid, low = split3(table)
    return np.concatenate([high, high, high, mid, mid, low], axis=1).astype(ml_dtypes.bfloat16)


def rounded(x):
    return x.astype(jnp.bfloat16).astype(jnp.float32)


def normal_part(slot, step, ag, ag_flat, cols, basis, col_ref, row_ref, sci_ref, svar_ref, bad_ref):
    x = ag[slot, 0:POSITIONS]
    y = pltpu.roll(x, LANES // 2, 2)
    lane = lax.broadcasted_iota(jnp.int32, y.shape, 2)
    block = lax.broadcasted_iota(jnp.int32, y.shape, 1)
    before = jnp.where(block == 0, 0.0, pltpu.roll(y, 1, 1))
    after = jnp.where(block == NBLOCKS - 1, 0.0, pltpu.roll(y, NBLOCKS - 1, 1))
    low = lane < LANES // 2
    left = jnp.where(low, before, y).reshape(POSITIONS * NBLOCKS, LANES)
    right = jnp.where(low, y, after).reshape(POSITIONS * NBLOCKS, LANES)
    window = jnp.concatenate([left, right], axis=1)
    height = POSITIONS * NBLOCKS
    high = rounded(window)
    both = jnp.concatenate([high, window - high], axis=0).astype(jnp.bfloat16)
    for k in range(NPROF):
        table = col_ref[:, k * LANES : (k + 1) * LANES]
        rest = col_ref[:, (NPROF + k) * LANES : (NPROF + k + 1) * LANES]
        main = jnp.dot(both, table, preferred_element_type=jnp.float32)
        more = jnp.dot(both[0:height], rest, preferred_element_type=jnp.float32)
        cols[k * height : (k + 1) * height, :] = main[0:height] + (main[height:] + more)

    def one_block(b, total):
        at = pl.multiple_of(b * LANES, LANES)
        c = jnp.concatenate(
            [
                cols[pl.ds(k * height + b, POSITIONS, stride=NBLOCKS), :]
                for k in range(NPROF)
            ],
            axis=1,
        )
        high = rounded(c)
        rest = c - high
        mid = rounded(rest)
        low = rest - mid
        stacked = jnp.concatenate([high, mid, low, high, mid, high], axis=0).astype(jnp.bfloat16)
        d = jnp.dot(row_ref[...], stacked, preferred_element_type=jnp.float32)
        science = sci_ref[step, 0, :, pl.ds(at, LANES)]
        usable = (1 - bad_ref[step, 0, :, pl.ds(at, LANES)]).astype(jnp.float32)
        tile_var = ag_flat[pl.ds((slot * 56 + VAR_AT) * NBLOCKS + b, ROWS, stride=NBLOCKS), :]
        scale = usable / jnp.sqrt(svar_ref[step, 0, :, pl.ds(at, LANES)] + tile_var)
        spread = jnp.broadcast_to(scale[:, None, :], (ROWS, 8, LANES)).reshape(ROWS * 8, LANES)
        sci_spread = jnp.broadcast_to(science[:, None, :], (ROWS, 8, LANES)).reshape(ROWS * 8, LANES)
        place = lax.broadcasted_iota(jnp.int32, (ROWS * 8, LANES), 0) & 7
        parts = [d[:, k * LANES : (k + 1) * LANES] for k in range(NPROF)]
        parts[0] = jnp.where(place == SCI, sci_spread, parts[0])
        parts = [part * spread for part in parts]
        for k in range(NPROF):
            basis[slot, b, :, k * LANES : (k + 1) * LANES] = parts[k]

        def arranged(pieces):
            return jnp.concatenate(
                [
                    jnp.concatenate([piece[h * 8 : h * 8 + 8] for piece in pieces], axis=0)
                    for h in range(ROWS)
                ],
                axis=1,
            ).astype(jnp.bfloat16)

        highs = [rounded(part) for part in parts]
        rests = [part - h for part, h in zip(parts, highs)]
        return total + lax.dot_general(
            arranged(highs + rests),
            arranged(highs),
            (((1,), (1,)), ((), ())),
            preferred_element_type=jnp.float32,
        )

    total = lax.fori_loop(0, NBLOCKS, one_block, jnp.zeros((80, 40), jnp.float32), unroll=4)
    return total[0:40] + (total[40:80] + total[40:80].T)


def packed(mat):
    wide = jnp.concatenate([mat, jnp.zeros((40, LANES - 40), jnp.float32)], axis=1)
    first = wide[0:8] + pltpu.roll(wide[8:16], 40, 1) + pltpu.roll(wide[16:24], 80, 1)
    return jnp.concatenate([first, wide[24:32] + pltpu.roll(wide[32:40], 40, 1)], axis=0)


def unpacked(tiles):
    first, second = tiles[0:8], tiles[8:16]
    return jnp.concatenate(
        [
            first,
            pltpu.roll(first, LANES - 40, 1),
            pltpu.roll(first, LANES - 80, 1),
            second,
            pltpu.roll(second, LANES - 40, 1),
        ],
        axis=0,
    )


def solve(mats):
    row = lax.broadcasted_iota(jnp.int32, (40, LANES), 0)
    col = lax.broadcasted_iota(jnp.int32, (40, LANES), 1)
    mats = [m + jnp.where(row == col, RIDGE, 0.0) for m in mats]
    for k in range(NPROF):
        for l in range(NPROF):
            p = k * 8 + l
            for s in range(STEPS):
                m = mats[s]
                pivot = m[p : p + 1, :] / m[p : p + 1, p : p + 1]
                mats[s] = jnp.where(row == p, pivot, m - m[:, p : p + 1] * pivot)
    return [
        jnp.where(row == SCI, -1.0, jnp.broadcast_to(m[:, SCI : SCI + 1], (40, LANES)))
        for m in mats
    ]


def kernel(
    owners, temp_hbm, sci_hbm, svar_hbm, bad_hbm, col_hbm, row_hbm, out_ref,
    temp_ref, sci_ref, svar_ref, bad_ref, col_ref, row_ref, load_sem,
    mine, recv1, send2, recv2, ag, red, cols, basis,
    ssem1, same_sem, cross_sem, ssem2, rsem2, static_send, static_recv, ssem3, rsem3, ssem4, rsem4,
):
    v = lax.axis_index("visit")
    p = lax.axis_index("patch")
    group = v // GROUP
    cls = v % GROUP

    def peer(t):
        return group * GROUP + t

    loads = [
        pltpu.make_async_copy(src, dst, load_sem.at[i])
        for i, (src, dst) in enumerate(
            (
                (temp_hbm, temp_ref),
                (col_hbm, col_ref),
                (row_hbm, row_ref),
                (svar_hbm, svar_ref),
                (bad_hbm, bad_ref),
                (sci_hbm, sci_ref),
            )
        )
    ]
    for load in loads:
        load.start()

    recv1[...] = jnp.zeros_like(recv1)

    barrier = pltpu.get_barrier_semaphore()

    def greet(vv, pp):
        pl.semaphore_signal(barrier, inc=1, device_id=(vv, pp), device_id_type=MESH)

    for d in range(1, GROUP):
        greet(peer((cls + d) % GROUP), p)
    for d in range(1, NGROUPS):
        greet(((group + d) % NGROUPS) * GROUP + cls, p)
    for d in range(1, NPATCH):
        greet(v, (p + d) % NPATCH)

    @pl.when((cls < 2) & (p > 0))
    def _():
        for d in range(1, GROUP):
            greet(peer((cls + d) % GROUP), p - 1)

    @pl.when(((cls == 4) | (cls == 5)) & (p < NPATCH - 1))
    def _():
        for d in range(1, GROUP):
            greet(peer((cls + d) % GROUP), p + 1)

    below = jnp.where(p < NPATCH - 1, jnp.where(cls < 2, 1, 2), 0)
    above = jnp.where(p > 0, jnp.where((cls == 4) | (cls == 5), 1, 2), 0)
    loads[0].wait()
    flat = mine.reshape(2 * ROWS * NBLOCKS, LANES)
    for kind in range(2):
        for half in range(2):
            for b in range(NBLOCKS):
                flat[pl.ds((kind * ROWS + half * 8) * NBLOCKS + b, 8, stride=NBLOCKS), :] = temp_ref[
                    0, kind, half * 8 : half * 8 + 8, b * LANES : (b + 1) * LANES
                ]

    pl.semaphore_wait(barrier, GROUP - 1 + NGROUPS - 1 + NPATCH - 1 + below + above)

    def first_copy(i):
        t, dp, at, n, to = PARTS[i]
        return pltpu.make_async_remote_copy(
            src_ref=mine.at[pl.ds(at, n)],
            dst_ref=recv1.at[pl.ds(cls * SLOT + to, n)],
            send_sem=ssem1.at[i],
            recv_sem=same_sem if dp == 0 else cross_sem,
            device_id=(peer(t), p + dp),
            device_id_type=MESH,
        )

    def sends(i):
        t, dp = PARTS[i][:2]
        if dp == 0:
            return cls != t
        return p < NPATCH - 1 if dp == 1 else p > 0

    for i in range(len(PARTS)):

        @pl.when(sends(i))
        def _(i=i):
            first_copy(i).start()

    for t, dp, at, n, to in PARTS:

        @pl.when(cls == t)
        def _(t=t, dp=dp, at=at, n=n, to=to):
            if dp == 0:
                recv1[pl.ds(t * SLOT + to, n)] = mine[pl.ds(at, n)]

    for t, dp, at, n, to in PARTS:
        if dp == 0:

            @pl.when(cls == t)
            def _(n=n):
                rows = recv1.at[pl.ds(0, (GROUP - 1) * n)]
                pltpu.make_async_copy(rows, rows, same_sem).wait()

        else:

            @pl.when((cls == t) & (p > 0 if dp == 1 else p < NPATCH - 1))
            def _(n=n):
                rows = recv1.at[pl.ds(0, GROUP * n)]
                pltpu.make_async_copy(rows, rows, cross_sem).wait()

    own = pl.ds(cls * SLOT, SLOT)
    fixed = pl.ds((FIXED % GROUP) * SLOT, SLOT)

    def static_copy(g):
        return pltpu.make_async_remote_copy(
            src_ref=recv1.at[fixed],
            dst_ref=ag.at[0, own],
            send_sem=static_send.at[g],
            recv_sem=static_recv,
            device_id=(g * GROUP + cls, p),
            device_id_type=MESH,
        )

    @pl.when(group == FIXED // GROUP)
    def _():
        for g in range(NGROUPS - 1):
            static_copy(g).start()
        ag[0, own] = recv1[fixed]

    other = owners[0] + owners[1] - FIXED
    chosen = recv1[pl.ds((other & 7) * SLOT, SLOT)]
    send2[...] = chosen
    recv2[pl.ds(group * SLOT, SLOT)] = chosen

    def second_copy(d):
        return pltpu.make_async_remote_copy(
            src_ref=send2,
            dst_ref=recv2.at[pl.ds(group * SLOT, SLOT)],
            send_sem=ssem2.at[d],
            recv_sem=rsem2.at[d],
            device_id=(((group + d) % NGROUPS) * GROUP + cls, p),
            device_id_type=MESH,
        )

    for d in (2, 1, 3):
        second_copy(d).start()

    def third_copy(slot, d):
        return pltpu.make_async_remote_copy(
            src_ref=ag.at[slot, own],
            dst_ref=ag.at[slot, own],
            send_sem=ssem3.at[slot, d],
            recv_sem=rsem3.at[slot],
            device_id=(peer((cls + d) % GROUP), p),
            device_id_type=MESH,
        )

    @pl.when(group != FIXED // GROUP)
    def _():
        pltpu.make_async_copy(ag.at[0, own], ag.at[0, own], static_recv).wait()

    for d in range(1, GROUP):
        third_copy(0, d).start()
    for d in range(1, NGROUPS):
        second_copy(d).wait_recv()
    ag[1, own] = recv2[pl.ds(((other >> 3) & 3) * SLOT, SLOT)]
    for d in range(1, GROUP):
        third_copy(1, d).start()

    ag_flat = ag.reshape(STEPS * 56 * NBLOCKS, LANES)
    fixed_step = jnp.where(owners[1] == FIXED, 1, 0)
    for load in loads[1:]:
        load.wait()

    def fourth_copy(slot, d):
        return pltpu.make_async_remote_copy(
            src_ref=red.at[slot, p],
            dst_ref=red.at[slot, p],
            send_sem=ssem4.at[slot, d],
            recv_sem=rsem4.at[slot],
            device_id=(v, (p + d) % NPATCH),
            device_id_type=MESH,
        )

    for slot in range(STEPS):
        rows = ag.at[slot, pl.ds(0, (GROUP - 1) * SLOT)]
        pltpu.make_async_copy(rows, rows, rsem3.at[slot]).wait()
        step = fixed_step if slot == 0 else 1 - fixed_step
        red[slot, p] = packed(
            normal_part(slot, step, ag, ag_flat, cols, basis, col_ref, row_ref, sci_ref, svar_ref, bad_ref)
        )
        for d in range(1, NPATCH):
            fourth_copy(slot, d).start()

    mats = []
    for slot in range(STEPS):
        rows = red.at[slot, pl.ds(0, NPATCH - 1)]
        pltpu.make_async_copy(rows, rows, rsem4.at[slot]).wait()
        total = red[slot, 0]
        for q in range(1, NPATCH):
            total = total + red[slot, q]
        mats.append(unpacked(total))
    coefs = solve(mats)

    for step in range(STEPS):
        slot = jnp.where(fixed_step == step, 0, 1)
        coef = jnp.where(fixed_step == step, coefs[0], coefs[1])

        def one_block(b, carry, step=step, slot=slot, coef=coef):
            at = pl.multiple_of(b * LANES, LANES)
            sums = jnp.zeros((ROWS, 8, LANES), jnp.float32)
            for k in range(NPROF):
                d = basis[slot, b, :, k * LANES : (k + 1) * LANES].reshape(ROWS, 8, LANES)
                sums = sums + d * coef[k * 8 : k * 8 + 8][None]
            out_ref[step, 0, :, pl.ds(at, LANES)] = -jnp.sum(sums, axis=1)
            return carry

        lax.fori_loop(0, NBLOCKS, one_block, 0, unroll=4)

    for i in range(len(PARTS)):

        @pl.when(sends(i))
        def _(i=i):
            first_copy(i).wait_send()

    @pl.when(group == FIXED // GROUP)
    def _():
        for g in range(NGROUPS - 1):
            static_copy(g).wait_send()

    for d in range(1, NGROUPS):
        second_copy(d).wait_send()
    for slot in range(STEPS):
        for d in range(1, GROUP):
            third_copy(slot, d).wait_send()
        for d in range(1, NPATCH):
            fourth_copy(slot, d).wait_send()


def shards(templates, owners, science, sci_var, bad_pixels):
    hbm = pl.BlockSpec(memory_space=pltpu.HBM)
    row_shape = (NBLOCKS, LANES)
    dma = pltpu.SemaphoreType.DMA
    col_table, rows_table = jnp.asarray(column_table()), jnp.asarray(row_table())
    operands = (templates, science, sci_var, bad_pixels, col_table, rows_table)
    return pl.pallas_call(
        kernel,
        out_shape=jax.ShapeDtypeStruct(science.shape, jnp.float32),
        in_specs=[pl.BlockSpec(memory_space=pltpu.SMEM)] + [hbm] * len(operands),
        out_specs=pl.BlockSpec(memory_space=pltpu.VMEM),
        scratch_shapes=[pltpu.VMEM(x.shape, x.dtype) for x in operands]
        + [
            dma((len(operands),)),
            pltpu.VMEM((2 * ROWS, *row_shape), jnp.float32),
            pltpu.VMEM((GROUP * SLOT, *row_shape), jnp.float32),
            pltpu.VMEM((SLOT, *row_shape), jnp.float32),
            pltpu.VMEM((NGROUPS * SLOT, *row_shape), jnp.float32),
            pltpu.VMEM((STEPS, GROUP * SLOT, *row_shape), jnp.float32),
            pltpu.VMEM((STEPS, NPATCH, 16, LANES), jnp.float32),
            pltpu.VMEM((NPROF * POSITIONS * NBLOCKS, LANES), jnp.float32),
            pltpu.VMEM((STEPS, NBLOCKS, ROWS * 8, NPROF * LANES), jnp.float32),
            dma((len(PARTS),)),
            dma,
            dma,
            dma((NGROUPS,)),
            dma((NGROUPS,)),
            dma((NGROUPS,)),
            dma,
            dma((STEPS, GROUP)),
            dma((STEPS,)),
            dma((STEPS, NPATCH)),
            dma((STEPS,)),
        ],
        compiler_params=pltpu.CompilerParams(
            collective_id=0, has_side_effects=True, vmem_limit_bytes=60 * 1024 * 1024
        ),
        name="difference",
    )(owners, *operands)


def solution(mesh):
    return jax.shard_map(
        shards,
        mesh=mesh,
        in_specs=(
            P("visit", None, "patch", None),
            P(),
            P(None, "visit", "patch", None),
            P(None, "visit", "patch", None),
            P(None, "visit", "patch", None),
        ),
        out_specs=P(None, "visit", "patch", None),
        check_vma=False,
    )
```

```python
import functools

import jax
import jax.numpy as jnp
import ml_dtypes
import numpy as np
from jax import lax
from jax.experimental import pallas as pl
from jax.experimental.pallas import tpu as pltpu
from jax.sharding import PartitionSpec as P

NPROF = 5
RAD = 10
STEPS = 2
RIDGE = 1.0

GROUP = 8
NGROUPS = 4
NPATCH = 16
SLOT = 7
FIXED = 31
ROWS = 16
LANES = 128
NBLOCKS = 8
SCI = 5
MESH = pl.DeviceIdType.MESH

PARTS = (
    (0, 1, 6, 7, 0),
    (1, 1, 13, 3, 0),
    (1, 0, 0, 3, 3),
    (2, 0, 3, 7, 0),
    (3, 0, 10, 6, 0),
    (4, -1, 0, 7, 0),
    (5, -1, 7, 3, 0),
    (5, 0, 16, 3, 4),
    (6, 0, 19, 7, 0),
    (7, 0, 26, 6, 0),
)
VAR_AT = 39
POSITIONS = 40


def image_positions():
    return list(range(0, 13)) + list(range(14, 27)) + list(range(28, 38))


def profile_table():
    offsets = np.arange(-RAD, RAD + 1) * 1.0
    recipe = [(1.0, 0), (1.5, 1), (2.0, 2), (3.0, 0), (4.0, 1)]
    profiles = []
    for spread, degree in recipe[:NPROF]:
        profile = offsets**degree * np.exp(-offsets * offsets / (2.0 * spread * spread))
        for earlier in profiles:
            profile = profile - np.dot(earlier, profile) * earlier
        profile = profile / np.sqrt(np.dot(profile, profile))
        profiles.append(profile)
    return np.stack(profiles)


def column_table():
    prof = profile_table().astype(np.float32)
    table = np.zeros((2 * LANES, NPROF * LANES), np.float32)
    for k in range(NPROF):
        for n in range(LANES):
            first = n + LANES // 2 - RAD
            table[first : first + 2 * RAD + 1, k * LANES + n] = prof[k]
    high, mid, _ = split3(table)
    return np.concatenate([high, mid], axis=1).astype(ml_dtypes.bfloat16)


def split3(x):
    high = x.astype(ml_dtypes.bfloat16).astype(np.float32)
    mid = (x - high).astype(ml_dtypes.bfloat16).astype(np.float32)
    low = (x - high - mid).astype(ml_dtypes.bfloat16).astype(np.float32)
    return high, mid, low


def row_table():
    prof = profile_table().astype(np.float32)
    places = image_positions()
    table = np.zeros((ROWS * 8, POSITIONS), np.float32)
    for h in range(ROWS):
        for l in range(NPROF):
            for a in range(2 * RAD + 1):
                table[h * 8 + l, places[h + a]] = prof[l, a]
    high, mid, low = split3(table)
    return np.concatenate([high, high, high, mid, mid, low], axis=1).astype(ml_dtypes.bfloat16)


def rounded(x):
    return x.astype(jnp.bfloat16).astype(jnp.float32)


def normal_part(slot, step, ag, ag_flat, cols, basis, col_ref, row_ref, sci_ref, svar_ref, bad_ref):
    x = ag[slot, 0:POSITIONS]
    y = pltpu.roll(x, LANES // 2, 2)
    lane = lax.broadcasted_iota(jnp.int32, y.shape, 2)
    block = lax.broadcasted_iota(jnp.int32, y.shape, 1)
    before = jnp.where(block == 0, 0.0, pltpu.roll(y, 1, 1))
    after = jnp.where(block == NBLOCKS - 1, 0.0, pltpu.roll(y, NBLOCKS - 1, 1))
    low = lane < LANES // 2
    left = jnp.where(low, before, y).reshape(POSITIONS * NBLOCKS, LANES)
    right = jnp.where(low, y, after).reshape(POSITIONS * NBLOCKS, LANES)
    window = jnp.concatenate([left, right], axis=1)
    height = POSITIONS * NBLOCKS
    high = rounded(window)
    both = jnp.concatenate([high, window - high], axis=0).astype(jnp.bfloat16)
    for k in range(NPROF):
        table = col_ref[:, k * LANES : (k + 1) * LANES]
        rest = col_ref[:, (NPROF + k) * LANES : (NPROF + k + 1) * LANES]
        main = jnp.dot(both, table, preferred_element_type=jnp.float32)
        more = jnp.dot(both[0:height], rest, preferred_element_type=jnp.float32)
        cols[k * height : (k + 1) * height, :] = main[0:height] + (main[height:] + more)

    def one_block(b, total):
        at = pl.multiple_of(b * LANES, LANES)
        c = jnp.concatenate(
            [
                cols[pl.ds(k * height + b, POSITIONS, stride=NBLOCKS), :]
                for k in range(NPROF)
            ],
            axis=1,
        )
        high = rounded(c)
        rest = c - high
        mid = rounded(rest)
        low = rest - mid
        stacked = jnp.concatenate([high, mid, low, high, mid, high], axis=0).astype(jnp.bfloat16)
        d = jnp.dot(row_ref[...], stacked, preferred_element_type=jnp.float32)
        science = sci_ref[step, 0, :, pl.ds(at, LANES)]
        usable = (1 - bad_ref[step, 0, :, pl.ds(at, LANES)]).astype(jnp.float32)
        tile_var = ag_flat[pl.ds((slot * 56 + VAR_AT) * NBLOCKS + b, ROWS, stride=NBLOCKS), :]
        scale = usable / jnp.sqrt(svar_ref[step, 0, :, pl.ds(at, LANES)] + tile_var)
        spread = jnp.broadcast_to(scale[:, None, :], (ROWS, 8, LANES)).reshape(ROWS * 8, LANES)
        sci_spread = jnp.broadcast_to(science[:, None, :], (ROWS, 8, LANES)).reshape(ROWS * 8, LANES)
        place = lax.broadcasted_iota(jnp.int32, (ROWS * 8, LANES), 0) & 7
        parts = [d[:, k * LANES : (k + 1) * LANES] for k in range(NPROF)]
        parts[0] = jnp.where(place == SCI, sci_spread, parts[0])
        parts = [part * spread for part in parts]
        for k in range(NPROF):
            basis[slot, b, :, k * LANES : (k + 1) * LANES] = parts[k]

        def arranged(pieces):
            return jnp.concatenate(
                [
                    jnp.concatenate([piece[h * 8 : h * 8 + 8] for piece in pieces], axis=0)
                    for h in range(ROWS)
                ],
                axis=1,
            ).astype(jnp.bfloat16)

        highs = [rounded(part) for part in parts]
        rests = [part - h for part, h in zip(parts, highs)]
        return total + lax.dot_general(
            arranged(highs + rests),
            arranged(highs),
            (((1,), (1,)), ((), ())),
            preferred_element_type=jnp.float32,
        )

    total = lax.fori_loop(0, NBLOCKS, one_block, jnp.zeros((80, 40), jnp.float32), unroll=4)
    return total[0:40] + (total[40:80] + total[40:80].T)


def packed(mat):
    wide = jnp.concatenate([mat, jnp.zeros((40, LANES - 40), jnp.float32)], axis=1)
    first = wide[0:8] + pltpu.roll(wide[8:16], 40, 1) + pltpu.roll(wide[16:24], 80, 1)
    return jnp.concatenate([first, wide[24:32] + pltpu.roll(wide[32:40], 40, 1)], axis=0)


def unpacked(tiles):
    first, second = tiles[0:8], tiles[8:16]
    return jnp.concatenate(
        [
            first,
            pltpu.roll(first, LANES - 40, 1),
            pltpu.roll(first, LANES - 80, 1),
            second,
            pltpu.roll(second, LANES - 40, 1),
        ],
        axis=0,
    )


def solve(mats):
    row = lax.broadcasted_iota(jnp.int32, (40, LANES), 0)
    col = lax.broadcasted_iota(jnp.int32, (40, LANES), 1)
    mats = [m + jnp.where(row == col, RIDGE, 0.0) for m in mats]
    for k in range(NPROF):
        for l in range(NPROF):
            p = k * 8 + l
            for s in range(STEPS):
                m = mats[s]
                pivot = m[p : p + 1, :] / m[p : p + 1, p : p + 1]
                mats[s] = jnp.where(row == p, pivot, m - m[:, p : p + 1] * pivot)
    return [
        jnp.where(row == SCI, -1.0, jnp.broadcast_to(m[:, SCI : SCI + 1], (40, LANES)))
        for m in mats
    ]


def kernel(
    owners, temp_hbm, sci_hbm, svar_hbm, bad_hbm, col_hbm, row_hbm, out_ref,
    temp_ref, sci_ref, svar_ref, bad_ref, col_ref, row_ref, load_sem,
    mine, recv1, send2, recv2, ag, red, cols, basis,
    ssem1, same_sem, cross_sem, ssem2, rsem2, static_send, static_recv, ssem3, rsem3, ssem4, rsem4, passed,
):
    v = lax.axis_index("visit")
    p = lax.axis_index("patch")
    group = v // GROUP
    cls = v % GROUP

    def peer(t):
        return group * GROUP + t

    loads = [
        pltpu.make_async_copy(src, dst, load_sem.at[i])
        for i, (src, dst) in enumerate(
            (
                (temp_hbm, temp_ref),
                (col_hbm, col_ref),
                (row_hbm, row_ref),
                (svar_hbm, svar_ref),
                (bad_hbm, bad_ref),
                (sci_hbm, sci_ref),
            )
        )
    ]
    for load in loads:
        load.start()

    recv1[...] = jnp.zeros_like(recv1)

    barrier = pltpu.get_barrier_semaphore()

    def greet(vv, pp):
        pl.semaphore_signal(barrier, inc=1, device_id=(vv, pp), device_id_type=MESH)

    for d in range(1, GROUP):
        greet(peer((cls + d) % GROUP), p)
    for d in (1, 3):
        greet(((group + d) % NGROUPS) * GROUP + cls, p)
    for d in range(1, NPATCH):
        greet(v, (p + d) % NPATCH)

    @pl.when((cls < 2) & (p > 0))
    def _():
        for d in range(1, GROUP):
            greet(peer((cls + d) % GROUP), p - 1)

    @pl.when(((cls == 4) | (cls == 5)) & (p < NPATCH - 1))
    def _():
        for d in range(1, GROUP):
            greet(peer((cls + d) % GROUP), p + 1)

    below = jnp.where(p < NPATCH - 1, jnp.where(cls < 2, 1, 2), 0)
    above = jnp.where(p > 0, jnp.where((cls == 4) | (cls == 5), 1, 2), 0)
    loads[0].wait()
    flat = mine.reshape(2 * ROWS * NBLOCKS, LANES)
    for kind in range(2):
        for half in range(2):
            for b in range(NBLOCKS):
                flat[pl.ds((kind * ROWS + half * 8) * NBLOCKS + b, 8, stride=NBLOCKS), :] = temp_ref[
                    0, kind, half * 8 : half * 8 + 8, b * LANES : (b + 1) * LANES
                ]

    pl.semaphore_wait(barrier, GROUP - 1 + 2 + NPATCH - 1 + below + above)

    pl.semaphore_signal(
        passed,
        inc=1,
        device_id=(((group + 1) % NGROUPS) * GROUP + cls, p),
        device_id_type=MESH,
    )

    def first_copy(i):
        t, dp, at, n, to = PARTS[i]
        return pltpu.make_async_remote_copy(
            src_ref=mine.at[pl.ds(at, n)],
            dst_ref=recv1.at[pl.ds(cls * SLOT + to, n)],
            send_sem=ssem1.at[i],
            recv_sem=same_sem if dp == 0 else cross_sem,
            device_id=(peer(t), p + dp),
            device_id_type=MESH,
        )

    def sends(i):
        t, dp = PARTS[i][:2]
        if dp == 0:
            return cls != t
        return p < NPATCH - 1 if dp == 1 else p > 0

    for i in range(len(PARTS)):

        @pl.when(sends(i))
        def _(i=i):
            first_copy(i).start()

    for t, dp, at, n, to in PARTS:

        @pl.when(cls == t)
        def _(t=t, dp=dp, at=at, n=n, to=to):
            if dp == 0:
                recv1[pl.ds(t * SLOT + to, n)] = mine[pl.ds(at, n)]

    for t, dp, at, n, to in PARTS:
        if dp == 0:

            @pl.when(cls == t)
            def _(n=n):
                rows = recv1.at[pl.ds(0, (GROUP - 1) * n)]
                pltpu.make_async_copy(rows, rows, same_sem).wait()

        else:

            @pl.when((cls == t) & (p > 0 if dp == 1 else p < NPATCH - 1))
            def _(n=n):
                rows = recv1.at[pl.ds(0, GROUP * n)]
                pltpu.make_async_copy(rows, rows, cross_sem).wait()

    own = pl.ds(cls * SLOT, SLOT)
    fixed = pl.ds((FIXED % GROUP) * SLOT, SLOT)

    def static_copy(g):
        return pltpu.make_async_remote_copy(
            src_ref=recv1.at[fixed],
            dst_ref=ag.at[0, own],
            send_sem=static_send.at[g],
            recv_sem=static_recv,
            device_id=(g * GROUP + cls, p),
            device_id_type=MESH,
        )

    @pl.when(group == FIXED // GROUP)
    def _():
        for g in (0, 2):
            static_copy(g).start()
        ag[0, own] = recv1[fixed]

    other = owners[0] + owners[1] - FIXED
    chosen = recv1[pl.ds((other & 7) * SLOT, SLOT)]
    send2[...] = chosen
    recv2[pl.ds(group * SLOT, SLOT)] = chosen

    def second_copy(d):
        return pltpu.make_async_remote_copy(
            src_ref=send2,
            dst_ref=recv2.at[pl.ds(group * SLOT, SLOT)],
            send_sem=ssem2.at[d],
            recv_sem=rsem2.at[d],
            device_id=(((group + d) % NGROUPS) * GROUP + cls, p),
            device_id_type=MESH,
        )

    second_copy(1).start()
    second_copy(3).start()
    pl.semaphore_wait(passed, 1)

    @pl.when(group == FIXED // GROUP)
    def _():
        static_copy(1).start()

    second_copy(2).start()

    def third_copy(slot, d):
        return pltpu.make_async_remote_copy(
            src_ref=ag.at[slot, own],
            dst_ref=ag.at[slot, own],
            send_sem=ssem3.at[slot, d],
            recv_sem=rsem3.at[slot],
            device_id=(peer((cls + d) % GROUP), p),
            device_id_type=MESH,
        )

    @pl.when(group != FIXED // GROUP)
    def _():
        pltpu.make_async_copy(ag.at[0, own], ag.at[0, own], static_recv).wait()

    for d in range(1, GROUP):
        third_copy(0, d).start()
    for d in range(1, NGROUPS):
        second_copy(d).wait_recv()
    ag[1, own] = recv2[pl.ds(((other >> 3) & 3) * SLOT, SLOT)]
    for d in range(1, GROUP):
        third_copy(1, d).start()

    ag_flat = ag.reshape(STEPS * 56 * NBLOCKS, LANES)
    fixed_step = jnp.where(owners[1] == FIXED, 1, 0)
    for load in loads[1:]:
        load.wait()

    def fourth_copy(slot, d):
        return pltpu.make_async_remote_copy(
            src_ref=red.at[slot, p],
            dst_ref=red.at[slot, p],
            send_sem=ssem4.at[slot, d],
            recv_sem=rsem4.at[slot],
            device_id=(v, (p + d) % NPATCH),
            device_id_type=MESH,
        )

    for slot in range(STEPS):
        rows = ag.at[slot, pl.ds(0, (GROUP - 1) * SLOT)]
        pltpu.make_async_copy(rows, rows, rsem3.at[slot]).wait()
        step = fixed_step if slot == 0 else 1 - fixed_step
        red[slot, p] = packed(
            normal_part(slot, step, ag, ag_flat, cols, basis, col_ref, row_ref, sci_ref, svar_ref, bad_ref)
        )
        for d in range(1, NPATCH):
            fourth_copy(slot, d).start()

    mats = []
    for slot in range(STEPS):
        rows = red.at[slot, pl.ds(0, NPATCH - 1)]
        pltpu.make_async_copy(rows, rows, rsem4.at[slot]).wait()
        total = red[slot, 0]
        for q in range(1, NPATCH):
            total = total + red[slot, q]
        mats.append(unpacked(total))
    coefs = solve(mats)

    for step in range(STEPS):
        slot = jnp.where(fixed_step == step, 0, 1)
        coef = jnp.where(fixed_step == step, coefs[0], coefs[1])

        def one_block(b, carry, step=step, slot=slot, coef=coef):
            at = pl.multiple_of(b * LANES, LANES)
            sums = jnp.zeros((ROWS, 8, LANES), jnp.float32)
            for k in range(NPROF):
                d = basis[slot, b, :, k * LANES : (k + 1) * LANES].reshape(ROWS, 8, LANES)
                sums = sums + d * coef[k * 8 : k * 8 + 8][None]
            out_ref[step, 0, :, pl.ds(at, LANES)] = -jnp.sum(sums, axis=1)
            return carry

        lax.fori_loop(0, NBLOCKS, one_block, 0, unroll=4)

    for i in range(len(PARTS)):

        @pl.when(sends(i))
        def _(i=i):
            first_copy(i).wait_send()

    @pl.when(group == FIXED // GROUP)
    def _():
        for g in range(NGROUPS - 1):
            static_copy(g).wait_send()

    for d in range(1, NGROUPS):
        second_copy(d).wait_send()
    for slot in range(STEPS):
        for d in range(1, GROUP):
            third_copy(slot, d).wait_send()
        for d in range(1, NPATCH):
            fourth_copy(slot, d).wait_send()


def shards(templates, owners, science, sci_var, bad_pixels):
    hbm = pl.BlockSpec(memory_space=pltpu.HBM)
    row_shape = (NBLOCKS, LANES)
    dma = pltpu.SemaphoreType.DMA
    col_table, rows_table = jnp.asarray(column_table()), jnp.asarray(row_table())
    operands = (templates, science, sci_var, bad_pixels, col_table, rows_table)
    return pl.pallas_call(
        kernel,
        out_shape=jax.ShapeDtypeStruct(science.shape, jnp.float32),
        in_specs=[pl.BlockSpec(memory_space=pltpu.SMEM)] + [hbm] * len(operands),
        out_specs=pl.BlockSpec(memory_space=pltpu.VMEM),
        scratch_shapes=[pltpu.VMEM(x.shape, x.dtype) for x in operands]
        + [
            dma((len(operands),)),
            pltpu.VMEM((2 * ROWS, *row_shape), jnp.float32),
            pltpu.VMEM((GROUP * SLOT, *row_shape), jnp.float32),
            pltpu.VMEM((SLOT, *row_shape), jnp.float32),
            pltpu.VMEM((NGROUPS * SLOT, *row_shape), jnp.float32),
            pltpu.VMEM((STEPS, GROUP * SLOT, *row_shape), jnp.float32),
            pltpu.VMEM((STEPS, NPATCH, 16, LANES), jnp.float32),
            pltpu.VMEM((NPROF * POSITIONS * NBLOCKS, LANES), jnp.float32),
            pltpu.VMEM((STEPS, NBLOCKS, ROWS * 8, NPROF * LANES), jnp.float32),
            dma((len(PARTS),)),
            dma,
            dma,
            dma((NGROUPS,)),
            dma((NGROUPS,)),
            dma((NGROUPS,)),
            dma,
            dma((STEPS, GROUP)),
            dma((STEPS,)),
            dma((STEPS, NPATCH)),
            dma((STEPS,)),
            pltpu.SemaphoreType.REGULAR,
        ],
        compiler_params=pltpu.CompilerParams(
            collective_id=0, has_side_effects=True, vmem_limit_bytes=60 * 1024 * 1024
        ),
        name="difference",
    )(owners, *operands)


def solution(mesh):
    return jax.shard_map(
        shards,
        mesh=mesh,
        in_specs=(
            P("visit", None, "patch", None),
            P(),
            P(None, "visit", "patch", None),
            P(None, "visit", "patch", None),
            P(None, "visit", "patch", None),
        ),
        out_specs=P(None, "visit", "patch", None),
        check_vma=False,
    )
```

```python
import functools

import jax
import jax.numpy as jnp
import ml_dtypes
import numpy as np
from jax import lax
from jax.experimental import pallas as pl
from jax.experimental.pallas import tpu as pltpu
from jax.sharding import PartitionSpec as P

NPROF = 5
RAD = 10
STEPS = 2
RIDGE = 1.0

GROUP = 8
NGROUPS = 4
DEPTHS = 16
NPATCH = 16
SLOT = 7
FIXED = 31
ROWS = 16
LANES = 128
NBLOCKS = 8
SCI = 5
MESH = pl.DeviceIdType.MESH

PARTS = (
    (0, 1, 6, 7, 0),
    (1, 1, 13, 3, 0),
    (1, 0, 0, 3, 3),
    (2, 0, 3, 7, 0),
    (3, 0, 10, 6, 0),
    (4, -1, 0, 7, 0),
    (5, -1, 7, 3, 0),
    (5, 0, 16, 3, 4),
    (6, 0, 19, 7, 0),
    (7, 0, 26, 6, 0),
)
SPREAD = (
    (2, 1, 0, 4),
    (-2, 1, 4, 3),
    (2, 0, 0, 4),
    (-2, 0, 4, 3),
    (1, 1, 0, 7),
    (-1, 1, 0, 7),
    (1, 0, 0, 7),
    (-1, 0, 0, 7),
    (0, 1, 0, 7),
)
VAR_AT = 39
POSITIONS = 40


def image_positions():
    return list(range(0, 13)) + list(range(14, 27)) + list(range(28, 38))


def profile_table():
    offsets = np.arange(-RAD, RAD + 1) * 1.0
    recipe = [(1.0, 0), (1.5, 1), (2.0, 2), (3.0, 0), (4.0, 1)]
    profiles = []
    for spread, degree in recipe[:NPROF]:
        profile = offsets**degree * np.exp(-offsets * offsets / (2.0 * spread * spread))
        for earlier in profiles:
            profile = profile - np.dot(earlier, profile) * earlier
        profile = profile / np.sqrt(np.dot(profile, profile))
        profiles.append(profile)
    return np.stack(profiles)


def column_table():
    prof = profile_table().astype(np.float32)
    table = np.zeros((2 * LANES, NPROF * LANES), np.float32)
    for k in range(NPROF):
        for n in range(LANES):
            first = n + LANES // 2 - RAD
            table[first : first + 2 * RAD + 1, k * LANES + n] = prof[k]
    high, mid, _ = split3(table)
    return np.concatenate([high, mid], axis=1).astype(ml_dtypes.bfloat16)


def split3(x):
    high = x.astype(ml_dtypes.bfloat16).astype(np.float32)
    mid = (x - high).astype(ml_dtypes.bfloat16).astype(np.float32)
    low = (x - high - mid).astype(ml_dtypes.bfloat16).astype(np.float32)
    return high, mid, low


def row_table():
    prof = profile_table().astype(np.float32)
    places = image_positions()
    table = np.zeros((ROWS * 8, POSITIONS), np.float32)
    for h in range(ROWS):
        for l in range(NPROF):
            for a in range(2 * RAD + 1):
                table[h * 8 + l, places[h + a]] = prof[l, a]
    high, mid, low = split3(table)
    return np.concatenate([high, high, high, mid, mid, low], axis=1).astype(ml_dtypes.bfloat16)


def rounded(x):
    return x.astype(jnp.bfloat16).astype(jnp.float32)


def normal_part(slot, step, ag, ag_flat, cols, basis, col_ref, row_ref, sci_ref, svar_ref, bad_ref):
    x = ag[slot, 0:POSITIONS]
    y = pltpu.roll(x, LANES // 2, 2)
    lane = lax.broadcasted_iota(jnp.int32, y.shape, 2)
    block = lax.broadcasted_iota(jnp.int32, y.shape, 1)
    before = jnp.where(block == 0, 0.0, pltpu.roll(y, 1, 1))
    after = jnp.where(block == NBLOCKS - 1, 0.0, pltpu.roll(y, NBLOCKS - 1, 1))
    low = lane < LANES // 2
    left = jnp.where(low, before, y).reshape(POSITIONS * NBLOCKS, LANES)
    right = jnp.where(low, y, after).reshape(POSITIONS * NBLOCKS, LANES)
    window = jnp.concatenate([left, right], axis=1)
    height = POSITIONS * NBLOCKS
    high = rounded(window)
    both = jnp.concatenate([high, window - high], axis=0).astype(jnp.bfloat16)
    for k in range(NPROF):
        table = col_ref[:, k * LANES : (k + 1) * LANES]
        rest = col_ref[:, (NPROF + k) * LANES : (NPROF + k + 1) * LANES]
        main = jnp.dot(both, table, preferred_element_type=jnp.float32)
        more = jnp.dot(both[0:height], rest, preferred_element_type=jnp.float32)
        cols[k * height : (k + 1) * height, :] = main[0:height] + (main[height:] + more)

    def one_block(b, total):
        at = pl.multiple_of(b * LANES, LANES)
        c = jnp.concatenate(
            [
                cols[pl.ds(k * height + b, POSITIONS, stride=NBLOCKS), :]
                for k in range(NPROF)
            ],
            axis=1,
        )
        high = rounded(c)
        rest = c - high
        mid = rounded(rest)
        low = rest - mid
        stacked = jnp.concatenate([high, mid, low, high, mid, high], axis=0).astype(jnp.bfloat16)
        d = jnp.dot(row_ref[...], stacked, preferred_element_type=jnp.float32)
        science = sci_ref[step, 0, :, pl.ds(at, LANES)]
        usable = (1 - bad_ref[step, 0, :, pl.ds(at, LANES)]).astype(jnp.float32)
        tile_var = ag_flat[pl.ds((slot * 56 + VAR_AT) * NBLOCKS + b, ROWS, stride=NBLOCKS), :]
        scale = usable / jnp.sqrt(svar_ref[step, 0, :, pl.ds(at, LANES)] + tile_var)
        spread = jnp.broadcast_to(scale[:, None, :], (ROWS, 8, LANES)).reshape(ROWS * 8, LANES)
        sci_spread = jnp.broadcast_to(science[:, None, :], (ROWS, 8, LANES)).reshape(ROWS * 8, LANES)
        place = lax.broadcasted_iota(jnp.int32, (ROWS * 8, LANES), 0) & 7
        parts = [d[:, k * LANES : (k + 1) * LANES] for k in range(NPROF)]
        parts[0] = jnp.where(place == SCI, sci_spread, parts[0])
        parts = [part * spread for part in parts]
        for k in range(NPROF):
            basis[slot, b, :, k * LANES : (k + 1) * LANES] = parts[k]

        def arranged(pieces):
            return jnp.concatenate(
                [
                    jnp.concatenate([piece[h * 8 : h * 8 + 8] for piece in pieces], axis=0)
                    for h in range(ROWS)
                ],
                axis=1,
            ).astype(jnp.bfloat16)

        highs = [rounded(part) for part in parts]
        rests = [part - h for part, h in zip(parts, highs)]
        return total + lax.dot_general(
            arranged(highs + rests),
            arranged(highs),
            (((1,), (1,)), ((), ())),
            preferred_element_type=jnp.float32,
        )

    total = lax.fori_loop(0, NBLOCKS, one_block, jnp.zeros((80, 40), jnp.float32), unroll=4)
    return total[0:40] + (total[40:80] + total[40:80].T)


def packed(mat):
    wide = jnp.concatenate([mat, jnp.zeros((40, LANES - 40), jnp.float32)], axis=1)
    first = wide[0:8] + pltpu.roll(wide[8:16], 40, 1) + pltpu.roll(wide[16:24], 80, 1)
    return jnp.concatenate([first, wide[24:32] + pltpu.roll(wide[32:40], 40, 1)], axis=0)


def unpacked(tiles):
    first, second = tiles[0:8], tiles[8:16]
    return jnp.concatenate(
        [
            first,
            pltpu.roll(first, LANES - 40, 1),
            pltpu.roll(first, LANES - 80, 1),
            second,
            pltpu.roll(second, LANES - 40, 1),
        ],
        axis=0,
    )


def solve(mats):
    row = lax.broadcasted_iota(jnp.int32, (40, LANES), 0)
    col = lax.broadcasted_iota(jnp.int32, (40, LANES), 1)
    mats = [m + jnp.where(row == col, RIDGE, 0.0) for m in mats]
    for k in range(NPROF):
        for l in range(NPROF):
            p = k * 8 + l
            for s in range(STEPS):
                m = mats[s]
                pivot = m[p : p + 1, :] / m[p : p + 1, p : p + 1]
                mats[s] = jnp.where(row == p, pivot, m - m[:, p : p + 1] * pivot)
    return [
        jnp.where(row == SCI, -1.0, jnp.broadcast_to(m[:, SCI : SCI + 1], (40, LANES)))
        for m in mats
    ]


def kernel(
    owners, temp_hbm, sci_hbm, svar_hbm, bad_hbm, col_hbm, row_hbm, out_ref,
    temp_ref, sci_ref, svar_ref, bad_ref, col_ref, row_ref, load_sem,
    mine, recv1, send2, recv2, ag, red, cols, basis,
    ssem1, same_sem, cross_sem, ssem2, rsem2, static_send, static_recv, ssem3, rsem3, ssem4, rsem4, passed,
):
    v = lax.axis_index("visit")
    p = lax.axis_index("patch")
    group = v // GROUP
    cls = v % GROUP
    depth = v // 2
    side = v % 2
    deep = cls // 2

    def near(dz, dx):
        return ((depth + dz + DEPTHS) % DEPTHS) * 2 + (side + dx) % 2

    def holder(t):
        return ((depth + (t // 2 - deep + 5) % 4 - 1 + DEPTHS) % DEPTHS) * 2 + t % 2

    loads = [
        pltpu.make_async_copy(src, dst, load_sem.at[i])
        for i, (src, dst) in enumerate(
            (
                (temp_hbm, temp_ref),
                (col_hbm, col_ref),
                (row_hbm, row_ref),
                (svar_hbm, svar_ref),
                (bad_hbm, bad_ref),
                (sci_hbm, sci_ref),
            )
        )
    ]
    for load in loads:
        load.start()

    recv1[...] = jnp.zeros_like(recv1)

    barrier = pltpu.get_barrier_semaphore()

    def greet(vv, pp):
        pl.semaphore_signal(barrier, inc=1, device_id=(vv, pp), device_id_type=MESH)

    for dz in range(-2, 3):
        for dx in range(2):
            if (dz, dx) != (0, 0):
                greet(near(dz, dx), p)
    for d in (1, 3):
        greet(((group + d) % NGROUPS) * GROUP + cls, p)
    for d in range(1, NPATCH):
        greet(v, (p + d) % NPATCH)

    @pl.when((cls < 2) & (p > 0))
    def _():
        for dz in range(-2, 2):
            for dx in range(2):
                if (dz, dx) != (0, 0):
                    greet(near(dz, dx), p - 1)

    @pl.when(((cls == 4) | (cls == 5)) & (p < NPATCH - 1))
    def _():
        for dz in range(-2, 2):
            for dx in range(2):
                if (dz, dx) != (0, 0):
                    greet(near(dz, dx), p + 1)

    below = jnp.where(p < NPATCH - 1, jnp.where(cls < 2, 1, 2), 0)
    above = jnp.where(p > 0, jnp.where((cls == 4) | (cls == 5), 1, 2), 0)
    loads[0].wait()
    flat = mine.reshape(2 * ROWS * NBLOCKS, LANES)
    for kind in range(2):
        for half in range(2):
            for b in range(NBLOCKS):
                flat[pl.ds((kind * ROWS + half * 8) * NBLOCKS + b, 8, stride=NBLOCKS), :] = temp_ref[
                    0, kind, half * 8 : half * 8 + 8, b * LANES : (b + 1) * LANES
                ]

    pl.semaphore_wait(barrier, 9 + 2 + NPATCH - 1 + below + above)

    pl.semaphore_signal(
        passed,
        inc=1,
        device_id=(((group + 1) % NGROUPS) * GROUP + cls, p),
        device_id_type=MESH,
    )

    def first_copy(i):
        t, dp, at, n, to = PARTS[i]
        return pltpu.make_async_remote_copy(
            src_ref=mine.at[pl.ds(at, n)],
            dst_ref=recv1.at[pl.ds((((deep - t // 2 + 2) & 3) * 2 + side) * SLOT + to, n)],
            send_sem=ssem1.at[i],
            recv_sem=same_sem if dp == 0 else cross_sem,
            device_id=(holder(t), p + dp),
            device_id_type=MESH,
        )

    def sends(i):
        t, dp = PARTS[i][:2]
        if dp == 0:
            return cls != t
        return p < NPATCH - 1 if dp == 1 else p > 0

    for i in range(len(PARTS)):

        @pl.when(sends(i))
        def _(i=i):
            first_copy(i).start()

    for t, dp, at, n, to in PARTS:

        @pl.when(cls == t)
        def _(t=t, dp=dp, at=at, n=n, to=to):
            if dp == 0:
                recv1[pl.ds((4 + t % 2) * SLOT + to, n)] = mine[pl.ds(at, n)]

    for t, dp, at, n, to in PARTS:
        if dp == 0:

            @pl.when(cls == t)
            def _(n=n):
                rows = recv1.at[pl.ds(0, (GROUP - 1) * n)]
                pltpu.make_async_copy(rows, rows, same_sem).wait()

        else:

            @pl.when((cls == t) & (p > 0 if dp == 1 else p < NPATCH - 1))
            def _(n=n):
                rows = recv1.at[pl.ds(0, GROUP * n)]
                pltpu.make_async_copy(rows, rows, cross_sem).wait()

    own = pl.ds(cls * SLOT, SLOT)
    fixed = pl.ds((((FIXED // 2 + 2 - deep) & 3) * 2 + FIXED % 2) * SLOT, SLOT)
    fixed_group = ((FIXED // 2 + 2 - deep) & (DEPTHS - 1)) >> 2
    from_fixed = group == fixed_group

    def static_copy(g):
        return pltpu.make_async_remote_copy(
            src_ref=recv1.at[fixed],
            dst_ref=ag.at[0, own],
            send_sem=static_send.at[g],
            recv_sem=static_recv,
            device_id=(((group + g) % NGROUPS) * GROUP + cls, p),
            device_id_type=MESH,
        )

    @pl.when(from_fixed)
    def _():
        for d in (1, 3):
            static_copy(d).start()
        ag[0, own] = recv1[fixed]

    other = owners[0] + owners[1] - FIXED
    far = (other >> 1) + 2 - deep
    chosen = recv1[pl.ds(((far & 3) * 2 + (other & 1)) * SLOT, SLOT)]
    send2[...] = chosen
    recv2[pl.ds(group * SLOT, SLOT)] = chosen

    def second_copy(d):
        return pltpu.make_async_remote_copy(
            src_ref=send2,
            dst_ref=recv2.at[pl.ds(group * SLOT, SLOT)],
            send_sem=ssem2.at[d],
            recv_sem=rsem2.at[d],
            device_id=(((group + d) % NGROUPS) * GROUP + cls, p),
            device_id_type=MESH,
        )

    second_copy(1).start()
    second_copy(3).start()
    pl.semaphore_wait(passed, 1)

    @pl.when(from_fixed)
    def _():
        static_copy(2).start()

    second_copy(2).start()

    def third_copy(slot, d):
        dz, dx, at, n = SPREAD[d]
        rows = pl.ds(cls * SLOT + at, n)
        return pltpu.make_async_remote_copy(
            src_ref=ag.at[slot, rows],
            dst_ref=ag.at[slot, rows],
            send_sem=ssem3.at[slot, d],
            recv_sem=rsem3.at[slot],
            device_id=(near(dz, dx), p),
            device_id_type=MESH,
        )

    @pl.when(group != fixed_group)
    def _():
        pltpu.make_async_copy(ag.at[0, own], ag.at[0, own], static_recv).wait()

    for d in range(len(SPREAD)):
        third_copy(0, d).start()
    for d in range(1, NGROUPS):
        second_copy(d).wait_recv()
    ag[1, own] = recv2[pl.ds(((far >> 2) & 3) * SLOT, SLOT)]
    for d in range(len(SPREAD)):
        third_copy(1, d).start()

    ag_flat = ag.reshape(STEPS * 56 * NBLOCKS, LANES)
    fixed_step = jnp.where(owners[1] == FIXED, 1, 0)
    for load in loads[1:]:
        load.wait()

    def fourth_copy(slot, d):
        return pltpu.make_async_remote_copy(
            src_ref=red.at[slot, p],
            dst_ref=red.at[slot, p],
            send_sem=ssem4.at[slot, d],
            recv_sem=rsem4.at[slot],
            device_id=(v, (p + d) % NPATCH),
            device_id_type=MESH,
        )

    for slot in range(STEPS):
        rows = ag.at[slot, pl.ds(0, (GROUP - 1) * SLOT)]
        pltpu.make_async_copy(rows, rows, rsem3.at[slot]).wait()
        step = fixed_step if slot == 0 else 1 - fixed_step
        red[slot, p] = packed(
            normal_part(slot, step, ag, ag_flat, cols, basis, col_ref, row_ref, sci_ref, svar_ref, bad_ref)
        )
        for d in range(1, NPATCH):
            fourth_copy(slot, d).start()

    mats = []
    for slot in range(STEPS):
        rows = red.at[slot, pl.ds(0, NPATCH - 1)]
        pltpu.make_async_copy(rows, rows, rsem4.at[slot]).wait()
        total = red[slot, 0]
        for q in range(1, NPATCH):
            total = total + red[slot, q]
        mats.append(unpacked(total))
    coefs = solve(mats)

    for step in range(STEPS):
        slot = jnp.where(fixed_step == step, 0, 1)
        coef = jnp.where(fixed_step == step, coefs[0], coefs[1])

        def one_block(b, carry, step=step, slot=slot, coef=coef):
            at = pl.multiple_of(b * LANES, LANES)
            sums = jnp.zeros((ROWS, 8, LANES), jnp.float32)
            for k in range(NPROF):
                d = basis[slot, b, :, k * LANES : (k + 1) * LANES].reshape(ROWS, 8, LANES)
                sums = sums + d * coef[k * 8 : k * 8 + 8][None]
            out_ref[step, 0, :, pl.ds(at, LANES)] = -jnp.sum(sums, axis=1)
            return carry

        lax.fori_loop(0, NBLOCKS, one_block, 0, unroll=4)

    for i in range(len(PARTS)):

        @pl.when(sends(i))
        def _(i=i):
            first_copy(i).wait_send()

    @pl.when(from_fixed)
    def _():
        for d in range(1, NGROUPS):
            static_copy(d).wait_send()

    for d in range(1, NGROUPS):
        second_copy(d).wait_send()
    for slot in range(STEPS):
        for d in range(len(SPREAD)):
            third_copy(slot, d).wait_send()
        for d in range(1, NPATCH):
            fourth_copy(slot, d).wait_send()


def shards(templates, owners, science, sci_var, bad_pixels):
    hbm = pl.BlockSpec(memory_space=pltpu.HBM)
    row_shape = (NBLOCKS, LANES)
    dma = pltpu.SemaphoreType.DMA
    col_table, rows_table = jnp.asarray(column_table()), jnp.asarray(row_table())
    operands = (templates, science, sci_var, bad_pixels, col_table, rows_table)
    return pl.pallas_call(
        kernel,
        out_shape=jax.ShapeDtypeStruct(science.shape, jnp.float32),
        in_specs=[pl.BlockSpec(memory_space=pltpu.SMEM)] + [hbm] * len(operands),
        out_specs=pl.BlockSpec(memory_space=pltpu.VMEM),
        scratch_shapes=[pltpu.VMEM(x.shape, x.dtype) for x in operands]
        + [
            dma((len(operands),)),
            pltpu.VMEM((2 * ROWS, *row_shape), jnp.float32),
            pltpu.VMEM((GROUP * SLOT, *row_shape), jnp.float32),
            pltpu.VMEM((SLOT, *row_shape), jnp.float32),
            pltpu.VMEM((NGROUPS * SLOT, *row_shape), jnp.float32),
            pltpu.VMEM((STEPS, GROUP * SLOT, *row_shape), jnp.float32),
            pltpu.VMEM((STEPS, NPATCH, 16, LANES), jnp.float32),
            pltpu.VMEM((NPROF * POSITIONS * NBLOCKS, LANES), jnp.float32),
            pltpu.VMEM((STEPS, NBLOCKS, ROWS * 8, NPROF * LANES), jnp.float32),
            dma((len(PARTS),)),
            dma,
            dma,
            dma((NGROUPS,)),
            dma((NGROUPS,)),
            dma((NGROUPS,)),
            dma,
            dma((STEPS, len(SPREAD))),
            dma((STEPS,)),
            dma((STEPS, NPATCH)),
            dma((STEPS,)),
            pltpu.SemaphoreType.REGULAR,
        ],
        compiler_params=pltpu.CompilerParams(
            collective_id=0, has_side_effects=True, vmem_limit_bytes=60 * 1024 * 1024
        ),
        name="difference",
    )(owners, *operands)


def solution(mesh):
    return jax.shard_map(
        shards,
        mesh=mesh,
        in_specs=(
            P("visit", None, "patch", None),
            P(),
            P(None, "visit", "patch", None),
            P(None, "visit", "patch", None),
            P(None, "visit", "patch", None),
        ),
        out_specs=P(None, "visit", "patch", None),
        check_vma=False,
    )
```

```python
import functools

import jax
import jax.numpy as jnp
import ml_dtypes
import numpy as np
from jax import lax
from jax.experimental import pallas as pl
from jax.experimental.pallas import tpu as pltpu
from jax.sharding import PartitionSpec as P

NPROF = 5
RAD = 10
STEPS = 2
RIDGE = 1.0

GROUP = 8
NGROUPS = 4
DEPTHS = 16
NPATCH = 16
SLOT = 7
FIXED = 31
ROWS = 16
LANES = 128
NBLOCKS = 8
SCI = 5
MESH = pl.DeviceIdType.MESH

PARTS = (
    (0, 1, 6, 7, 0),
    (1, 1, 13, 3, 0),
    (1, 0, 0, 3, 3),
    (2, 0, 3, 7, 0),
    (3, 0, 10, 6, 0),
    (4, -1, 0, 7, 0),
    (5, -1, 7, 3, 0),
    (5, 0, 16, 3, 4),
    (6, 0, 19, 7, 0),
    (7, 0, 26, 6, 0),
)
SPREAD = (
    (2, 1, 0, 4),
    (-2, 1, 4, 3),
    (2, 0, 0, 4),
    (-2, 0, 4, 3),
    (1, 1, 0, 7),
    (-1, 1, 0, 7),
    (1, 0, 0, 7),
    (-1, 0, 0, 7),
    (0, 1, 0, 7),
)
VAR_AT = 39
POSITIONS = 40


def image_positions():
    return list(range(0, 13)) + list(range(14, 27)) + list(range(28, 38))


def profile_table():
    offsets = np.arange(-RAD, RAD + 1) * 1.0
    recipe = [(1.0, 0), (1.5, 1), (2.0, 2), (3.0, 0), (4.0, 1)]
    profiles = []
    for spread, degree in recipe[:NPROF]:
        profile = offsets**degree * np.exp(-offsets * offsets / (2.0 * spread * spread))
        for earlier in profiles:
            profile = profile - np.dot(earlier, profile) * earlier
        profile = profile / np.sqrt(np.dot(profile, profile))
        profiles.append(profile)
    return np.stack(profiles)


def column_table():
    prof = profile_table().astype(np.float32)
    table = np.zeros((2 * LANES, NPROF * LANES), np.float32)
    for k in range(NPROF):
        for n in range(LANES):
            first = n + LANES // 2 - RAD
            table[first : first + 2 * RAD + 1, k * LANES + n] = prof[k]
    high, mid, _ = split3(table)
    return np.concatenate([high, mid], axis=1).astype(ml_dtypes.bfloat16)


def split3(x):
    high = x.astype(ml_dtypes.bfloat16).astype(np.float32)
    mid = (x - high).astype(ml_dtypes.bfloat16).astype(np.float32)
    low = (x - high - mid).astype(ml_dtypes.bfloat16).astype(np.float32)
    return high, mid, low


def row_table():
    prof = profile_table().astype(np.float32)
    places = image_positions()
    table = np.zeros((ROWS * 8, POSITIONS), np.float32)
    for h in range(ROWS):
        for l in range(NPROF):
            for a in range(2 * RAD + 1):
                table[h * 8 + l, places[h + a]] = prof[l, a]
    high, mid, _ = split3(table)
    blank = np.zeros((ROWS * 8, 8), np.float32)
    return np.concatenate([high, high, mid, blank], axis=1).astype(ml_dtypes.bfloat16)


def rounded(x):
    return x.astype(jnp.bfloat16).astype(jnp.float32)


def normal_part(slot, step, ag, ag_flat, cols, basis, col_ref, row_ref, sci_ref, svar_ref, bad_ref):
    x = ag[slot, 0:POSITIONS]
    y = pltpu.roll(x, LANES // 2, 2)
    lane = lax.broadcasted_iota(jnp.int32, y.shape, 2)
    block = lax.broadcasted_iota(jnp.int32, y.shape, 1)
    before = jnp.where(block == 0, 0.0, pltpu.roll(y, 1, 1))
    after = jnp.where(block == NBLOCKS - 1, 0.0, pltpu.roll(y, NBLOCKS - 1, 1))
    low = lane < LANES // 2
    left = jnp.where(low, before, y).reshape(POSITIONS * NBLOCKS, LANES)
    right = jnp.where(low, y, after).reshape(POSITIONS * NBLOCKS, LANES)
    window = jnp.concatenate([left, right], axis=1)
    height = POSITIONS * NBLOCKS
    high = rounded(window)
    both = jnp.concatenate([high, window - high], axis=0).astype(jnp.bfloat16)
    for k in range(NPROF):
        table = col_ref[:, k * LANES : (k + 1) * LANES]
        rest = col_ref[:, (NPROF + k) * LANES : (NPROF + k + 1) * LANES]
        main = jnp.dot(both, table, preferred_element_type=jnp.float32)
        more = jnp.dot(both[0:height], rest, preferred_element_type=jnp.float32)
        cols[k * height : (k + 1) * height, :] = main[0:height] + (main[height:] + more)

    def one_block(b, total):
        at = pl.multiple_of(b * LANES, LANES)
        c = jnp.concatenate(
            [
                cols[pl.ds(k * height + b, POSITIONS, stride=NBLOCKS), :]
                for k in range(NPROF)
            ],
            axis=1,
        )
        high = rounded(c)
        blank = jnp.zeros((8, NPROF * LANES), jnp.float32)
        stacked = jnp.concatenate([high, c - high, high, blank], axis=0).astype(jnp.bfloat16)
        d = jnp.dot(row_ref[...], stacked, preferred_element_type=jnp.float32)
        science = sci_ref[step, 0, :, pl.ds(at, LANES)]
        usable = (1 - bad_ref[step, 0, :, pl.ds(at, LANES)]).astype(jnp.float32)
        tile_var = ag_flat[pl.ds((slot * 56 + VAR_AT) * NBLOCKS + b, ROWS, stride=NBLOCKS), :]
        scale = usable / jnp.sqrt(svar_ref[step, 0, :, pl.ds(at, LANES)] + tile_var)
        spread = jnp.broadcast_to(scale[:, None, :], (ROWS, 8, LANES)).reshape(ROWS * 8, LANES)
        sci_spread = jnp.broadcast_to(science[:, None, :], (ROWS, 8, LANES)).reshape(ROWS * 8, LANES)
        place = lax.broadcasted_iota(jnp.int32, (ROWS * 8, LANES), 0) & 7
        parts = [d[:, k * LANES : (k + 1) * LANES] for k in range(NPROF)]
        parts[0] = jnp.where(place == SCI, sci_spread, parts[0])
        parts = [part * spread for part in parts]
        for k in range(NPROF):
            basis[slot, b, :, k * LANES : (k + 1) * LANES] = parts[k]

        def arranged(pieces):
            return jnp.concatenate(
                [
                    jnp.concatenate([piece[h * 8 : h * 8 + 8] for piece in pieces], axis=0)
                    for h in range(ROWS)
                ],
                axis=1,
            ).astype(jnp.bfloat16)

        highs = [rounded(part) for part in parts]
        rests = [part - h for part, h in zip(parts, highs)]
        return total + lax.dot_general(
            arranged(highs + rests),
            arranged(highs),
            (((1,), (1,)), ((), ())),
            preferred_element_type=jnp.float32,
        )

    total = lax.fori_loop(0, NBLOCKS, one_block, jnp.zeros((80, 40), jnp.float32), unroll=4)
    return total[0:40] + (total[40:80] + total[40:80].T)


def packed(mat):
    wide = jnp.concatenate([mat, jnp.zeros((40, LANES - 40), jnp.float32)], axis=1)
    first = wide[0:8] + pltpu.roll(wide[8:16], 40, 1) + pltpu.roll(wide[16:24], 80, 1)
    return jnp.concatenate([first, wide[24:32] + pltpu.roll(wide[32:40], 40, 1)], axis=0)


def unpacked(tiles):
    first, second = tiles[0:8], tiles[8:16]
    return jnp.concatenate(
        [
            first,
            pltpu.roll(first, LANES - 40, 1),
            pltpu.roll(first, LANES - 80, 1),
            second,
            pltpu.roll(second, LANES - 40, 1),
        ],
        axis=0,
    )


def solve(mats):
    row = lax.broadcasted_iota(jnp.int32, (40, LANES), 0)
    col = lax.broadcasted_iota(jnp.int32, (40, LANES), 1)
    mats = [m + jnp.where(row == col, RIDGE, 0.0) for m in mats]
    for k in range(NPROF):
        for l in range(NPROF):
            p = k * 8 + l
            for s in range(len(mats)):
                m = mats[s]
                pivot = m[p : p + 1, :] / m[p : p + 1, p : p + 1]
                mats[s] = jnp.where(row == p, pivot, m - m[:, p : p + 1] * pivot)
    return [
        jnp.where(row == SCI, -1.0, jnp.broadcast_to(m[:, SCI : SCI + 1], (40, LANES)))
        for m in mats
    ]


def kernel(
    owners, temp_hbm, sci_hbm, svar_hbm, bad_hbm, col_hbm, row_hbm, out_ref,
    temp_ref, sci_ref, svar_ref, bad_ref, col_ref, row_ref, load_sem,
    mine, recv1, send2, recv2, ag, red, cols, basis, fitted,
    ssem1, same_sem, cross_sem, ssem2, rsem2, static_send, static_recv, ssem3, rsem3, ssem4, rsem4, passed,
):
    v = lax.axis_index("visit")
    p = lax.axis_index("patch")
    group = v // GROUP
    cls = v % GROUP
    depth = v // 2
    side = v % 2
    deep = cls // 2

    def near(dz, dx):
        return ((depth + dz + DEPTHS) % DEPTHS) * 2 + (side + dx) % 2

    def holder(t):
        return ((depth + (t // 2 - deep + 5) % 4 - 1 + DEPTHS) % DEPTHS) * 2 + t % 2

    loads = [
        pltpu.make_async_copy(src, dst, load_sem.at[i])
        for i, (src, dst) in enumerate(
            (
                (temp_hbm, temp_ref),
                (col_hbm, col_ref),
                (row_hbm, row_ref),
                (svar_hbm, svar_ref),
                (bad_hbm, bad_ref),
                (sci_hbm, sci_ref),
            )
        )
    ]
    for load in loads:
        load.start()

    recv1[...] = jnp.zeros_like(recv1)

    barrier = pltpu.get_barrier_semaphore()

    def greet(vv, pp):
        pl.semaphore_signal(barrier, inc=1, device_id=(vv, pp), device_id_type=MESH)

    for dz in range(-2, 3):
        for dx in range(2):
            if (dz, dx) != (0, 0):
                greet(near(dz, dx), p)
    for d in (1, 3):
        greet(((group + d) % NGROUPS) * GROUP + cls, p)
    for d in range(1, NPATCH):
        greet(v, (p + d) % NPATCH)

    @pl.when((cls < 2) & (p > 0))
    def _():
        for dz in range(-2, 2):
            for dx in range(2):
                if (dz, dx) != (0, 0):
                    greet(near(dz, dx), p - 1)

    @pl.when(((cls == 4) | (cls == 5)) & (p < NPATCH - 1))
    def _():
        for dz in range(-2, 2):
            for dx in range(2):
                if (dz, dx) != (0, 0):
                    greet(near(dz, dx), p + 1)

    below = jnp.where(p < NPATCH - 1, jnp.where(cls < 2, 1, 2), 0)
    above = jnp.where(p > 0, jnp.where((cls == 4) | (cls == 5), 1, 2), 0)
    loads[0].wait()
    flat = mine.reshape(2 * ROWS * NBLOCKS, LANES)
    for kind in range(2):
        for half in range(2):
            for b in range(NBLOCKS):
                flat[pl.ds((kind * ROWS + half * 8) * NBLOCKS + b, 8, stride=NBLOCKS), :] = temp_ref[
                    0, kind, half * 8 : half * 8 + 8, b * LANES : (b + 1) * LANES
                ]

    pl.semaphore_wait(barrier, 9 + 2 + NPATCH - 1 + below + above)

    pl.semaphore_signal(
        passed,
        inc=1,
        device_id=(((group + 1) % NGROUPS) * GROUP + cls, p),
        device_id_type=MESH,
    )

    def first_copy(i):
        t, dp, at, n, to = PARTS[i]
        return pltpu.make_async_remote_copy(
            src_ref=mine.at[pl.ds(at, n)],
            dst_ref=recv1.at[pl.ds((((deep - t // 2 + 2) & 3) * 2 + side) * SLOT + to, n)],
            send_sem=ssem1.at[i],
            recv_sem=same_sem if dp == 0 else cross_sem,
            device_id=(holder(t), p + dp),
            device_id_type=MESH,
        )

    def sends(i):
        t, dp = PARTS[i][:2]
        if dp == 0:
            return cls != t
        return p < NPATCH - 1 if dp == 1 else p > 0

    for i in range(len(PARTS)):

        @pl.when(sends(i))
        def _(i=i):
            first_copy(i).start()

    for t, dp, at, n, to in PARTS:

        @pl.when(cls == t)
        def _(t=t, dp=dp, at=at, n=n, to=to):
            if dp == 0:
                recv1[pl.ds((4 + t % 2) * SLOT + to, n)] = mine[pl.ds(at, n)]

    for t, dp, at, n, to in PARTS:
        if dp == 0:

            @pl.when(cls == t)
            def _(n=n):
                rows = recv1.at[pl.ds(0, (GROUP - 1) * n)]
                pltpu.make_async_copy(rows, rows, same_sem).wait()

        else:

            @pl.when((cls == t) & (p > 0 if dp == 1 else p < NPATCH - 1))
            def _(n=n):
                rows = recv1.at[pl.ds(0, GROUP * n)]
                pltpu.make_async_copy(rows, rows, cross_sem).wait()

    own = pl.ds(cls * SLOT, SLOT)
    fixed = pl.ds((((FIXED // 2 + 2 - deep) & 3) * 2 + FIXED % 2) * SLOT, SLOT)
    fixed_group = ((FIXED // 2 + 2 - deep) & (DEPTHS - 1)) >> 2
    from_fixed = group == fixed_group

    def static_copy(g):
        return pltpu.make_async_remote_copy(
            src_ref=recv1.at[fixed],
            dst_ref=ag.at[0, own],
            send_sem=static_send.at[g],
            recv_sem=static_recv,
            device_id=(((group + g) % NGROUPS) * GROUP + cls, p),
            device_id_type=MESH,
        )

    @pl.when(from_fixed)
    def _():
        for d in (1, 3):
            static_copy(d).start()
        ag[0, own] = recv1[fixed]

    other = owners[0] + owners[1] - FIXED
    far = (other >> 1) + 2 - deep
    chosen = recv1[pl.ds(((far & 3) * 2 + (other & 1)) * SLOT, SLOT)]
    send2[...] = chosen
    recv2[pl.ds(group * SLOT, SLOT)] = chosen

    def second_copy(d):
        return pltpu.make_async_remote_copy(
            src_ref=send2,
            dst_ref=recv2.at[pl.ds(group * SLOT, SLOT)],
            send_sem=ssem2,
            recv_sem=rsem2,
            device_id=(((group + d) % NGROUPS) * GROUP + cls, p),
            device_id_type=MESH,
        )

    second_copy(1).start()
    second_copy(3).start()
    pl.semaphore_wait(passed, 1)

    @pl.when(from_fixed)
    def _():
        static_copy(2).start()

    second_copy(2).start()

    def third_copy(slot, d):
        dz, dx, at, n = SPREAD[d]
        rows = pl.ds(cls * SLOT + at, n)
        return pltpu.make_async_remote_copy(
            src_ref=ag.at[slot, rows],
            dst_ref=ag.at[slot, rows],
            send_sem=ssem3.at[slot],
            recv_sem=rsem3.at[slot],
            device_id=(near(dz, dx), p),
            device_id_type=MESH,
        )

    @pl.when(group != fixed_group)
    def _():
        pltpu.make_async_copy(ag.at[0, own], ag.at[0, own], static_recv).wait()

    for d in range(len(SPREAD)):
        third_copy(0, d).start()
    three = recv2.at[pl.ds(0, (NGROUPS - 1) * SLOT)]
    pltpu.make_async_copy(three, three, rsem2).wait()
    ag[1, own] = recv2[pl.ds(((far >> 2) & 3) * SLOT, SLOT)]
    for d in range(len(SPREAD)):
        third_copy(1, d).start()

    ag_flat = ag.reshape(STEPS * 56 * NBLOCKS, LANES)
    fixed_step = jnp.where(owners[1] == FIXED, 1, 0)
    for load in loads[1:]:
        load.wait()

    def fourth_copy(slot, d):
        return pltpu.make_async_remote_copy(
            src_ref=red.at[slot, p],
            dst_ref=red.at[slot, p],
            send_sem=ssem4.at[slot],
            recv_sem=rsem4.at[slot],
            device_id=(v, (p + d) % NPATCH),
            device_id_type=MESH,
        )

    for slot in range(STEPS):
        rows = ag.at[slot, pl.ds(0, (GROUP - 1) * SLOT)]
        pltpu.make_async_copy(rows, rows, rsem3.at[slot]).wait()
        step = fixed_step if slot == 0 else 1 - fixed_step
        red[slot, p] = packed(
            normal_part(slot, step, ag, ag_flat, cols, basis, col_ref, row_ref, sci_ref, svar_ref, bad_ref)
        )
        for d in range(1, NPATCH):
            fourth_copy(slot, d).start()

    for i in range(len(PARTS)):

        @pl.when(sends(i))
        def _(i=i):
            first_copy(i).wait_send()

    @pl.when(from_fixed)
    def _():
        for d in range(1, NGROUPS):
            static_copy(d).wait_send()

    pltpu.make_async_copy(three, three, ssem2).wait()
    for slot in range(STEPS):
        rows = ag.at[slot, pl.ds(0, (GROUP - 1) * SLOT)]
        pltpu.make_async_copy(rows, rows, ssem3.at[slot]).wait()

    def coefs(slot):
        rows = red.at[slot, pl.ds(0, NPATCH - 1)]
        pltpu.make_async_copy(rows, rows, rsem4.at[slot]).wait()
        total = red[slot, 0]
        for q in range(1, NPATCH):
            total = total + red[slot, q]
        return solve([unpacked(total)])[0]

    def fit(slot, coef, b):
        sums = jnp.zeros((ROWS, 8, LANES), jnp.float32)
        for k in range(NPROF):
            d = basis[slot, b, :, k * LANES : (k + 1) * LANES].reshape(ROWS, 8, LANES)
            sums = sums + d * coef[k * 8 : k * 8 + 8][None]
        return -jnp.sum(sums, axis=1)

    coef0 = coefs(0)

    def fixed_block(b, carry):
        fitted[:, pl.ds(pl.multiple_of(b * LANES, LANES), LANES)] = fit(0, coef0, b)
        return carry

    lax.fori_loop(0, NBLOCKS, fixed_block, 0, unroll=4)
    coef1 = coefs(1)

    def other_block(b, carry):
        at = pl.multiple_of(b * LANES, LANES)
        ours, theirs = fitted[:, pl.ds(at, LANES)], fit(1, coef1, b)
        for step in range(STEPS):
            out_ref[step, 0, :, pl.ds(at, LANES)] = jnp.where(fixed_step == step, ours, theirs)
        return carry

    lax.fori_loop(0, NBLOCKS, other_block, 0, unroll=4)
    for slot in range(STEPS):
        rows = red.at[slot, pl.ds(0, NPATCH - 1)]
        pltpu.make_async_copy(rows, rows, ssem4.at[slot]).wait()


def shards(templates, owners, science, sci_var, bad_pixels):
    hbm = pl.BlockSpec(memory_space=pltpu.HBM)
    row_shape = (NBLOCKS, LANES)
    dma = pltpu.SemaphoreType.DMA
    col_table, rows_table = jnp.asarray(column_table()), jnp.asarray(row_table())
    operands = (templates, science, sci_var, bad_pixels, col_table, rows_table)
    return pl.pallas_call(
        kernel,
        out_shape=jax.ShapeDtypeStruct(science.shape, jnp.float32),
        in_specs=[pl.BlockSpec(memory_space=pltpu.SMEM)] + [hbm] * len(operands),
        out_specs=pl.BlockSpec(memory_space=pltpu.VMEM),
        scratch_shapes=[pltpu.VMEM(x.shape, x.dtype) for x in operands]
        + [
            dma((len(operands),)),
            pltpu.VMEM((2 * ROWS, *row_shape), jnp.float32),
            pltpu.VMEM((GROUP * SLOT, *row_shape), jnp.float32),
            pltpu.VMEM((SLOT, *row_shape), jnp.float32),
            pltpu.VMEM((NGROUPS * SLOT, *row_shape), jnp.float32),
            pltpu.VMEM((STEPS, GROUP * SLOT, *row_shape), jnp.float32),
            pltpu.VMEM((STEPS, NPATCH, 16, LANES), jnp.float32),
            pltpu.VMEM((NPROF * POSITIONS * NBLOCKS, LANES), jnp.float32),
            pltpu.VMEM((STEPS, NBLOCKS, ROWS * 8, NPROF * LANES), jnp.float32),
            pltpu.VMEM((ROWS, NBLOCKS * LANES), jnp.float32),
            dma((len(PARTS),)),
            dma,
            dma,
            dma,
            dma,
            dma((NGROUPS,)),
            dma,
            dma((STEPS,)),
            dma((STEPS,)),
            dma((STEPS,)),
            dma((STEPS,)),
            pltpu.SemaphoreType.REGULAR,
        ],
        compiler_params=pltpu.CompilerParams(
            collective_id=0, has_side_effects=True, vmem_limit_bytes=60 * 1024 * 1024
        ),
        name="difference",
    )(owners, *operands)


def solution(mesh):
    return jax.shard_map(
        shards,
        mesh=mesh,
        in_specs=(
            P("visit", None, "patch", None),
            P(),
            P(None, "visit", "patch", None),
            P(None, "visit", "patch", None),
            P(None, "visit", "patch", None),
        ),
        out_specs=P(None, "visit", "patch", None),
        check_vma=False,
    )
```

```python
import functools

import jax
import jax.numpy as jnp
import ml_dtypes
import numpy as np
from jax import lax
from jax.experimental import pallas as pl
from jax.experimental.pallas import tpu as pltpu
from jax.sharding import PartitionSpec as P

NPROF = 5
RAD = 10
STEPS = 2
RIDGE = 1.0

GROUP = 8
NGROUPS = 4
DEPTHS = 16
NPATCH = 16
SLOT = 7
FIXED = 31
ROWS = 16
LANES = 128
NBLOCKS = 8
SCI = 5
MESH = pl.DeviceIdType.MESH

PARTS = (
    (0, 1, 6, 7, 0),
    (1, 1, 13, 3, 0),
    (1, 0, 0, 3, 3),
    (2, 0, 3, 7, 0),
    (3, 0, 10, 6, 0),
    (4, -1, 0, 7, 0),
    (5, -1, 7, 3, 0),
    (5, 0, 16, 3, 4),
    (6, 0, 19, 7, 0),
    (7, 0, 26, 6, 0),
)
SPREAD = (
    (2, 1, 0, 4),
    (-2, 1, 4, 3),
    (2, 0, 0, 4),
    (-2, 0, 4, 3),
    (1, 1, 0, 7),
    (-1, 1, 0, 7),
    (1, 0, 0, 7),
    (-1, 0, 0, 7),
    (0, 1, 0, 7),
)
VAR_AT = 39
POSITIONS = 40


def image_positions():
    return list(range(0, 13)) + list(range(14, 27)) + list(range(28, 38))


def profile_table():
    offsets = np.arange(-RAD, RAD + 1) * 1.0
    recipe = [(1.0, 0), (1.5, 1), (2.0, 2), (3.0, 0), (4.0, 1)]
    profiles = []
    for spread, degree in recipe[:NPROF]:
        profile = offsets**degree * np.exp(-offsets * offsets / (2.0 * spread * spread))
        for earlier in profiles:
            profile = profile - np.dot(earlier, profile) * earlier
        profile = profile / np.sqrt(np.dot(profile, profile))
        profiles.append(profile)
    return np.stack(profiles)


def column_table():
    prof = profile_table().astype(np.float32)
    table = np.zeros((2 * LANES, NPROF * LANES), np.float32)
    for k in range(NPROF):
        for n in range(LANES):
            first = n + LANES // 2 - RAD
            table[first : first + 2 * RAD + 1, k * LANES + n] = prof[k]
    high, mid, _ = split3(table)
    return np.concatenate([high, mid], axis=1).astype(ml_dtypes.bfloat16)


def split3(x):
    high = x.astype(ml_dtypes.bfloat16).astype(np.float32)
    mid = (x - high).astype(ml_dtypes.bfloat16).astype(np.float32)
    low = (x - high - mid).astype(ml_dtypes.bfloat16).astype(np.float32)
    return high, mid, low


def row_table():
    prof = profile_table().astype(np.float32)
    places = image_positions()
    table = np.zeros((ROWS * 8, POSITIONS), np.float32)
    for h in range(ROWS):
        for l in range(NPROF):
            for a in range(2 * RAD + 1):
                table[h * 8 + l, places[h + a]] = prof[l, a]
    high, mid, _ = split3(table)
    blank = np.zeros((ROWS * 8, 8), np.float32)
    return np.concatenate([high, high, mid, blank], axis=1).astype(ml_dtypes.bfloat16)


def rounded(x):
    return x.astype(jnp.bfloat16).astype(jnp.float32)


def normal_part(slot, step, ag, ag_flat, cols, basis, col_ref, row_ref, sci_ref, svar_ref, bad_ref):
    x = ag[slot, 0:POSITIONS]
    y = pltpu.roll(x, LANES // 2, 2)
    lane = lax.broadcasted_iota(jnp.int32, y.shape, 2)
    block = lax.broadcasted_iota(jnp.int32, y.shape, 1)
    before = jnp.where(block == 0, 0.0, pltpu.roll(y, 1, 1))
    after = jnp.where(block == NBLOCKS - 1, 0.0, pltpu.roll(y, NBLOCKS - 1, 1))
    low = lane < LANES // 2
    left = jnp.where(low, before, y).reshape(POSITIONS * NBLOCKS, LANES)
    right = jnp.where(low, y, after).reshape(POSITIONS * NBLOCKS, LANES)
    window = jnp.concatenate([left, right], axis=1)
    height = POSITIONS * NBLOCKS
    high = rounded(window)
    both = jnp.concatenate([high, window - high], axis=0).astype(jnp.bfloat16)
    for k in range(NPROF):
        table = col_ref[:, k * LANES : (k + 1) * LANES]
        rest = col_ref[:, (NPROF + k) * LANES : (NPROF + k + 1) * LANES]
        main = jnp.dot(both, table, preferred_element_type=jnp.float32)
        more = jnp.dot(both[0:height], rest, preferred_element_type=jnp.float32)
        cols[k * height : (k + 1) * height, :] = main[0:height] + (main[height:] + more)

    def one_block(b, total):
        at = pl.multiple_of(b * LANES, LANES)
        c = jnp.concatenate(
            [
                cols[pl.ds(k * height + b, POSITIONS, stride=NBLOCKS), :]
                for k in range(NPROF)
            ],
            axis=1,
        )
        high = rounded(c)
        blank = jnp.zeros((8, NPROF * LANES), jnp.float32)
        stacked = jnp.concatenate([high, c - high, high, blank], axis=0).astype(jnp.bfloat16)
        d = jnp.dot(row_ref[...], stacked, preferred_element_type=jnp.float32)
        science = sci_ref[step, 0, :, pl.ds(at, LANES)]
        usable = (1 - bad_ref[step, 0, :, pl.ds(at, LANES)]).astype(jnp.float32)
        tile_var = ag_flat[pl.ds((slot * 56 + VAR_AT) * NBLOCKS + b, ROWS, stride=NBLOCKS), :]
        scale = usable / jnp.sqrt(svar_ref[step, 0, :, pl.ds(at, LANES)] + tile_var)
        spread = jnp.broadcast_to(scale[:, None, :], (ROWS, 8, LANES)).reshape(ROWS * 8, LANES)
        sci_spread = jnp.broadcast_to(science[:, None, :], (ROWS, 8, LANES)).reshape(ROWS * 8, LANES)
        place = lax.broadcasted_iota(jnp.int32, (ROWS * 8, LANES), 0) & 7
        parts = [d[:, k * LANES : (k + 1) * LANES] for k in range(NPROF)]
        parts[0] = jnp.where(place == SCI, sci_spread, parts[0])
        parts = [part * spread for part in parts]
        for k in range(NPROF):
            basis[slot, b, :, k * LANES : (k + 1) * LANES] = parts[k]

        def arranged(pieces):
            return jnp.concatenate(
                [
                    jnp.concatenate([piece[h * 8 : h * 8 + 8] for piece in pieces], axis=0)
                    for h in range(ROWS)
                ],
                axis=1,
            ).astype(jnp.bfloat16)

        highs = [rounded(part) for part in parts]
        rests = [part - h for part, h in zip(parts, highs)]
        return total + lax.dot_general(
            arranged(highs + rests),
            arranged(highs),
            (((1,), (1,)), ((), ())),
            preferred_element_type=jnp.float32,
        )

    total = lax.fori_loop(0, NBLOCKS, one_block, jnp.zeros((80, 40), jnp.float32), unroll=4)
    return total[0:40] + (total[40:80] + total[40:80].T)


def packed(mat):
    wide = jnp.concatenate([mat, jnp.zeros((40, LANES - 40), jnp.float32)], axis=1)
    first = wide[0:8] + pltpu.roll(wide[8:16], 40, 1) + pltpu.roll(wide[16:24], 80, 1)
    return jnp.concatenate([first, wide[24:32] + pltpu.roll(wide[32:40], 40, 1)], axis=0)


def unpacked(tiles):
    first, second = tiles[0:8], tiles[8:16]
    return jnp.concatenate(
        [
            first,
            pltpu.roll(first, LANES - 40, 1),
            pltpu.roll(first, LANES - 80, 1),
            second,
            pltpu.roll(second, LANES - 40, 1),
        ],
        axis=0,
    )


def solve(mats):
    row = lax.broadcasted_iota(jnp.int32, (40, LANES), 0)
    col = lax.broadcasted_iota(jnp.int32, (40, LANES), 1)
    mats = [m + jnp.where(row == col, RIDGE, 0.0) for m in mats]
    for k in range(NPROF):
        for l in range(NPROF):
            p = k * 8 + l
            for s in range(len(mats)):
                m = mats[s]
                pivot = m[p : p + 1, :] / m[p : p + 1, p : p + 1]
                mats[s] = jnp.where(row == p, pivot, m - m[:, p : p + 1] * pivot)
    return [
        jnp.where(row == SCI, -1.0, jnp.broadcast_to(m[:, SCI : SCI + 1], (40, LANES)))
        for m in mats
    ]


def kernel(
    owners, temp_hbm, sci_hbm, svar_hbm, bad_hbm, col_hbm, row_hbm, out_ref,
    temp_ref, sci_ref, svar_ref, bad_ref, col_ref, row_ref, load_sem,
    mine, recv1, send2, recv2, ag, red, cols, basis, fitted,
    ssem1, same_sem, cross_sem, ssem2, rsem2, static_send, static_recv, ssem3, rsem3, ssem4, rsem4, passed, known,
):
    v = lax.axis_index("visit")
    p = lax.axis_index("patch")
    group = v // GROUP
    cls = v % GROUP
    depth = v // 2
    side = v % 2
    deep = cls // 2

    def near(dz, dx):
        return ((depth + dz + DEPTHS) % DEPTHS) * 2 + (side + dx) % 2

    def holder(t):
        return ((depth + (t // 2 - deep + 5) % 4 - 1 + DEPTHS) % DEPTHS) * 2 + t % 2

    loads = [
        pltpu.make_async_copy(src, dst, load_sem.at[i])
        for i, (src, dst) in enumerate(
            (
                (temp_hbm, temp_ref),
                (col_hbm, col_ref),
                (row_hbm, row_ref),
                (svar_hbm, svar_ref),
                (bad_hbm, bad_ref),
                (sci_hbm, sci_ref),
            )
        )
    ]
    for load in loads:
        load.start()

    recv1[...] = jnp.zeros_like(recv1)

    barrier = pltpu.get_barrier_semaphore()

    def greet(vv, pp):
        pl.semaphore_signal(barrier, inc=1, device_id=(vv, pp), device_id_type=MESH)

    for dz in range(-2, 3):
        for dx in range(2):
            if (dz, dx) != (0, 0):
                greet(near(dz, dx), p)
    for d in (1, 3):
        greet(((group + d) % NGROUPS) * GROUP + cls, p)
    for d in (1, NPATCH - 1):
        greet(v, (p + d) % NPATCH)

    @pl.when((cls < 2) & (p > 0))
    def _():
        for dz in range(-2, 2):
            for dx in range(2):
                if (dz, dx) != (0, 0):
                    greet(near(dz, dx), p - 1)

    @pl.when(((cls == 4) | (cls == 5)) & (p < NPATCH - 1))
    def _():
        for dz in range(-2, 2):
            for dx in range(2):
                if (dz, dx) != (0, 0):
                    greet(near(dz, dx), p + 1)

    below = jnp.where(p < NPATCH - 1, jnp.where(cls < 2, 1, 2), 0)
    above = jnp.where(p > 0, jnp.where((cls == 4) | (cls == 5), 1, 2), 0)
    loads[0].wait()
    flat = mine.reshape(2 * ROWS * NBLOCKS, LANES)
    for kind in range(2):
        for half in range(2):
            for b in range(NBLOCKS):
                flat[pl.ds((kind * ROWS + half * 8) * NBLOCKS + b, 8, stride=NBLOCKS), :] = temp_ref[
                    0, kind, half * 8 : half * 8 + 8, b * LANES : (b + 1) * LANES
                ]

    pl.semaphore_wait(barrier, 9 + 2 + 2 + below + above)

    pl.semaphore_signal(
        passed,
        inc=1,
        device_id=(((group + 1) % NGROUPS) * GROUP + cls, p),
        device_id_type=MESH,
    )

    def first_copy(i):
        t, dp, at, n, to = PARTS[i]
        return pltpu.make_async_remote_copy(
            src_ref=mine.at[pl.ds(at, n)],
            dst_ref=recv1.at[pl.ds((((deep - t // 2 + 2) & 3) * 2 + side) * SLOT + to, n)],
            send_sem=ssem1.at[i],
            recv_sem=same_sem if dp == 0 else cross_sem,
            device_id=(holder(t), p + dp),
            device_id_type=MESH,
        )

    def sends(i):
        t, dp = PARTS[i][:2]
        if dp == 0:
            return cls != t
        return p < NPATCH - 1 if dp == 1 else p > 0

    for i in range(len(PARTS)):

        @pl.when(sends(i))
        def _(i=i):
            first_copy(i).start()

    def spread_word(r):
        for d in (1 << r, NPATCH - (1 << r)):
            pl.semaphore_signal(
                known.at[r], inc=1, device_id=(v, (p + d) % NPATCH), device_id_type=MESH
            )

    spread_word(0)

    for t, dp, at, n, to in PARTS:

        @pl.when(cls == t)
        def _(t=t, dp=dp, at=at, n=n, to=to):
            if dp == 0:
                recv1[pl.ds((4 + t % 2) * SLOT + to, n)] = mine[pl.ds(at, n)]

    for t, dp, at, n, to in PARTS:
        if dp == 0:

            @pl.when(cls == t)
            def _(n=n):
                rows = recv1.at[pl.ds(0, (GROUP - 1) * n)]
                pltpu.make_async_copy(rows, rows, same_sem).wait()

        else:

            @pl.when((cls == t) & (p > 0 if dp == 1 else p < NPATCH - 1))
            def _(n=n):
                rows = recv1.at[pl.ds(0, GROUP * n)]
                pltpu.make_async_copy(rows, rows, cross_sem).wait()

    own = pl.ds(cls * SLOT, SLOT)
    fixed = pl.ds((((FIXED // 2 + 2 - deep) & 3) * 2 + FIXED % 2) * SLOT, SLOT)
    fixed_group = ((FIXED // 2 + 2 - deep) & (DEPTHS - 1)) >> 2
    from_fixed = group == fixed_group

    def static_copy(g):
        return pltpu.make_async_remote_copy(
            src_ref=recv1.at[fixed],
            dst_ref=ag.at[0, own],
            send_sem=static_send.at[g],
            recv_sem=static_recv,
            device_id=(((group + g) % NGROUPS) * GROUP + cls, p),
            device_id_type=MESH,
        )

    pl.semaphore_wait(passed, 1)

    @pl.when(from_fixed)
    def _():
        for d in (2, 1, 3):
            static_copy(d).start()
        ag[0, own] = recv1[fixed]

    other = owners[0] + owners[1] - FIXED
    far = (other >> 1) + 2 - deep
    chosen = recv1[pl.ds(((far & 3) * 2 + (other & 1)) * SLOT, SLOT)]
    send2[...] = chosen
    recv2[pl.ds(group * SLOT, SLOT)] = chosen

    def second_copy(d):
        return pltpu.make_async_remote_copy(
            src_ref=send2,
            dst_ref=recv2.at[pl.ds(group * SLOT, SLOT)],
            send_sem=ssem2,
            recv_sem=rsem2,
            device_id=(((group + d) % NGROUPS) * GROUP + cls, p),
            device_id_type=MESH,
        )

    for d in (2, 1, 3):
        second_copy(d).start()
    pl.semaphore_wait(known.at[0], 2)
    spread_word(1)

    def third_copy(slot, d):
        dz, dx, at, n = SPREAD[d]
        rows = pl.ds(cls * SLOT + at, n)
        return pltpu.make_async_remote_copy(
            src_ref=ag.at[slot, rows],
            dst_ref=ag.at[slot, rows],
            send_sem=ssem3.at[slot],
            recv_sem=rsem3.at[slot],
            device_id=(near(dz, dx), p),
            device_id_type=MESH,
        )

    @pl.when(group != fixed_group)
    def _():
        pltpu.make_async_copy(ag.at[0, own], ag.at[0, own], static_recv).wait()

    for d in range(len(SPREAD)):
        third_copy(0, d).start()
    three = recv2.at[pl.ds(0, (NGROUPS - 1) * SLOT)]
    pltpu.make_async_copy(three, three, rsem2).wait()
    ag[1, own] = recv2[pl.ds(((far >> 2) & 3) * SLOT, SLOT)]
    for d in range(len(SPREAD)):
        third_copy(1, d).start()
    pl.semaphore_wait(known.at[1], 2)
    spread_word(2)

    ag_flat = ag.reshape(STEPS * 56 * NBLOCKS, LANES)
    fixed_step = jnp.where(owners[1] == FIXED, 1, 0)
    for load in loads[1:]:
        load.wait()

    def fourth_copy(slot, d):
        return pltpu.make_async_remote_copy(
            src_ref=red.at[slot, p],
            dst_ref=red.at[slot, p],
            send_sem=ssem4.at[slot],
            recv_sem=rsem4.at[slot],
            device_id=(v, (p + d) % NPATCH),
            device_id_type=MESH,
        )

    for slot in range(STEPS):
        rows = ag.at[slot, pl.ds(0, (GROUP - 1) * SLOT)]
        pltpu.make_async_copy(rows, rows, rsem3.at[slot]).wait()
        step = fixed_step if slot == 0 else 1 - fixed_step
        red[slot, p] = packed(
            normal_part(slot, step, ag, ag_flat, cols, basis, col_ref, row_ref, sci_ref, svar_ref, bad_ref)
        )
        if slot == 0:
            pl.semaphore_wait(known.at[2], 2)
        for d in range(1, NPATCH):
            fourth_copy(slot, d).start()

    for i in range(len(PARTS)):

        @pl.when(sends(i))
        def _(i=i):
            first_copy(i).wait_send()

    @pl.when(from_fixed)
    def _():
        for d in range(1, NGROUPS):
            static_copy(d).wait_send()

    pltpu.make_async_copy(three, three, ssem2).wait()
    for slot in range(STEPS):
        rows = ag.at[slot, pl.ds(0, (GROUP - 1) * SLOT)]
        pltpu.make_async_copy(rows, rows, ssem3.at[slot]).wait()

    def coefs(slot):
        rows = red.at[slot, pl.ds(0, NPATCH - 1)]
        pltpu.make_async_copy(rows, rows, rsem4.at[slot]).wait()
        total = red[slot, 0]
        for q in range(1, NPATCH):
            total = total + red[slot, q]
        return solve([unpacked(total)])[0]

    def fit(slot, coef, b):
        sums = jnp.zeros((ROWS, 8, LANES), jnp.float32)
        for k in range(NPROF):
            d = basis[slot, b, :, k * LANES : (k + 1) * LANES].reshape(ROWS, 8, LANES)
            sums = sums + d * coef[k * 8 : k * 8 + 8][None]
        return -jnp.sum(sums, axis=1)

    coef0 = coefs(0)

    def fixed_block(b, carry):
        fitted[:, pl.ds(pl.multiple_of(b * LANES, LANES), LANES)] = fit(0, coef0, b)
        return carry

    lax.fori_loop(0, NBLOCKS, fixed_block, 0, unroll=4)
    coef1 = coefs(1)

    def other_block(b, carry):
        at = pl.multiple_of(b * LANES, LANES)
        ours, theirs = fitted[:, pl.ds(at, LANES)], fit(1, coef1, b)
        for step in range(STEPS):
            out_ref[step, 0, :, pl.ds(at, LANES)] = jnp.where(fixed_step == step, ours, theirs)
        return carry

    lax.fori_loop(0, NBLOCKS, other_block, 0, unroll=4)
    for slot in range(STEPS):
        rows = red.at[slot, pl.ds(0, NPATCH - 1)]
        pltpu.make_async_copy(rows, rows, ssem4.at[slot]).wait()


def shards(templates, owners, science, sci_var, bad_pixels):
    hbm = pl.BlockSpec(memory_space=pltpu.HBM)
    row_shape = (NBLOCKS, LANES)
    dma = pltpu.SemaphoreType.DMA
    col_table, rows_table = jnp.asarray(column_table()), jnp.asarray(row_table())
    operands = (templates, science, sci_var, bad_pixels, col_table, rows_table)
    return pl.pallas_call(
        kernel,
        out_shape=jax.ShapeDtypeStruct(science.shape, jnp.float32),
        in_specs=[pl.BlockSpec(memory_space=pltpu.SMEM)] + [hbm] * len(operands),
        out_specs=pl.BlockSpec(memory_space=pltpu.VMEM),
        scratch_shapes=[pltpu.VMEM(x.shape, x.dtype) for x in operands]
        + [
            dma((len(operands),)),
            pltpu.VMEM((2 * ROWS, *row_shape), jnp.float32),
            pltpu.VMEM((GROUP * SLOT, *row_shape), jnp.float32),
            pltpu.VMEM((SLOT, *row_shape), jnp.float32),
            pltpu.VMEM((NGROUPS * SLOT, *row_shape), jnp.float32),
            pltpu.VMEM((STEPS, GROUP * SLOT, *row_shape), jnp.float32),
            pltpu.VMEM((STEPS, NPATCH, 16, LANES), jnp.float32),
            pltpu.VMEM((NPROF * POSITIONS * NBLOCKS, LANES), jnp.float32),
            pltpu.VMEM((STEPS, NBLOCKS, ROWS * 8, NPROF * LANES), jnp.float32),
            pltpu.VMEM((ROWS, NBLOCKS * LANES), jnp.float32),
            dma((len(PARTS),)),
            dma,
            dma,
            dma,
            dma,
            dma((NGROUPS,)),
            dma,
            dma((STEPS,)),
            dma((STEPS,)),
            dma((STEPS,)),
            dma((STEPS,)),
            pltpu.SemaphoreType.REGULAR,
            pltpu.SemaphoreType.REGULAR((3,)),
        ],
        compiler_params=pltpu.CompilerParams(
            collective_id=0, has_side_effects=True, vmem_limit_bytes=60 * 1024 * 1024
        ),
        name="difference",
    )(owners, *operands)


def solution(mesh):
    return jax.shard_map(
        shards,
        mesh=mesh,
        in_specs=(
            P("visit", None, "patch", None),
            P(),
            P(None, "visit", "patch", None),
            P(None, "visit", "patch", None),
            P(None, "visit", "patch", None),
        ),
        out_specs=P(None, "visit", "patch", None),
        check_vma=False,
    )
```

```python
import functools

import jax
import jax.numpy as jnp
import ml_dtypes
import numpy as np
from jax import lax
from jax.experimental import pallas as pl
from jax.experimental.pallas import tpu as pltpu
from jax.sharding import PartitionSpec as P

NPROF = 5
RAD = 10
STEPS = 2
RIDGE = 1.0

GROUP = 8
NGROUPS = 4
DEPTHS = 16
NPATCH = 16
SLOT = 7
FIXED = 31
ROWS = 16
LANES = 128
NBLOCKS = 8
SCI = 5
MESH = pl.DeviceIdType.MESH

PARTS = (
    (0, 1, 6, 7, 0),
    (1, 1, 13, 3, 0),
    (1, 0, 0, 3, 3),
    (2, 0, 3, 7, 0),
    (3, 0, 10, 6, 0),
    (4, -1, 0, 7, 0),
    (5, -1, 7, 3, 0),
    (5, 0, 16, 3, 4),
    (6, 0, 19, 7, 0),
    (7, 0, 26, 6, 0),
)
SPREAD = (
    (2, 1, 0, 4),
    (-2, 1, 4, 3),
    (2, 0, 0, 4),
    (-2, 0, 4, 3),
    (1, 1, 0, 7),
    (-1, 1, 0, 7),
    (1, 0, 0, 7),
    (-1, 0, 0, 7),
    (0, 1, 0, 7),
)
VAR_AT = 39
POSITIONS = 40


def image_positions():
    return list(range(0, 13)) + list(range(14, 27)) + list(range(28, 38))


def profile_table():
    offsets = np.arange(-RAD, RAD + 1) * 1.0
    recipe = [(1.0, 0), (1.5, 1), (2.0, 2), (3.0, 0), (4.0, 1)]
    profiles = []
    for spread, degree in recipe[:NPROF]:
        profile = offsets**degree * np.exp(-offsets * offsets / (2.0 * spread * spread))
        for earlier in profiles:
            profile = profile - np.dot(earlier, profile) * earlier
        profile = profile / np.sqrt(np.dot(profile, profile))
        profiles.append(profile)
    return np.stack(profiles)


def column_table():
    prof = profile_table().astype(np.float32)
    table = np.zeros((2 * LANES, NPROF * LANES), np.float32)
    for k in range(NPROF):
        for n in range(LANES):
            first = n + LANES // 2 - RAD
            table[first : first + 2 * RAD + 1, k * LANES + n] = prof[k]
    high, mid, _ = split3(table)
    return np.concatenate([high, mid], axis=1).astype(ml_dtypes.bfloat16)


def split3(x):
    high = x.astype(ml_dtypes.bfloat16).astype(np.float32)
    mid = (x - high).astype(ml_dtypes.bfloat16).astype(np.float32)
    low = (x - high - mid).astype(ml_dtypes.bfloat16).astype(np.float32)
    return high, mid, low


def row_table():
    prof = profile_table().astype(np.float32)
    places = image_positions()
    table = np.zeros((ROWS * 8, POSITIONS), np.float32)
    for h in range(ROWS):
        for l in range(NPROF):
            for a in range(2 * RAD + 1):
                table[h * 8 + l, places[h + a]] = prof[l, a]
    high, mid, _ = split3(table)
    blank = np.zeros((ROWS * 8, 8), np.float32)
    return np.concatenate([high, high, mid, blank], axis=1).astype(ml_dtypes.bfloat16)


def rounded(x):
    return x.astype(jnp.bfloat16).astype(jnp.float32)


def normal_part(slot, step, ag, ag_flat, cols, basis, col_ref, row_ref, sci_ref, svar_ref, bad_ref):
    x = ag[slot, 0:POSITIONS]
    y = pltpu.roll(x, LANES // 2, 2)
    lane = lax.broadcasted_iota(jnp.int32, y.shape, 2)
    block = lax.broadcasted_iota(jnp.int32, y.shape, 1)
    before = jnp.where(block == 0, 0.0, pltpu.roll(y, 1, 1))
    after = jnp.where(block == NBLOCKS - 1, 0.0, pltpu.roll(y, NBLOCKS - 1, 1))
    low = lane < LANES // 2
    left = jnp.where(low, before, y).reshape(POSITIONS * NBLOCKS, LANES)
    right = jnp.where(low, y, after).reshape(POSITIONS * NBLOCKS, LANES)
    window = jnp.concatenate([left, right], axis=1)
    height = POSITIONS * NBLOCKS
    high = rounded(window)
    both = jnp.concatenate([high, window - high], axis=0).astype(jnp.bfloat16)
    for k in range(NPROF):
        table = col_ref[:, k * LANES : (k + 1) * LANES]
        rest = col_ref[:, (NPROF + k) * LANES : (NPROF + k + 1) * LANES]
        main = jnp.dot(both, table, preferred_element_type=jnp.float32)
        more = jnp.dot(both[0:height], rest, preferred_element_type=jnp.float32)
        cols[k * height : (k + 1) * height, :] = main[0:height] + (main[height:] + more)

    def one_block(b, total):
        at = pl.multiple_of(b * LANES, LANES)
        c = jnp.concatenate(
            [
                cols[pl.ds(k * height + b, POSITIONS, stride=NBLOCKS), :]
                for k in range(NPROF)
            ],
            axis=1,
        )
        high = rounded(c)
        blank = jnp.zeros((8, NPROF * LANES), jnp.float32)
        stacked = jnp.concatenate([high, c - high, high, blank], axis=0).astype(jnp.bfloat16)
        d = jnp.dot(row_ref[...], stacked, preferred_element_type=jnp.float32)
        science = sci_ref[step, 0, :, pl.ds(at, LANES)]
        usable = (1 - bad_ref[step, 0, :, pl.ds(at, LANES)]).astype(jnp.float32)
        tile_var = ag_flat[pl.ds((slot * 56 + VAR_AT) * NBLOCKS + b, ROWS, stride=NBLOCKS), :]
        scale = usable / jnp.sqrt(svar_ref[step, 0, :, pl.ds(at, LANES)] + tile_var)
        spread = jnp.broadcast_to(scale[:, None, :], (ROWS, 8, LANES)).reshape(ROWS * 8, LANES)
        sci_spread = jnp.broadcast_to(science[:, None, :], (ROWS, 8, LANES)).reshape(ROWS * 8, LANES)
        place = lax.broadcasted_iota(jnp.int32, (ROWS * 8, LANES), 0) & 7
        parts = [d[:, k * LANES : (k + 1) * LANES] for k in range(NPROF)]
        parts[0] = jnp.where(place == SCI, sci_spread, parts[0])
        parts = [part * spread for part in parts]
        for k in range(NPROF):
            basis[slot, b, :, k * LANES : (k + 1) * LANES] = parts[k]

        def arranged(pieces):
            return jnp.concatenate(
                [
                    jnp.concatenate([piece[h * 8 : h * 8 + 8] for piece in pieces], axis=0)
                    for h in range(ROWS)
                ],
                axis=1,
            ).astype(jnp.bfloat16)

        highs = [rounded(part) for part in parts]
        rests = [part - h for part, h in zip(parts, highs)]
        return total + lax.dot_general(
            arranged(highs + rests),
            arranged(highs),
            (((1,), (1,)), ((), ())),
            preferred_element_type=jnp.float32,
        )

    total = lax.fori_loop(0, NBLOCKS, one_block, jnp.zeros((80, 40), jnp.float32), unroll=4)
    return total[0:40] + (total[40:80] + total[40:80].T)


def packed(mat):
    wide = jnp.concatenate([mat, jnp.zeros((40, LANES - 40), jnp.float32)], axis=1)
    first = wide[0:8] + pltpu.roll(wide[8:16], 40, 1) + pltpu.roll(wide[16:24], 80, 1)
    return jnp.concatenate([first, wide[24:32] + pltpu.roll(wide[32:40], 40, 1)], axis=0)


def unpacked(tiles):
    first, second = tiles[0:8], tiles[8:16]
    return jnp.concatenate(
        [
            first,
            pltpu.roll(first, LANES - 40, 1),
            pltpu.roll(first, LANES - 80, 1),
            second,
            pltpu.roll(second, LANES - 40, 1),
        ],
        axis=0,
    )


def solve(mats):
    row = lax.broadcasted_iota(jnp.int32, (40, LANES), 0)
    col = lax.broadcasted_iota(jnp.int32, (40, LANES), 1)
    mats = [m + jnp.where(row == col, RIDGE, 0.0) for m in mats]
    for k in range(NPROF):
        pivots = [k * 8 + l for l in range(NPROF)]
        for s, m in enumerate(mats):
            columns = [jnp.broadcast_to(m[:, p : p + 1], (40, LANES)) for p in pivots]
            for i, p in enumerate(pivots):
                ours = columns[i]
                inverse = 1.0 / ours[p : p + 1]
                pivot = m[p : p + 1] * inverse
                m = jnp.where(row == p, pivot, m - ours * pivot)
                for j in range(i + 1, NPROF):
                    other = columns[j][p : p + 1] * inverse
                    columns[j] = jnp.where(row == p, other, columns[j] - ours * other)
            mats[s] = m
    return [
        jnp.where(row == SCI, -1.0, jnp.broadcast_to(m[:, SCI : SCI + 1], (40, LANES)))
        for m in mats
    ]


def kernel(
    owners, temp_hbm, sci_hbm, svar_hbm, bad_hbm, col_hbm, row_hbm, out_ref,
    temp_ref, sci_ref, svar_ref, bad_ref, col_ref, row_ref, load_sem,
    mine, recv1, send2, recv2, ag, red, cols, basis, fitted,
    ssem1, same_sem, cross_sem, ssem2, rsem2, static_send, static_recv, ssem3, rsem3, ssem4, rsem4, passed, known,
):
    v = lax.axis_index("visit")
    p = lax.axis_index("patch")
    group = v // GROUP
    cls = v % GROUP
    depth = v // 2
    side = v % 2
    deep = cls // 2

    def near(dz, dx):
        return ((depth + dz + DEPTHS) % DEPTHS) * 2 + (side + dx) % 2

    def holder(t):
        return ((depth + (t // 2 - deep + 5) % 4 - 1 + DEPTHS) % DEPTHS) * 2 + t % 2

    loads = [
        pltpu.make_async_copy(src, dst, load_sem.at[i])
        for i, (src, dst) in enumerate(
            (
                (temp_hbm, temp_ref),
                (col_hbm, col_ref),
                (row_hbm, row_ref),
                (svar_hbm, svar_ref),
                (bad_hbm, bad_ref),
                (sci_hbm, sci_ref),
            )
        )
    ]
    for load in loads:
        load.start()

    recv1[...] = jnp.zeros_like(recv1)

    barrier = pltpu.get_barrier_semaphore()

    def greet(vv, pp):
        pl.semaphore_signal(barrier, inc=1, device_id=(vv, pp), device_id_type=MESH)

    for dz in range(-2, 3):
        for dx in range(2):
            if (dz, dx) != (0, 0):
                greet(near(dz, dx), p)
    for d in (1, 3):
        greet(((group + d) % NGROUPS) * GROUP + cls, p)
    for d in (1, NPATCH - 1):
        greet(v, (p + d) % NPATCH)

    @pl.when((cls < 2) & (p > 0))
    def _():
        for dz in range(-2, 2):
            for dx in range(2):
                if (dz, dx) != (0, 0):
                    greet(near(dz, dx), p - 1)

    @pl.when(((cls == 4) | (cls == 5)) & (p < NPATCH - 1))
    def _():
        for dz in range(-2, 2):
            for dx in range(2):
                if (dz, dx) != (0, 0):
                    greet(near(dz, dx), p + 1)

    below = jnp.where(p < NPATCH - 1, jnp.where(cls < 2, 1, 2), 0)
    above = jnp.where(p > 0, jnp.where((cls == 4) | (cls == 5), 1, 2), 0)
    loads[0].wait()
    flat = mine.reshape(2 * ROWS * NBLOCKS, LANES)
    for kind in range(2):
        for half in range(2):
            for b in range(NBLOCKS):
                flat[pl.ds((kind * ROWS + half * 8) * NBLOCKS + b, 8, stride=NBLOCKS), :] = temp_ref[
                    0, kind, half * 8 : half * 8 + 8, b * LANES : (b + 1) * LANES
                ]

    pl.semaphore_wait(barrier, 9 + 2 + 2 + below + above)

    pl.semaphore_signal(
        passed,
        inc=1,
        device_id=(((group + 1) % NGROUPS) * GROUP + cls, p),
        device_id_type=MESH,
    )

    def first_copy(i):
        t, dp, at, n, to = PARTS[i]
        return pltpu.make_async_remote_copy(
            src_ref=mine.at[pl.ds(at, n)],
            dst_ref=recv1.at[pl.ds((((deep - t // 2 + 2) & 3) * 2 + side) * SLOT + to, n)],
            send_sem=ssem1.at[i],
            recv_sem=same_sem if dp == 0 else cross_sem,
            device_id=(holder(t), p + dp),
            device_id_type=MESH,
        )

    def sends(i):
        t, dp = PARTS[i][:2]
        if dp == 0:
            return cls != t
        return p < NPATCH - 1 if dp == 1 else p > 0

    for i in range(len(PARTS)):

        @pl.when(sends(i))
        def _(i=i):
            first_copy(i).start()

    def spread_word(r):
        for d in (1 << r, NPATCH - (1 << r)):
            pl.semaphore_signal(
                known.at[r], inc=1, device_id=(v, (p + d) % NPATCH), device_id_type=MESH
            )

    spread_word(0)

    for t, dp, at, n, to in PARTS:

        @pl.when(cls == t)
        def _(t=t, dp=dp, at=at, n=n, to=to):
            if dp == 0:
                recv1[pl.ds((4 + t % 2) * SLOT + to, n)] = mine[pl.ds(at, n)]

    for t, dp, at, n, to in PARTS:
        if dp == 0:

            @pl.when(cls == t)
            def _(n=n):
                rows = recv1.at[pl.ds(0, (GROUP - 1) * n)]
                pltpu.make_async_copy(rows, rows, same_sem).wait()

        else:

            @pl.when((cls == t) & (p > 0 if dp == 1 else p < NPATCH - 1))
            def _(n=n):
                rows = recv1.at[pl.ds(0, GROUP * n)]
                pltpu.make_async_copy(rows, rows, cross_sem).wait()

    own = pl.ds(cls * SLOT, SLOT)
    fixed = pl.ds((((FIXED // 2 + 2 - deep) & 3) * 2 + FIXED % 2) * SLOT, SLOT)
    fixed_group = ((FIXED // 2 + 2 - deep) & (DEPTHS - 1)) >> 2
    from_fixed = group == fixed_group

    def static_copy(g):
        return pltpu.make_async_remote_copy(
            src_ref=recv1.at[fixed],
            dst_ref=ag.at[0, own],
            send_sem=static_send.at[g],
            recv_sem=static_recv,
            device_id=(((group + g) % NGROUPS) * GROUP + cls, p),
            device_id_type=MESH,
        )

    pl.semaphore_wait(passed, 1)

    @pl.when(from_fixed)
    def _():
        for d in (2, 1, 3):
            static_copy(d).start()
        ag[0, own] = recv1[fixed]

    other = owners[0] + owners[1] - FIXED
    far = (other >> 1) + 2 - deep
    chosen = recv1[pl.ds(((far & 3) * 2 + (other & 1)) * SLOT, SLOT)]
    send2[...] = chosen
    recv2[pl.ds(group * SLOT, SLOT)] = chosen

    def second_copy(d):
        return pltpu.make_async_remote_copy(
            src_ref=send2,
            dst_ref=recv2.at[pl.ds(group * SLOT, SLOT)],
            send_sem=ssem2,
            recv_sem=rsem2,
            device_id=(((group + d) % NGROUPS) * GROUP + cls, p),
            device_id_type=MESH,
        )

    for d in (2, 1, 3):
        second_copy(d).start()
    pl.semaphore_wait(known.at[0], 2)
    spread_word(1)

    def third_copy(slot, d):
        dz, dx, at, n = SPREAD[d]
        rows = pl.ds(cls * SLOT + at, n)
        return pltpu.make_async_remote_copy(
            src_ref=ag.at[slot, rows],
            dst_ref=ag.at[slot, rows],
            send_sem=ssem3.at[slot],
            recv_sem=rsem3.at[slot],
            device_id=(near(dz, dx), p),
            device_id_type=MESH,
        )

    @pl.when(group != fixed_group)
    def _():
        pltpu.make_async_copy(ag.at[0, own], ag.at[0, own], static_recv).wait()

    for d in range(len(SPREAD)):
        third_copy(0, d).start()
    three = recv2.at[pl.ds(0, (NGROUPS - 1) * SLOT)]
    pltpu.make_async_copy(three, three, rsem2).wait()
    ag[1, own] = recv2[pl.ds(((far >> 2) & 3) * SLOT, SLOT)]
    for d in range(len(SPREAD)):
        third_copy(1, d).start()
    pl.semaphore_wait(known.at[1], 2)
    spread_word(2)

    ag_flat = ag.reshape(STEPS * 56 * NBLOCKS, LANES)
    fixed_step = jnp.where(owners[1] == FIXED, 1, 0)
    for load in loads[1:]:
        load.wait()

    def fourth_copy(slot, d):
        return pltpu.make_async_remote_copy(
            src_ref=red.at[slot, p],
            dst_ref=red.at[slot, p],
            send_sem=ssem4.at[slot],
            recv_sem=rsem4.at[slot],
            device_id=(v, (p + d) % NPATCH),
            device_id_type=MESH,
        )

    for slot in range(STEPS):
        rows = ag.at[slot, pl.ds(0, (GROUP - 1) * SLOT)]
        pltpu.make_async_copy(rows, rows, rsem3.at[slot]).wait()
        step = fixed_step if slot == 0 else 1 - fixed_step
        red[slot, p] = packed(
            normal_part(slot, step, ag, ag_flat, cols, basis, col_ref, row_ref, sci_ref, svar_ref, bad_ref)
        )
        if slot == 0:
            pl.semaphore_wait(known.at[2], 2)
        for d in range(1, NPATCH):
            fourth_copy(slot, d).start()

    for i in range(len(PARTS)):

        @pl.when(sends(i))
        def _(i=i):
            first_copy(i).wait_send()

    @pl.when(from_fixed)
    def _():
        for d in range(1, NGROUPS):
            static_copy(d).wait_send()

    pltpu.make_async_copy(three, three, ssem2).wait()
    for slot in range(STEPS):
        rows = ag.at[slot, pl.ds(0, (GROUP - 1) * SLOT)]
        pltpu.make_async_copy(rows, rows, ssem3.at[slot]).wait()

    def coefs(slot):
        rows = red.at[slot, pl.ds(0, NPATCH - 1)]
        pltpu.make_async_copy(rows, rows, rsem4.at[slot]).wait()
        total = red[slot, 0]
        for q in range(1, NPATCH):
            total = total + red[slot, q]
        return solve([unpacked(total)])[0]

    def fit(slot, coef, b):
        sums = jnp.zeros((ROWS, 8, LANES), jnp.float32)
        for k in range(NPROF):
            d = basis[slot, b, :, k * LANES : (k + 1) * LANES].reshape(ROWS, 8, LANES)
            sums = sums + d * coef[k * 8 : k * 8 + 8][None]
        return -jnp.sum(sums, axis=1)

    coef0 = coefs(0)

    def fixed_block(b, carry):
        fitted[:, pl.ds(pl.multiple_of(b * LANES, LANES), LANES)] = fit(0, coef0, b)
        return carry

    lax.fori_loop(0, NBLOCKS, fixed_block, 0, unroll=4)
    coef1 = coefs(1)

    def other_block(b, carry):
        at = pl.multiple_of(b * LANES, LANES)
        ours, theirs = fitted[:, pl.ds(at, LANES)], fit(1, coef1, b)
        for step in range(STEPS):
            out_ref[step, 0, :, pl.ds(at, LANES)] = jnp.where(fixed_step == step, ours, theirs)
        return carry

    lax.fori_loop(0, NBLOCKS, other_block, 0, unroll=4)
    for slot in range(STEPS):
        rows = red.at[slot, pl.ds(0, NPATCH - 1)]
        pltpu.make_async_copy(rows, rows, ssem4.at[slot]).wait()


def shards(templates, owners, science, sci_var, bad_pixels):
    hbm = pl.BlockSpec(memory_space=pltpu.HBM)
    row_shape = (NBLOCKS, LANES)
    dma = pltpu.SemaphoreType.DMA
    col_table, rows_table = jnp.asarray(column_table()), jnp.asarray(row_table())
    operands = (templates, science, sci_var, bad_pixels, col_table, rows_table)
    return pl.pallas_call(
        kernel,
        out_shape=jax.ShapeDtypeStruct(science.shape, jnp.float32),
        in_specs=[pl.BlockSpec(memory_space=pltpu.SMEM)] + [hbm] * len(operands),
        out_specs=pl.BlockSpec(memory_space=pltpu.VMEM),
        scratch_shapes=[pltpu.VMEM(x.shape, x.dtype) for x in operands]
        + [
            dma((len(operands),)),
            pltpu.VMEM((2 * ROWS, *row_shape), jnp.float32),
            pltpu.VMEM((GROUP * SLOT, *row_shape), jnp.float32),
            pltpu.VMEM((SLOT, *row_shape), jnp.float32),
            pltpu.VMEM((NGROUPS * SLOT, *row_shape), jnp.float32),
            pltpu.VMEM((STEPS, GROUP * SLOT, *row_shape), jnp.float32),
            pltpu.VMEM((STEPS, NPATCH, 16, LANES), jnp.float32),
            pltpu.VMEM((NPROF * POSITIONS * NBLOCKS, LANES), jnp.float32),
            pltpu.VMEM((STEPS, NBLOCKS, ROWS * 8, NPROF * LANES), jnp.float32),
            pltpu.VMEM((ROWS, NBLOCKS * LANES), jnp.float32),
            dma((len(PARTS),)),
            dma,
            dma,
            dma,
            dma,
            dma((NGROUPS,)),
            dma,
            dma((STEPS,)),
            dma((STEPS,)),
            dma((STEPS,)),
            dma((STEPS,)),
            pltpu.SemaphoreType.REGULAR,
            pltpu.SemaphoreType.REGULAR((3,)),
        ],
        compiler_params=pltpu.CompilerParams(
            collective_id=0, has_side_effects=True, vmem_limit_bytes=60 * 1024 * 1024
        ),
        name="difference",
    )(owners, *operands)


def solution(mesh):
    return jax.shard_map(
        shards,
        mesh=mesh,
        in_specs=(
            P("visit", None, "patch", None),
            P(),
            P(None, "visit", "patch", None),
            P(None, "visit", "patch", None),
            P(None, "visit", "patch", None),
        ),
        out_specs=P(None, "visit", "patch", None),
        check_vma=False,
    )
```

```python
import functools

import jax
import jax.numpy as jnp
import ml_dtypes
import numpy as np
from jax import lax
from jax.experimental import pallas as pl
from jax.experimental.pallas import tpu as pltpu
from jax.sharding import PartitionSpec as P

NPROF = 5
RAD = 10
STEPS = 2
RIDGE = 1.0

GROUP = 8
NGROUPS = 4
DEPTHS = 16
NPATCH = 16
SLOT = 7
FIXED = 31
ROWS = 16
LANES = 128
NBLOCKS = 8
SCI = 5
MESH = pl.DeviceIdType.MESH

PARTS = (
    (0, 1, 6, 7, 0),
    (1, 1, 13, 3, 0),
    (1, 0, 0, 3, 3),
    (2, 0, 3, 7, 0),
    (3, 0, 10, 6, 0),
    (4, -1, 0, 7, 0),
    (5, -1, 7, 3, 0),
    (5, 0, 16, 3, 4),
    (6, 0, 19, 7, 0),
    (7, 0, 26, 6, 0),
)
SPREAD = (
    (2, 1, 0, 4),
    (-2, 1, 4, 3),
    (2, 0, 0, 4),
    (-2, 0, 4, 3),
    (1, 1, 0, 7),
    (-1, 1, 0, 7),
    (1, 0, 0, 7),
    (-1, 0, 0, 7),
    (0, 1, 0, 7),
)
VAR_AT = 39
POSITIONS = 40


def image_positions():
    return list(range(0, 13)) + list(range(14, 27)) + list(range(28, 38))


def profile_table():
    offsets = np.arange(-RAD, RAD + 1) * 1.0
    recipe = [(1.0, 0), (1.5, 1), (2.0, 2), (3.0, 0), (4.0, 1)]
    profiles = []
    for spread, degree in recipe[:NPROF]:
        profile = offsets**degree * np.exp(-offsets * offsets / (2.0 * spread * spread))
        for earlier in profiles:
            profile = profile - np.dot(earlier, profile) * earlier
        profile = profile / np.sqrt(np.dot(profile, profile))
        profiles.append(profile)
    return np.stack(profiles)


def column_table():
    prof = profile_table().astype(np.float32)
    table = np.zeros((2 * LANES, NPROF * LANES), np.float32)
    for k in range(NPROF):
        for n in range(LANES):
            first = n + LANES // 2 - RAD
            table[first : first + 2 * RAD + 1, k * LANES + n] = prof[k]
    high, mid, _ = split3(table)
    return np.concatenate([high, mid], axis=1).astype(ml_dtypes.bfloat16)


def split3(x):
    high = x.astype(ml_dtypes.bfloat16).astype(np.float32)
    mid = (x - high).astype(ml_dtypes.bfloat16).astype(np.float32)
    low = (x - high - mid).astype(ml_dtypes.bfloat16).astype(np.float32)
    return high, mid, low


def row_table():
    prof = profile_table().astype(np.float32)
    places = image_positions()
    table = np.zeros((ROWS * 8, POSITIONS), np.float32)
    for h in range(ROWS):
        for l in range(NPROF):
            for a in range(2 * RAD + 1):
                table[h * 8 + l, places[h + a]] = prof[l, a]
    high, mid, _ = split3(table)
    blank = np.zeros((ROWS * 8, 8), np.float32)
    return np.concatenate([high, high, mid, blank], axis=1).astype(ml_dtypes.bfloat16)


def rounded(x):
    return x.astype(jnp.bfloat16).astype(jnp.float32)


def normal_part(slot, step, ag, ag_flat, cols, basis, col_ref, row_ref, sci_ref, svar_ref, bad_ref):
    x = ag[slot, 0:POSITIONS]
    y = pltpu.roll(x, LANES // 2, 2)
    lane = lax.broadcasted_iota(jnp.int32, y.shape, 2)
    block = lax.broadcasted_iota(jnp.int32, y.shape, 1)
    before = jnp.where(block == 0, 0.0, pltpu.roll(y, 1, 1))
    after = jnp.where(block == NBLOCKS - 1, 0.0, pltpu.roll(y, NBLOCKS - 1, 1))
    low = lane < LANES // 2
    left = jnp.where(low, before, y).reshape(POSITIONS * NBLOCKS, LANES)
    right = jnp.where(low, y, after).reshape(POSITIONS * NBLOCKS, LANES)
    window = jnp.concatenate([left, right], axis=1)
    height = POSITIONS * NBLOCKS
    high = rounded(window)
    both = jnp.concatenate([high, window - high], axis=0).astype(jnp.bfloat16)
    for k in range(NPROF):
        table = col_ref[:, k * LANES : (k + 1) * LANES]
        rest = col_ref[:, (NPROF + k) * LANES : (NPROF + k + 1) * LANES]
        main = jnp.dot(both, table, preferred_element_type=jnp.float32)
        more = jnp.dot(both[0:height], rest, preferred_element_type=jnp.float32)
        cols[k * height : (k + 1) * height, :] = main[0:height] + (main[height:] + more)

    def one_block(b, total):
        at = pl.multiple_of(b * LANES, LANES)
        c = jnp.concatenate(
            [
                cols[pl.ds(k * height + b, POSITIONS, stride=NBLOCKS), :]
                for k in range(NPROF)
            ],
            axis=1,
        )
        high = rounded(c)
        blank = jnp.zeros((8, NPROF * LANES), jnp.float32)
        stacked = jnp.concatenate([high, c - high, high, blank], axis=0).astype(jnp.bfloat16)
        d = jnp.dot(row_ref[...], stacked, preferred_element_type=jnp.float32)
        science = sci_ref[step, 0, :, pl.ds(at, LANES)]
        usable = (1 - bad_ref[step, 0, :, pl.ds(at, LANES)]).astype(jnp.float32)
        tile_var = ag_flat[pl.ds((slot * 56 + VAR_AT) * NBLOCKS + b, ROWS, stride=NBLOCKS), :]
        scale = usable / jnp.sqrt(svar_ref[step, 0, :, pl.ds(at, LANES)] + tile_var)
        spread = jnp.broadcast_to(scale[:, None, :], (ROWS, 8, LANES)).reshape(ROWS * 8, LANES)
        sci_spread = jnp.broadcast_to(science[:, None, :], (ROWS, 8, LANES)).reshape(ROWS * 8, LANES)
        place = lax.broadcasted_iota(jnp.int32, (ROWS * 8, LANES), 0) & 7
        parts = [d[:, k * LANES : (k + 1) * LANES] for k in range(NPROF)]
        parts[0] = jnp.where(place == SCI, sci_spread, parts[0])
        parts = [part * spread for part in parts]
        for k in range(NPROF):
            basis[slot, b, :, k * LANES : (k + 1) * LANES] = parts[k]

        def arranged(pieces):
            return jnp.concatenate(
                [
                    jnp.concatenate([piece[h * 8 : h * 8 + 8] for piece in pieces], axis=0)
                    for h in range(ROWS)
                ],
                axis=1,
            ).astype(jnp.bfloat16)

        highs = [rounded(part) for part in parts]
        rests = [part - h for part, h in zip(parts, highs)]
        return total + lax.dot_general(
            arranged(highs + rests),
            arranged(highs),
            (((1,), (1,)), ((), ())),
            preferred_element_type=jnp.float32,
        )

    total = lax.fori_loop(0, NBLOCKS, one_block, jnp.zeros((80, 40), jnp.float32), unroll=4)
    return total[0:40] + (total[40:80] + total[40:80].T)


def packed(mat):
    wide = jnp.concatenate([mat, jnp.zeros((40, LANES - 40), jnp.float32)], axis=1)
    first = wide[0:8] + pltpu.roll(wide[8:16], 40, 1) + pltpu.roll(wide[16:24], 80, 1)
    return jnp.concatenate([first, wide[24:32] + pltpu.roll(wide[32:40], 40, 1)], axis=0)


def unpacked(tiles):
    first, second = tiles[0:8], tiles[8:16]
    return jnp.concatenate(
        [
            first,
            pltpu.roll(first, LANES - 40, 1),
            pltpu.roll(first, LANES - 80, 1),
            second,
            pltpu.roll(second, LANES - 40, 1),
        ],
        axis=0,
    )


def solve(mats):
    row = lax.broadcasted_iota(jnp.int32, (40, LANES), 0)
    col = lax.broadcasted_iota(jnp.int32, (40, LANES), 1)
    mats = [m + jnp.where(row == col, RIDGE, 0.0) for m in mats]
    for k in range(NPROF):
        pivots = [k * 8 + l for l in range(NPROF)]
        for s, m in enumerate(mats):
            columns = [jnp.broadcast_to(m[:, p : p + 1], (40, LANES)) for p in pivots]
            for i, p in enumerate(pivots):
                ours = columns[i]
                inverse = 1.0 / ours[p : p + 1]
                pivot = m[p : p + 1] * inverse
                m = jnp.where(row == p, pivot, m - ours * pivot)
                for j in range(i + 1, NPROF):
                    other = columns[j][p : p + 1] * inverse
                    columns[j] = jnp.where(row == p, other, columns[j] - ours * other)
            mats[s] = m
    return [
        jnp.where(row == SCI, -1.0, jnp.broadcast_to(m[:, SCI : SCI + 1], (40, LANES)))
        for m in mats
    ]


def kernel(
    owners, temp_hbm, sci_hbm, svar_hbm, bad_hbm, col_hbm, row_hbm, out_ref,
    temp_ref, sci_ref, svar_ref, bad_ref, col_ref, row_ref, load_sem,
    mine, recv1, send2, recv2, ag, red, cols, basis, fitted,
    ssem1, same_sem, cross_sem, ssem2, rsem2, static_send, static_recv, ssem3, rsem3, ssem4, rsem4, passed, known,
):
    v = lax.axis_index("visit")
    p = lax.axis_index("patch")
    group = v // GROUP
    cls = v % GROUP
    depth = v // 2
    side = v % 2
    deep = cls // 2

    def near(dz, dx):
        return ((depth + dz + DEPTHS) % DEPTHS) * 2 + (side + dx) % 2

    def holder(t):
        return ((depth + (t // 2 - deep + 5) % 4 - 1 + DEPTHS) % DEPTHS) * 2 + t % 2

    loads = [
        pltpu.make_async_copy(src, dst, load_sem.at[i])
        for i, (src, dst) in enumerate(
            (
                (temp_hbm, temp_ref),
                (col_hbm, col_ref),
                (row_hbm, row_ref),
                (svar_hbm, svar_ref),
                (bad_hbm, bad_ref),
                (sci_hbm, sci_ref),
            )
        )
    ]
    for load in loads:
        load.start()

    recv1[...] = jnp.zeros_like(recv1)

    barrier = pltpu.get_barrier_semaphore()

    def greet(vv, pp):
        pl.semaphore_signal(barrier, inc=1, device_id=(vv, pp), device_id_type=MESH)

    for dz in range(-2, 3):
        for dx in range(2):
            if (dz, dx) != (0, 0):
                greet(near(dz, dx), p)
    for d in (1, 3):
        greet(((group + d) % NGROUPS) * GROUP + cls, p)
    for d in (1, NPATCH - 1):
        greet(v, (p + d) % NPATCH)

    @pl.when((cls < 2) & (p > 0))
    def _():
        for dz in range(-2, 2):
            for dx in range(2):
                if (dz, dx) != (0, 0):
                    greet(near(dz, dx), p - 1)

    @pl.when(((cls == 4) | (cls == 5)) & (p < NPATCH - 1))
    def _():
        for dz in range(-2, 2):
            for dx in range(2):
                if (dz, dx) != (0, 0):
                    greet(near(dz, dx), p + 1)

    below = jnp.where(p < NPATCH - 1, jnp.where(cls < 2, 1, 2), 0)
    above = jnp.where(p > 0, jnp.where((cls == 4) | (cls == 5), 1, 2), 0)
    loads[0].wait()
    flat = mine.reshape(2 * ROWS * NBLOCKS, LANES)
    for kind in range(2):
        for half in range(2):
            for b in range(NBLOCKS):
                flat[pl.ds((kind * ROWS + half * 8) * NBLOCKS + b, 8, stride=NBLOCKS), :] = temp_ref[
                    0, kind, half * 8 : half * 8 + 8, b * LANES : (b + 1) * LANES
                ]

    pl.semaphore_wait(barrier, 9 + 2 + 2 + below + above)

    pl.semaphore_signal(
        passed,
        inc=1,
        device_id=(((group + 1) % NGROUPS) * GROUP + cls, p),
        device_id_type=MESH,
    )

    def first_copy(i):
        t, dp, at, n, to = PARTS[i]
        return pltpu.make_async_remote_copy(
            src_ref=mine.at[pl.ds(at, n)],
            dst_ref=recv1.at[pl.ds((((deep - t // 2 + 2) & 3) * 2 + side) * SLOT + to, n)],
            send_sem=ssem1.at[i],
            recv_sem=same_sem if dp == 0 else cross_sem,
            device_id=(holder(t), p + dp),
            device_id_type=MESH,
        )

    def sends(i):
        t, dp = PARTS[i][:2]
        if dp == 0:
            return cls != t
        return p < NPATCH - 1 if dp == 1 else p > 0

    for i in range(len(PARTS)):

        @pl.when(sends(i))
        def _(i=i):
            first_copy(i).start()

    def spread_word(r):
        for d in (1 << r, NPATCH - (1 << r)):
            pl.semaphore_signal(
                known.at[r], inc=1, device_id=(v, (p + d) % NPATCH), device_id_type=MESH
            )

    spread_word(0)

    for t, dp, at, n, to in PARTS:

        @pl.when(cls == t)
        def _(t=t, dp=dp, at=at, n=n, to=to):
            if dp == 0:
                recv1[pl.ds((4 + t % 2) * SLOT + to, n)] = mine[pl.ds(at, n)]

    for t, dp, at, n, to in PARTS:
        if dp == 0:

            @pl.when(cls == t)
            def _(n=n):
                rows = recv1.at[pl.ds(0, (GROUP - 1) * n)]
                pltpu.make_async_copy(rows, rows, same_sem).wait()

        else:

            @pl.when((cls == t) & (p > 0 if dp == 1 else p < NPATCH - 1))
            def _(n=n):
                rows = recv1.at[pl.ds(0, GROUP * n)]
                pltpu.make_async_copy(rows, rows, cross_sem).wait()

    own = pl.ds(cls * SLOT, SLOT)
    fixed = pl.ds((((FIXED // 2 + 2 - deep) & 3) * 2 + FIXED % 2) * SLOT, SLOT)
    fixed_group = ((FIXED // 2 + 2 - deep) & (DEPTHS - 1)) >> 2
    from_fixed = group == fixed_group

    def static_copy(g):
        return pltpu.make_async_remote_copy(
            src_ref=recv1.at[fixed],
            dst_ref=ag.at[0, own],
            send_sem=static_send.at[g],
            recv_sem=static_recv,
            device_id=(((group + g) % NGROUPS) * GROUP + cls, p),
            device_id_type=MESH,
        )

    pl.semaphore_wait(passed, 1)

    @pl.when(from_fixed)
    def _():
        for d in (2, 1, 3):
            static_copy(d).start()
        ag[0, own] = recv1[fixed]

    other = owners[0] + owners[1] - FIXED
    far = (other >> 1) + 2 - deep
    chosen = recv1[pl.ds(((far & 3) * 2 + (other & 1)) * SLOT, SLOT)]
    send2[...] = chosen
    recv2[pl.ds(group * SLOT, SLOT)] = chosen

    def second_copy(d):
        return pltpu.make_async_remote_copy(
            src_ref=send2,
            dst_ref=recv2.at[pl.ds(group * SLOT, SLOT)],
            send_sem=ssem2,
            recv_sem=rsem2,
            device_id=(((group + d) % NGROUPS) * GROUP + cls, p),
            device_id_type=MESH,
        )

    for d in (2, 1, 3):
        second_copy(d).start()
    pl.semaphore_wait(known.at[0], 2)
    spread_word(1)

    def third_copy(slot, d):
        dz, dx, at, n = SPREAD[d]
        rows = pl.ds(cls * SLOT + at, n)
        return pltpu.make_async_remote_copy(
            src_ref=ag.at[slot, rows],
            dst_ref=ag.at[slot, rows],
            send_sem=ssem3.at[slot],
            recv_sem=rsem3.at[slot],
            device_id=(near(dz, dx), p),
            device_id_type=MESH,
        )

    @pl.when(group != fixed_group)
    def _():
        pltpu.make_async_copy(ag.at[0, own], ag.at[0, own], static_recv).wait()

    for d in range(len(SPREAD)):
        third_copy(0, d).start()
    three = recv2.at[pl.ds(0, (NGROUPS - 1) * SLOT)]
    pltpu.make_async_copy(three, three, rsem2).wait()
    ag[1, own] = recv2[pl.ds(((far >> 2) & 3) * SLOT, SLOT)]
    for d in range(len(SPREAD)):
        third_copy(1, d).start()
    pl.semaphore_wait(known.at[1], 2)
    spread_word(2)

    ag_flat = ag.reshape(STEPS * 56 * NBLOCKS, LANES)
    fixed_step = jnp.where(owners[1] == FIXED, 1, 0)
    for load in loads[1:]:
        load.wait()

    def fourth_copy(slot, d):
        return pltpu.make_async_remote_copy(
            src_ref=red.at[slot, p],
            dst_ref=red.at[slot, p],
            send_sem=ssem4.at[slot],
            recv_sem=rsem4.at[slot],
            device_id=(v, (p + d) % NPATCH),
            device_id_type=MESH,
        )

    for slot in range(STEPS):
        rows = ag.at[slot, pl.ds(0, (GROUP - 1) * SLOT)]
        pltpu.make_async_copy(rows, rows, rsem3.at[slot]).wait()
        step = fixed_step if slot == 0 else 1 - fixed_step
        red[slot, p] = packed(
            normal_part(slot, step, ag, ag_flat, cols, basis, col_ref, row_ref, sci_ref, svar_ref, bad_ref)
        )
        if slot == 0:
            pl.semaphore_wait(known.at[2], 2)
        for d in (12, 4, 13, 11, 5, 3, 10, 6, 14, 8, 9, 7, 2, 15, 1):
            fourth_copy(slot, d).start()

    for i in range(len(PARTS)):

        @pl.when(sends(i))
        def _(i=i):
            first_copy(i).wait_send()

    @pl.when(from_fixed)
    def _():
        for d in range(1, NGROUPS):
            static_copy(d).wait_send()

    pltpu.make_async_copy(three, three, ssem2).wait()
    for slot in range(STEPS):
        rows = ag.at[slot, pl.ds(0, (GROUP - 1) * SLOT)]
        pltpu.make_async_copy(rows, rows, ssem3.at[slot]).wait()

    def coefs(slot):
        rows = red.at[slot, pl.ds(0, NPATCH - 1)]
        pltpu.make_async_copy(rows, rows, rsem4.at[slot]).wait()
        total = red[slot, 0]
        for q in range(1, NPATCH):
            total = total + red[slot, q]
        return solve([unpacked(total)])[0]

    def fit(slot, coef, b):
        sums = jnp.zeros((ROWS, 8, LANES), jnp.float32)
        for k in range(NPROF):
            d = basis[slot, b, :, k * LANES : (k + 1) * LANES].reshape(ROWS, 8, LANES)
            sums = sums + d * coef[k * 8 : k * 8 + 8][None]
        return -jnp.sum(sums, axis=1)

    coef0 = coefs(0)

    def fixed_block(b, carry):
        fitted[:, pl.ds(pl.multiple_of(b * LANES, LANES), LANES)] = fit(0, coef0, b)
        return carry

    lax.fori_loop(0, NBLOCKS, fixed_block, 0, unroll=4)
    coef1 = coefs(1)

    def other_block(b, carry):
        at = pl.multiple_of(b * LANES, LANES)
        ours, theirs = fitted[:, pl.ds(at, LANES)], fit(1, coef1, b)
        for step in range(STEPS):
            out_ref[step, 0, :, pl.ds(at, LANES)] = jnp.where(fixed_step == step, ours, theirs)
        return carry

    lax.fori_loop(0, NBLOCKS, other_block, 0, unroll=4)
    for slot in range(STEPS):
        rows = red.at[slot, pl.ds(0, NPATCH - 1)]
        pltpu.make_async_copy(rows, rows, ssem4.at[slot]).wait()


def shards(templates, owners, science, sci_var, bad_pixels):
    hbm = pl.BlockSpec(memory_space=pltpu.HBM)
    row_shape = (NBLOCKS, LANES)
    dma = pltpu.SemaphoreType.DMA
    col_table, rows_table = jnp.asarray(column_table()), jnp.asarray(row_table())
    operands = (templates, science, sci_var, bad_pixels, col_table, rows_table)
    return pl.pallas_call(
        kernel,
        out_shape=jax.ShapeDtypeStruct(science.shape, jnp.float32),
        in_specs=[pl.BlockSpec(memory_space=pltpu.SMEM)] + [hbm] * len(operands),
        out_specs=pl.BlockSpec(memory_space=pltpu.VMEM),
        scratch_shapes=[pltpu.VMEM(x.shape, x.dtype) for x in operands]
        + [
            dma((len(operands),)),
            pltpu.VMEM((2 * ROWS, *row_shape), jnp.float32),
            pltpu.VMEM((GROUP * SLOT, *row_shape), jnp.float32),
            pltpu.VMEM((SLOT, *row_shape), jnp.float32),
            pltpu.VMEM((NGROUPS * SLOT, *row_shape), jnp.float32),
            pltpu.VMEM((STEPS, GROUP * SLOT, *row_shape), jnp.float32),
            pltpu.VMEM((STEPS, NPATCH, 16, LANES), jnp.float32),
            pltpu.VMEM((NPROF * POSITIONS * NBLOCKS, LANES), jnp.float32),
            pltpu.VMEM((STEPS, NBLOCKS, ROWS * 8, NPROF * LANES), jnp.float32),
            pltpu.VMEM((ROWS, NBLOCKS * LANES), jnp.float32),
            dma((len(PARTS),)),
            dma,
            dma,
            dma,
            dma,
            dma((NGROUPS,)),
            dma,
            dma((STEPS,)),
            dma((STEPS,)),
            dma((STEPS,)),
            dma((STEPS,)),
            pltpu.SemaphoreType.REGULAR,
            pltpu.SemaphoreType.REGULAR((3,)),
        ],
        compiler_params=pltpu.CompilerParams(
            collective_id=0, has_side_effects=True, vmem_limit_bytes=60 * 1024 * 1024
        ),
        name="difference",
    )(owners, *operands)


def solution(mesh):
    return jax.shard_map(
        shards,
        mesh=mesh,
        in_specs=(
            P("visit", None, "patch", None),
            P(),
            P(None, "visit", "patch", None),
            P(None, "visit", "patch", None),
            P(None, "visit", "patch", None),
        ),
        out_specs=P(None, "visit", "patch", None),
        check_vma=False,
    )
```

```python
import functools

import jax
import jax.numpy as jnp
import ml_dtypes
import numpy as np
from jax import lax
from jax.experimental import pallas as pl
from jax.experimental.pallas import tpu as pltpu
from jax.sharding import PartitionSpec as P

NPROF = 5
RAD = 10
STEPS = 2
RIDGE = 1.0

GROUP = 8
NGROUPS = 4
DEPTHS = 16
NPATCH = 16
SLOT = 7
FIXED = 31
ROWS = 16
LANES = 128
NBLOCKS = 8
SCI = 5
MESH = pl.DeviceIdType.MESH

PARTS = (
    (0, 1, 6, 7, 0),
    (1, 1, 13, 3, 0),
    (1, 0, 0, 3, 3),
    (2, 0, 3, 7, 0),
    (3, 0, 10, 6, 0),
    (4, -1, 0, 7, 0),
    (5, -1, 7, 3, 0),
    (5, 0, 16, 3, 4),
    (6, 0, 19, 7, 0),
    (7, 0, 26, 6, 0),
)
SPREAD = (
    (2, 1, 0, 4),
    (-2, 1, 4, 3),
    (2, 0, 0, 4),
    (-2, 0, 4, 3),
    (1, 1, 0, 7),
    (-1, 1, 0, 7),
    (1, 0, 0, 7),
    (-1, 0, 0, 7),
    (0, 1, 0, 7),
)
VAR_AT = 39
POSITIONS = 40


def image_positions():
    return list(range(0, 13)) + list(range(14, 27)) + list(range(28, 38))


def profile_table():
    offsets = np.arange(-RAD, RAD + 1) * 1.0
    recipe = [(1.0, 0), (1.5, 1), (2.0, 2), (3.0, 0), (4.0, 1)]
    profiles = []
    for spread, degree in recipe[:NPROF]:
        profile = offsets**degree * np.exp(-offsets * offsets / (2.0 * spread * spread))
        for earlier in profiles:
            profile = profile - np.dot(earlier, profile) * earlier
        profile = profile / np.sqrt(np.dot(profile, profile))
        profiles.append(profile)
    return np.stack(profiles)


def column_table():
    prof = profile_table().astype(np.float32)
    table = np.zeros((2 * LANES, NPROF * LANES), np.float32)
    for k in range(NPROF):
        for n in range(LANES):
            first = n + LANES // 2 - RAD
            table[first : first + 2 * RAD + 1, k * LANES + n] = prof[k]
    high, mid, _ = split3(table)
    return np.concatenate([high, mid], axis=1).astype(ml_dtypes.bfloat16)


def split3(x):
    high = x.astype(ml_dtypes.bfloat16).astype(np.float32)
    mid = (x - high).astype(ml_dtypes.bfloat16).astype(np.float32)
    low = (x - high - mid).astype(ml_dtypes.bfloat16).astype(np.float32)
    return high, mid, low


def row_table():
    prof = profile_table().astype(np.float32)
    places = image_positions()
    table = np.zeros((ROWS * 8, POSITIONS), np.float32)
    for h in range(ROWS):
        for l in range(NPROF):
            for a in range(2 * RAD + 1):
                table[h * 8 + l, places[h + a]] = prof[l, a]
    high, mid, _ = split3(table)
    blank = np.zeros((ROWS * 8, 8), np.float32)
    return np.concatenate([high, high, mid, blank], axis=1).astype(ml_dtypes.bfloat16)


def rounded(x):
    return x.astype(jnp.bfloat16).astype(jnp.float32)


def normal_part(slot, step, ag, ag_flat, cols, basis, col_ref, row_ref, sci_ref, svar_ref, bad_ref):
    x = ag[slot, 0:POSITIONS]
    y = pltpu.roll(x, LANES // 2, 2)
    lane = lax.broadcasted_iota(jnp.int32, y.shape, 2)
    block = lax.broadcasted_iota(jnp.int32, y.shape, 1)
    before = jnp.where(block == 0, 0.0, pltpu.roll(y, 1, 1))
    after = jnp.where(block == NBLOCKS - 1, 0.0, pltpu.roll(y, NBLOCKS - 1, 1))
    low = lane < LANES // 2
    left = jnp.where(low, before, y).reshape(POSITIONS * NBLOCKS, LANES)
    right = jnp.where(low, y, after).reshape(POSITIONS * NBLOCKS, LANES)
    window = jnp.concatenate([left, right], axis=1)
    height = POSITIONS * NBLOCKS
    high = rounded(window)
    both = jnp.concatenate([high, window - high], axis=0).astype(jnp.bfloat16)
    for k in range(NPROF):
        table = col_ref[:, k * LANES : (k + 1) * LANES]
        rest = col_ref[:, (NPROF + k) * LANES : (NPROF + k + 1) * LANES]
        main = jnp.dot(both, table, preferred_element_type=jnp.float32)
        more = jnp.dot(both[0:height], rest, preferred_element_type=jnp.float32)
        cols[k * height : (k + 1) * height, :] = main[0:height] + (main[height:] + more)

    def one_block(b, total):
        at = pl.multiple_of(b * LANES, LANES)
        c = jnp.concatenate(
            [
                cols[pl.ds(k * height + b, POSITIONS, stride=NBLOCKS), :]
                for k in range(NPROF)
            ],
            axis=1,
        )
        high = rounded(c)
        blank = jnp.zeros((8, NPROF * LANES), jnp.float32)
        stacked = jnp.concatenate([high, c - high, high, blank], axis=0).astype(jnp.bfloat16)
        d = jnp.dot(row_ref[...], stacked, preferred_element_type=jnp.float32)
        science = sci_ref[step, 0, :, pl.ds(at, LANES)]
        usable = (1 - bad_ref[step, 0, :, pl.ds(at, LANES)]).astype(jnp.float32)
        tile_var = ag_flat[pl.ds((slot * 56 + VAR_AT) * NBLOCKS + b, ROWS, stride=NBLOCKS), :]
        scale = usable / jnp.sqrt(svar_ref[step, 0, :, pl.ds(at, LANES)] + tile_var)
        spread = jnp.broadcast_to(scale[:, None, :], (ROWS, 8, LANES)).reshape(ROWS * 8, LANES)
        sci_spread = jnp.broadcast_to(science[:, None, :], (ROWS, 8, LANES)).reshape(ROWS * 8, LANES)
        place = lax.broadcasted_iota(jnp.int32, (ROWS * 8, LANES), 0) & 7
        parts = [d[:, k * LANES : (k + 1) * LANES] for k in range(NPROF)]
        parts[0] = jnp.where(place == SCI, sci_spread, parts[0])
        parts = [part * spread for part in parts]
        for k in range(NPROF):
            basis[slot, b, :, k * LANES : (k + 1) * LANES] = parts[k]

        def arranged(pieces):
            return jnp.concatenate(
                [
                    jnp.concatenate([piece[h * 8 : h * 8 + 8] for piece in pieces], axis=0)
                    for h in range(ROWS)
                ],
                axis=1,
            ).astype(jnp.bfloat16)

        highs = [rounded(part) for part in parts]
        rests = [part - h for part, h in zip(parts, highs)]
        return total + lax.dot_general(
            arranged(highs + rests),
            arranged(highs),
            (((1,), (1,)), ((), ())),
            preferred_element_type=jnp.float32,
        )

    total = lax.fori_loop(0, NBLOCKS, one_block, jnp.zeros((80, 40), jnp.float32), unroll=4)
    return total[0:40] + (total[40:80] + total[40:80].T)


def packed(mat):
    wide = jnp.concatenate([mat, jnp.zeros((40, LANES - 40), jnp.float32)], axis=1)
    first = wide[0:8] + pltpu.roll(wide[8:16], 40, 1) + pltpu.roll(wide[16:24], 80, 1)
    return jnp.concatenate([first, wide[24:32] + pltpu.roll(wide[32:40], 40, 1)], axis=0)


def unpacked(tiles):
    first, second = tiles[0:8], tiles[8:16]
    return jnp.concatenate(
        [
            first,
            pltpu.roll(first, LANES - 40, 1),
            pltpu.roll(first, LANES - 80, 1),
            second,
            pltpu.roll(second, LANES - 40, 1),
        ],
        axis=0,
    )


def solve(mats):
    row = lax.broadcasted_iota(jnp.int32, (40, LANES), 0)
    col = lax.broadcasted_iota(jnp.int32, (40, LANES), 1)
    mats = [m + jnp.where(row == col, RIDGE, 0.0) for m in mats]
    for k in range(NPROF):
        pivots = [k * 8 + l for l in range(NPROF)]
        for s, m in enumerate(mats):
            columns = [jnp.broadcast_to(m[:, p : p + 1], (40, LANES)) for p in pivots]
            for i, p in enumerate(pivots):
                ours = columns[i]
                inverse = 1.0 / ours[p : p + 1]
                pivot = m[p : p + 1] * inverse
                m = jnp.where(row == p, pivot, m - ours * pivot)
                for j in range(i + 1, NPROF):
                    other = columns[j][p : p + 1] * inverse
                    columns[j] = jnp.where(row == p, other, columns[j] - ours * other)
            mats[s] = m
    return [
        jnp.where(row == SCI, -1.0, jnp.broadcast_to(m[:, SCI : SCI + 1], (40, LANES)))
        for m in mats
    ]


def kernel(
    owners, temp_hbm, sci_hbm, svar_hbm, bad_hbm, col_hbm, row_hbm, out_ref,
    temp_ref, sci_ref, svar_ref, bad_ref, col_ref, row_ref, load_sem,
    mine, recv1, recv2, ag, red, cols, basis, fitted,
    ssem1, same_sem, cross_sem, ssem2, rsem2, static_send, static_recv, ssem3, rsem3, ssem4, rsem4, passed, known,
):
    v = lax.axis_index("visit")
    p = lax.axis_index("patch")
    group = v // GROUP
    cls = v % GROUP
    depth = v // 2
    side = v % 2
    deep = cls // 2

    def near(dz, dx):
        return ((depth + dz + DEPTHS) % DEPTHS) * 2 + (side + dx) % 2

    def holder(t):
        return ((depth + (t // 2 - deep + 5) % 4 - 1 + DEPTHS) % DEPTHS) * 2 + t % 2

    loads = [
        pltpu.make_async_copy(src, dst, load_sem.at[i])
        for i, (src, dst) in enumerate(
            (
                (temp_hbm, temp_ref),
                (col_hbm, col_ref),
                (row_hbm, row_ref),
                (svar_hbm, svar_ref),
                (bad_hbm, bad_ref),
                (sci_hbm, sci_ref),
            )
        )
    ]
    for load in loads:
        load.start()

    recv1[...] = jnp.zeros_like(recv1)

    barrier = pltpu.get_barrier_semaphore()

    def greet(vv, pp):
        pl.semaphore_signal(barrier, inc=1, device_id=(vv, pp), device_id_type=MESH)

    for dz in range(-2, 3):
        for dx in range(2):
            if (dz, dx) != (0, 0):
                greet(near(dz, dx), p)

    @pl.when((cls < 2) & (p > 0))
    def _():
        for dz in range(-2, 2):
            for dx in range(2):
                if (dz, dx) != (0, 0):
                    greet(near(dz, dx), p - 1)

    @pl.when(((cls == 4) | (cls == 5)) & (p < NPATCH - 1))
    def _():
        for dz in range(-2, 2):
            for dx in range(2):
                if (dz, dx) != (0, 0):
                    greet(near(dz, dx), p + 1)

    for d in (1, 3):
        greet(((group + d) % NGROUPS) * GROUP + cls, p)
    for d in (1, NPATCH - 1):
        greet(v, (p + d) % NPATCH)
    below = jnp.where(p < NPATCH - 1, jnp.where(cls < 2, 1, 2), 0)
    above = jnp.where(p > 0, jnp.where((cls == 4) | (cls == 5), 1, 2), 0)
    loads[0].wait()
    flat = mine.reshape((2 * ROWS + 1) * NBLOCKS, LANES)
    for kind in range(2):
        for half in range(2):
            for b in range(NBLOCKS):
                flat[pl.ds((kind * ROWS + half * 8) * NBLOCKS + b, 8, stride=NBLOCKS), :] = temp_ref[
                    0, kind, half * 8 : half * 8 + 8, b * LANES : (b + 1) * LANES
                ]

    pl.semaphore_wait(barrier, 9 + 2 + 2 + below + above)

    pl.semaphore_signal(
        passed,
        inc=1,
        device_id=(((group + 1) % NGROUPS) * GROUP + cls, p),
        device_id_type=MESH,
    )

    def first_copy(i):
        t, dp, at, n, to = PARTS[i]
        return pltpu.make_async_remote_copy(
            src_ref=mine.at[pl.ds(at, n)],
            dst_ref=recv1.at[pl.ds((((deep - t // 2 + 2) & 3) * 2 + side) * SLOT + to, n)],
            send_sem=ssem1.at[i],
            recv_sem=same_sem if dp == 0 else cross_sem,
            device_id=(holder(t), p + dp),
            device_id_type=MESH,
        )

    def sends(i):
        t, dp = PARTS[i][:2]
        if dp == 0:
            return cls != t
        return p < NPATCH - 1 if dp == 1 else p > 0

    for i in range(len(PARTS)):

        @pl.when(sends(i))
        def _(i=i):
            first_copy(i).start()

    def spread_word(r):
        for d in (1 << r, NPATCH - (1 << r)):
            pl.semaphore_signal(
                known.at[r], inc=1, device_id=(v, (p + d) % NPATCH), device_id_type=MESH
            )

    spread_word(0)

    for t, dp, at, n, to in PARTS:

        @pl.when(cls == t)
        def _(t=t, dp=dp, at=at, n=n, to=to):
            if dp == 0:
                recv1[pl.ds((4 + t % 2) * SLOT + to, n)] = mine[pl.ds(at, n)]

    for t, dp, at, n, to in PARTS:
        if dp == 0:

            @pl.when(cls == t)
            def _(n=n):
                rows = recv1.at[pl.ds(0, (GROUP - 1) * n)]
                pltpu.make_async_copy(rows, rows, same_sem).wait()

        else:

            @pl.when((cls == t) & (p > 0 if dp == 1 else p < NPATCH - 1))
            def _(n=n):
                rows = recv1.at[pl.ds(0, GROUP * n)]
                pltpu.make_async_copy(rows, rows, cross_sem).wait()

    own = pl.ds(cls * SLOT, SLOT)
    fixed = pl.ds((((FIXED // 2 + 2 - deep) & 3) * 2 + FIXED % 2) * SLOT, SLOT)
    fixed_group = ((FIXED // 2 + 2 - deep) & (DEPTHS - 1)) >> 2
    from_fixed = group == fixed_group

    def static_copy(g):
        return pltpu.make_async_remote_copy(
            src_ref=recv1.at[fixed],
            dst_ref=ag.at[0, own],
            send_sem=static_send.at[g],
            recv_sem=static_recv,
            device_id=(((group + g) % NGROUPS) * GROUP + cls, p),
            device_id_type=MESH,
        )

    pl.semaphore_wait(passed, 1)

    @pl.when(from_fixed)
    def _():
        for d in (2, 1, 3):
            static_copy(d).start()
        ag[0, own] = recv1[fixed]

    other = owners[0] + owners[1] - FIXED
    far = (other >> 1) + 2 - deep
    chosen = recv1[pl.ds(((far & 3) * 2 + (other & 1)) * SLOT, SLOT)]
    recv2[pl.ds(group * SLOT, SLOT)] = chosen

    def second_copy(d):
        return pltpu.make_async_remote_copy(
            src_ref=recv2.at[pl.ds(group * SLOT, SLOT)],
            dst_ref=recv2.at[pl.ds(group * SLOT, SLOT)],
            send_sem=ssem2,
            recv_sem=rsem2,
            device_id=(((group + d) % NGROUPS) * GROUP + cls, p),
            device_id_type=MESH,
        )

    for d in (2, 1, 3):
        second_copy(d).start()
    pl.semaphore_wait(known.at[0], 2)
    spread_word(1)

    def third_copy(slot, d):
        dz, dx, at, n = SPREAD[d]
        rows = pl.ds(cls * SLOT + at, n)
        return pltpu.make_async_remote_copy(
            src_ref=ag.at[slot, rows],
            dst_ref=ag.at[slot, rows],
            send_sem=ssem3.at[slot],
            recv_sem=rsem3.at[slot],
            device_id=(near(dz, dx), p),
            device_id_type=MESH,
        )

    @pl.when(group != fixed_group)
    def _():
        pltpu.make_async_copy(ag.at[0, own], ag.at[0, own], static_recv).wait()

    for d in range(len(SPREAD)):
        third_copy(0, d).start()
    three = recv2.at[pl.ds(0, (NGROUPS - 1) * SLOT)]
    pltpu.make_async_copy(three, three, rsem2).wait()
    ag[1, own] = recv2[pl.ds(((far >> 2) & 3) * SLOT, SLOT)]
    for d in range(len(SPREAD)):
        third_copy(1, d).start()
    pl.semaphore_wait(known.at[1], 2)
    spread_word(2)

    ag_flat = ag.reshape(STEPS * 56 * NBLOCKS, LANES)
    fixed_step = jnp.where(owners[1] == FIXED, 1, 0)
    for load in loads[1:]:
        load.wait()

    def fourth_copy(slot, d):
        return pltpu.make_async_remote_copy(
            src_ref=red.at[slot, p],
            dst_ref=red.at[slot, p],
            send_sem=ssem4.at[slot],
            recv_sem=rsem4.at[slot],
            device_id=(v, (p + d) % NPATCH),
            device_id_type=MESH,
        )

    for slot in range(STEPS):
        rows = ag.at[slot, pl.ds(0, (GROUP - 1) * SLOT)]
        pltpu.make_async_copy(rows, rows, rsem3.at[slot]).wait()
        step = fixed_step if slot == 0 else 1 - fixed_step
        red[slot, p] = packed(
            normal_part(slot, step, ag, ag_flat, cols, basis, col_ref, row_ref, sci_ref, svar_ref, bad_ref)
        )
        if slot == 0:
            pl.semaphore_wait(known.at[2], 2)
        for d in range(1, NPATCH):
            fourth_copy(slot, d).start()

    for i in range(len(PARTS)):

        @pl.when(sends(i))
        def _(i=i):
            first_copy(i).wait_send()

    @pl.when(from_fixed)
    def _():
        for d in range(1, NGROUPS):
            static_copy(d).wait_send()

    pltpu.make_async_copy(three, three, ssem2).wait()
    for slot in range(STEPS):
        rows = ag.at[slot, pl.ds(0, (GROUP - 1) * SLOT)]
        pltpu.make_async_copy(rows, rows, ssem3.at[slot]).wait()

    def coefs(slot):
        rows = red.at[slot, pl.ds(0, NPATCH - 1)]
        pltpu.make_async_copy(rows, rows, rsem4.at[slot]).wait()
        total = red[slot, 0]
        for q in range(1, NPATCH):
            total = total + red[slot, q]
        return solve([unpacked(total)])[0]

    def fit(slot, coef, b):
        sums = jnp.zeros((ROWS, 8, LANES), jnp.float32)
        for k in range(NPROF):
            d = basis[slot, b, :, k * LANES : (k + 1) * LANES].reshape(ROWS, 8, LANES)
            sums = sums + d * coef[k * 8 : k * 8 + 8][None]
        return -jnp.sum(sums, axis=1)

    coef0 = coefs(0)

    def fixed_block(b, carry):
        fitted[:, pl.ds(pl.multiple_of(b * LANES, LANES), LANES)] = fit(0, coef0, b)
        return carry

    lax.fori_loop(0, NBLOCKS, fixed_block, 0, unroll=4)
    coef1 = coefs(1)

    def other_block(b, carry):
        at = pl.multiple_of(b * LANES, LANES)
        ours, theirs = fitted[:, pl.ds(at, LANES)], fit(1, coef1, b)
        for step in range(STEPS):
            out_ref[step, 0, :, pl.ds(at, LANES)] = jnp.where(fixed_step == step, ours, theirs)
        return carry

    lax.fori_loop(0, NBLOCKS, other_block, 0, unroll=4)
    for slot in range(STEPS):
        rows = red.at[slot, pl.ds(0, NPATCH - 1)]
        pltpu.make_async_copy(rows, rows, ssem4.at[slot]).wait()


def shards(templates, owners, science, sci_var, bad_pixels):
    hbm = pl.BlockSpec(memory_space=pltpu.HBM)
    row_shape = (NBLOCKS, LANES)
    dma = pltpu.SemaphoreType.DMA
    col_table, rows_table = jnp.asarray(column_table()), jnp.asarray(row_table())
    operands = (templates, science, sci_var, bad_pixels, col_table, rows_table)
    return pl.pallas_call(
        kernel,
        out_shape=jax.ShapeDtypeStruct(science.shape, jnp.float32),
        in_specs=[pl.BlockSpec(memory_space=pltpu.SMEM)] + [hbm] * len(operands),
        out_specs=pl.BlockSpec(memory_space=pltpu.VMEM),
        scratch_shapes=[pltpu.VMEM(x.shape, x.dtype) for x in operands]
        + [
            dma((len(operands),)),
            pltpu.VMEM((2 * ROWS + 1, *row_shape), jnp.float32),
            pltpu.VMEM((GROUP * SLOT, *row_shape), jnp.float32),
            pltpu.VMEM((NGROUPS * SLOT, *row_shape), jnp.float32),
            pltpu.VMEM((STEPS, GROUP * SLOT, *row_shape), jnp.float32),
            pltpu.VMEM((STEPS, NPATCH, 16, LANES), jnp.float32),
            pltpu.VMEM((NPROF * POSITIONS * NBLOCKS + 8, LANES), jnp.float32),
            pltpu.VMEM((STEPS, NBLOCKS, ROWS * 8, NPROF * LANES), jnp.float32),
            pltpu.VMEM((ROWS, NBLOCKS * LANES), jnp.float32),
            dma((len(PARTS),)),
            dma,
            dma,
            dma,
            dma,
            dma((NGROUPS,)),
            dma,
            dma((STEPS,)),
            dma((STEPS,)),
            dma((STEPS,)),
            dma((STEPS,)),
            pltpu.SemaphoreType.REGULAR,
            pltpu.SemaphoreType.REGULAR((3,)),
        ],
        compiler_params=pltpu.CompilerParams(
            collective_id=0, has_side_effects=True, vmem_limit_bytes=60 * 1024 * 1024
        ),
        name="difference",
    )(owners, *operands)


def solution(mesh):
    return jax.shard_map(
        shards,
        mesh=mesh,
        in_specs=(
            P("visit", None, "patch", None),
            P(),
            P(None, "visit", "patch", None),
            P(None, "visit", "patch", None),
            P(None, "visit", "patch", None),
        ),
        out_specs=P(None, "visit", "patch", None),
        check_vma=False,
    )
```

```python
import functools

import jax
import jax.numpy as jnp
import ml_dtypes
import numpy as np
from jax import lax
from jax.experimental import pallas as pl
from jax.experimental.pallas import tpu as pltpu
from jax.sharding import PartitionSpec as P

NPROF = 5
RAD = 10
STEPS = 2
RIDGE = 1.0

GROUP = 8
NGROUPS = 4
DEPTHS = 16
NPATCH = 16
SLOT = 7
FIXED = 31
ROWS = 16
LANES = 128
NBLOCKS = 8
SCI = 5
MESH = pl.DeviceIdType.MESH

PARTS = (
    (0, 1, 6, 7, 0),
    (1, 1, 13, 3, 0),
    (1, 0, 0, 3, 3),
    (2, 0, 3, 7, 0),
    (3, 0, 10, 6, 0),
    (4, -1, 0, 7, 0),
    (5, -1, 7, 3, 0),
    (5, 0, 16, 3, 4),
    (6, 0, 19, 7, 0),
    (7, 0, 26, 6, 0),
)
SPREAD = (
    (2, 1, 0, 4),
    (-2, 1, 4, 3),
    (2, 0, 0, 4),
    (-2, 0, 4, 3),
    (1, 1, 0, 7),
    (-1, 1, 0, 7),
    (1, 0, 0, 7),
    (-1, 0, 0, 7),
    (0, 1, 0, 7),
)
VAR_AT = 39
POSITIONS = 40


def image_positions():
    return list(range(0, 13)) + list(range(14, 27)) + list(range(28, 38))


def profile_table():
    offsets = np.arange(-RAD, RAD + 1) * 1.0
    recipe = [(1.0, 0), (1.5, 1), (2.0, 2), (3.0, 0), (4.0, 1)]
    profiles = []
    for spread, degree in recipe[:NPROF]:
        profile = offsets**degree * np.exp(-offsets * offsets / (2.0 * spread * spread))
        for earlier in profiles:
            profile = profile - np.dot(earlier, profile) * earlier
        profile = profile / np.sqrt(np.dot(profile, profile))
        profiles.append(profile)
    return np.stack(profiles)


def column_table():
    prof = profile_table().astype(np.float32)
    table = np.zeros((2 * LANES, NPROF * LANES), np.float32)
    for k in range(NPROF):
        for n in range(LANES):
            first = n + LANES // 2 - RAD
            table[first : first + 2 * RAD + 1, k * LANES + n] = prof[k]
    high, mid, _ = split3(table)
    return np.concatenate([high, mid], axis=1).astype(ml_dtypes.bfloat16)


def split3(x):
    high = x.astype(ml_dtypes.bfloat16).astype(np.float32)
    mid = (x - high).astype(ml_dtypes.bfloat16).astype(np.float32)
    low = (x - high - mid).astype(ml_dtypes.bfloat16).astype(np.float32)
    return high, mid, low


def row_table():
    prof = profile_table().astype(np.float32)
    places = image_positions()
    table = np.zeros((ROWS * 8, POSITIONS), np.float32)
    for h in range(ROWS):
        for l in range(NPROF):
            for a in range(2 * RAD + 1):
                table[h * 8 + l, places[h + a]] = prof[l, a]
    high, mid, _ = split3(table)
    blank = np.zeros((ROWS * 8, 8), np.float32)
    return np.concatenate([high, high, mid, blank], axis=1).astype(ml_dtypes.bfloat16)


def rounded(x):
    return x.astype(jnp.bfloat16).astype(jnp.float32)


def normal_part(slot, step, ag, ag_flat, cols, basis, col_ref, row_ref, sci_ref, svar_ref, bad_ref):
    x = ag[slot, 0:POSITIONS]
    y = pltpu.roll(x, LANES // 2, 2)
    lane = lax.broadcasted_iota(jnp.int32, y.shape, 2)
    block = lax.broadcasted_iota(jnp.int32, y.shape, 1)
    before = jnp.where(block == 0, 0.0, pltpu.roll(y, 1, 1))
    after = jnp.where(block == NBLOCKS - 1, 0.0, pltpu.roll(y, NBLOCKS - 1, 1))
    low = lane < LANES // 2
    left = jnp.where(low, before, y).reshape(POSITIONS * NBLOCKS, LANES)
    right = jnp.where(low, y, after).reshape(POSITIONS * NBLOCKS, LANES)
    window = jnp.concatenate([left, right], axis=1)
    height = POSITIONS * NBLOCKS
    high = rounded(window)
    both = jnp.concatenate([high, window - high], axis=0).astype(jnp.bfloat16)
    for k in range(NPROF):
        table = col_ref[:, k * LANES : (k + 1) * LANES]
        rest = col_ref[:, (NPROF + k) * LANES : (NPROF + k + 1) * LANES]
        main = jnp.dot(both, table, preferred_element_type=jnp.float32)
        more = jnp.dot(both[0:height], rest, preferred_element_type=jnp.float32)
        cols[k * height : (k + 1) * height, :] = main[0:height] + (main[height:] + more)

    def one_block(b, total):
        at = pl.multiple_of(b * LANES, LANES)
        c = jnp.concatenate(
            [
                cols[pl.ds(k * height + b, POSITIONS, stride=NBLOCKS), :]
                for k in range(NPROF)
            ],
            axis=1,
        )
        high = rounded(c)
        blank = jnp.zeros((8, NPROF * LANES), jnp.float32)
        stacked = jnp.concatenate([high, c - high, high, blank], axis=0).astype(jnp.bfloat16)
        d = jnp.dot(row_ref[...], stacked, preferred_element_type=jnp.float32)
        science = sci_ref[step, 0, :, pl.ds(at, LANES)]
        usable = (1 - bad_ref[step, 0, :, pl.ds(at, LANES)]).astype(jnp.float32)
        tile_var = ag_flat[pl.ds((slot * 56 + VAR_AT) * NBLOCKS + b, ROWS, stride=NBLOCKS), :]
        scale = usable / jnp.sqrt(svar_ref[step, 0, :, pl.ds(at, LANES)] + tile_var)
        spread = jnp.broadcast_to(scale[:, None, :], (ROWS, 8, LANES)).reshape(ROWS * 8, LANES)
        sci_spread = jnp.broadcast_to(science[:, None, :], (ROWS, 8, LANES)).reshape(ROWS * 8, LANES)
        place = lax.broadcasted_iota(jnp.int32, (ROWS * 8, LANES), 0) & 7
        parts = [d[:, k * LANES : (k + 1) * LANES] for k in range(NPROF)]
        parts[0] = jnp.where(place == SCI, sci_spread, parts[0])
        parts = [part * spread for part in parts]
        for k in range(NPROF):
            basis[slot, b, :, k * LANES : (k + 1) * LANES] = parts[k]

        def arranged(pieces):
            return jnp.concatenate(
                [
                    jnp.concatenate([piece[h * 8 : h * 8 + 8] for piece in pieces], axis=0)
                    for h in range(ROWS)
                ],
                axis=1,
            ).astype(jnp.bfloat16)

        highs = [rounded(part) for part in parts]
        rests = [part - h for part, h in zip(parts, highs)]
        return total + lax.dot_general(
            arranged(highs + rests),
            arranged(highs),
            (((1,), (1,)), ((), ())),
            preferred_element_type=jnp.float32,
        )

    total = lax.fori_loop(0, NBLOCKS, one_block, jnp.zeros((80, 40), jnp.float32), unroll=4)
    return total[0:40] + (total[40:80] + total[40:80].T)


def packed(mat):
    wide = jnp.concatenate([mat, jnp.zeros((40, LANES - 40), jnp.float32)], axis=1)
    first = wide[0:8] + pltpu.roll(wide[8:16], 40, 1) + pltpu.roll(wide[16:24], 80, 1)
    return jnp.concatenate([first, wide[24:32] + pltpu.roll(wide[32:40], 40, 1)], axis=0)


def unpacked(tiles):
    first, second = tiles[0:8], tiles[8:16]
    return jnp.concatenate(
        [
            first,
            pltpu.roll(first, LANES - 40, 1),
            pltpu.roll(first, LANES - 80, 1),
            second,
            pltpu.roll(second, LANES - 40, 1),
        ],
        axis=0,
    )


def solve(mats):
    row = lax.broadcasted_iota(jnp.int32, (40, LANES), 0)
    col = lax.broadcasted_iota(jnp.int32, (40, LANES), 1)
    mats = [m + jnp.where(row == col, RIDGE, 0.0) for m in mats]
    for k in range(NPROF):
        pivots = [k * 8 + l for l in range(NPROF)]
        for s, m in enumerate(mats):
            columns = [jnp.broadcast_to(m[:, p : p + 1], (40, LANES)) for p in pivots]
            for i, p in enumerate(pivots):
                ours = columns[i]
                inverse = 1.0 / ours[p : p + 1]
                pivot = m[p : p + 1] * inverse
                m = jnp.where(row == p, pivot, m - ours * pivot)
                for j in range(i + 1, NPROF):
                    other = columns[j][p : p + 1] * inverse
                    columns[j] = jnp.where(row == p, other, columns[j] - ours * other)
            mats[s] = m
    return [
        jnp.where(row == SCI, -1.0, jnp.broadcast_to(m[:, SCI : SCI + 1], (40, LANES)))
        for m in mats
    ]


def kernel(
    owners, temp_hbm, sci_hbm, svar_hbm, bad_hbm, col_hbm, row_hbm, out_ref,
    temp_ref, sci_ref, svar_ref, bad_ref, col_ref, row_ref, load_sem,
    mine, recv1, send2, recv2, ag, red, cols, basis, fitted,
    ssem1, same_sem, cross_sem, ssem2, rsem2, static_send, static_recv, ssem3, rsem3, ssem4, rsem4, passed, known,
):
    v = lax.axis_index("visit")
    p = lax.axis_index("patch")
    group = v // GROUP
    cls = v % GROUP
    depth = v // 2
    side = v % 2
    deep = cls // 2

    def near(dz, dx):
        return ((depth + dz + DEPTHS) % DEPTHS) * 2 + (side + dx) % 2

    def holder(t):
        return ((depth + (t // 2 - deep + 5) % 4 - 1 + DEPTHS) % DEPTHS) * 2 + t % 2

    loads = [
        pltpu.make_async_copy(src, dst, load_sem.at[i])
        for i, (src, dst) in enumerate(
            (
                (temp_hbm, temp_ref),
                (col_hbm, col_ref),
                (row_hbm, row_ref),
                (svar_hbm, svar_ref),
                (bad_hbm, bad_ref),
                (sci_hbm, sci_ref),
            )
        )
    ]
    for load in loads:
        load.start()

    recv1[...] = jnp.zeros_like(recv1)

    barrier = pltpu.get_barrier_semaphore()

    def greet(vv, pp):
        pl.semaphore_signal(barrier, inc=1, device_id=(vv, pp), device_id_type=MESH)

    for d in (1, 3):
        greet(((group + d) % NGROUPS) * GROUP + cls, p)
    for dz in range(-2, 3):
        for dx in range(2):
            if (dz, dx) != (0, 0):
                greet(near(dz, dx), p)
    for d in (1, NPATCH - 1):
        greet(v, (p + d) % NPATCH)

    @pl.when((cls < 2) & (p > 0))
    def _():
        for dz in range(-2, 2):
            for dx in range(2):
                if (dz, dx) != (0, 0):
                    greet(near(dz, dx), p - 1)

    @pl.when(((cls == 4) | (cls == 5)) & (p < NPATCH - 1))
    def _():
        for dz in range(-2, 2):
            for dx in range(2):
                if (dz, dx) != (0, 0):
                    greet(near(dz, dx), p + 1)

    below = jnp.where(p < NPATCH - 1, jnp.where(cls < 2, 1, 2), 0)
    above = jnp.where(p > 0, jnp.where((cls == 4) | (cls == 5), 1, 2), 0)
    loads[0].wait()
    flat = mine.reshape(2 * ROWS * NBLOCKS, LANES)
    for kind in range(2):
        for half in range(2):
            for b in range(NBLOCKS):
                flat[pl.ds((kind * ROWS + half * 8) * NBLOCKS + b, 8, stride=NBLOCKS), :] = temp_ref[
                    0, kind, half * 8 : half * 8 + 8, b * LANES : (b + 1) * LANES
                ]

    pl.semaphore_wait(barrier, 9 + 2 + 2 + below + above)

    pl.semaphore_signal(
        passed,
        inc=1,
        device_id=(((group + 1) % NGROUPS) * GROUP + cls, p),
        device_id_type=MESH,
    )

    def first_copy(i):
        t, dp, at, n, to = PARTS[i]
        return pltpu.make_async_remote_copy(
            src_ref=mine.at[pl.ds(at, n)],
            dst_ref=recv1.at[pl.ds((((deep - t // 2 + 2) & 3) * 2 + side) * SLOT + to, n)],
            send_sem=ssem1.at[i],
            recv_sem=same_sem if dp == 0 else cross_sem,
            device_id=(holder(t), p + dp),
            device_id_type=MESH,
        )

    def sends(i):
        t, dp = PARTS[i][:2]
        if dp == 0:
            return cls != t
        return p < NPATCH - 1 if dp == 1 else p > 0

    for i in range(len(PARTS)):

        @pl.when(sends(i))
        def _(i=i):
            first_copy(i).start()

    def spread_word(r):
        for d in (1 << r, NPATCH - (1 << r)):
            pl.semaphore_signal(
                known.at[r], inc=1, device_id=(v, (p + d) % NPATCH), device_id_type=MESH
            )

    spread_word(0)

    for t, dp, at, n, to in PARTS:

        @pl.when(cls == t)
        def _(t=t, dp=dp, at=at, n=n, to=to):
            if dp == 0:
                recv1[pl.ds((4 + t % 2) * SLOT + to, n)] = mine[pl.ds(at, n)]

    for t, dp, at, n, to in PARTS:
        if dp == 0:

            @pl.when(cls == t)
            def _(n=n):
                rows = recv1.at[pl.ds(0, (GROUP - 1) * n)]
                pltpu.make_async_copy(rows, rows, same_sem).wait()

        else:

            @pl.when((cls == t) & (p > 0 if dp == 1 else p < NPATCH - 1))
            def _(n=n):
                rows = recv1.at[pl.ds(0, GROUP * n)]
                pltpu.make_async_copy(rows, rows, cross_sem).wait()

    own = pl.ds(cls * SLOT, SLOT)
    fixed = pl.ds((((FIXED // 2 + 2 - deep) & 3) * 2 + FIXED % 2) * SLOT, SLOT)
    fixed_group = ((FIXED // 2 + 2 - deep) & (DEPTHS - 1)) >> 2
    from_fixed = group == fixed_group

    def static_copy(g):
        return pltpu.make_async_remote_copy(
            src_ref=recv1.at[fixed],
            dst_ref=ag.at[0, own],
            send_sem=static_send.at[g],
            recv_sem=static_recv,
            device_id=(((group + g) % NGROUPS) * GROUP + cls, p),
            device_id_type=MESH,
        )

    pl.semaphore_wait(passed, 1)

    @pl.when(from_fixed)
    def _():
        for d in (2, 1, 3):
            static_copy(d).start()
        ag[0, own] = recv1[fixed]

    other = owners[0] + owners[1] - FIXED
    far = (other >> 1) + 2 - deep
    chosen = recv1[pl.ds(((far & 3) * 2 + (other & 1)) * SLOT, SLOT)]
    send2[...] = chosen
    recv2[pl.ds(group * SLOT, SLOT)] = chosen

    def second_copy(d):
        return pltpu.make_async_remote_copy(
            src_ref=send2,
            dst_ref=recv2.at[pl.ds(group * SLOT, SLOT)],
            send_sem=ssem2,
            recv_sem=rsem2,
            device_id=(((group + d) % NGROUPS) * GROUP + cls, p),
            device_id_type=MESH,
        )

    for d in (2, 1, 3):
        second_copy(d).start()
    pl.semaphore_wait(known.at[0], 2)
    spread_word(1)

    def third_copy(slot, d):
        dz, dx, at, n = SPREAD[d]
        rows = pl.ds(cls * SLOT + at, n)
        return pltpu.make_async_remote_copy(
            src_ref=ag.at[slot, rows],
            dst_ref=ag.at[slot, rows],
            send_sem=ssem3.at[slot],
            recv_sem=rsem3.at[slot],
            device_id=(near(dz, dx), p),
            device_id_type=MESH,
        )

    @pl.when(group != fixed_group)
    def _():
        pltpu.make_async_copy(ag.at[0, own], ag.at[0, own], static_recv).wait()

    for d in range(len(SPREAD)):
        third_copy(0, d).start()
    three = recv2.at[pl.ds(0, (NGROUPS - 1) * SLOT)]
    pltpu.make_async_copy(three, three, rsem2).wait()
    ag[1, own] = recv2[pl.ds(((far >> 2) & 3) * SLOT, SLOT)]
    for d in range(len(SPREAD)):
        third_copy(1, d).start()
    pl.semaphore_wait(known.at[1], 2)
    spread_word(2)

    ag_flat = ag.reshape(STEPS * 56 * NBLOCKS, LANES)
    fixed_step = jnp.where(owners[1] == FIXED, 1, 0)
    for load in loads[1:]:
        load.wait()

    def fourth_copy(slot, d):
        return pltpu.make_async_remote_copy(
            src_ref=red.at[slot, p],
            dst_ref=red.at[slot, p],
            send_sem=ssem4.at[slot],
            recv_sem=rsem4.at[slot],
            device_id=(v, (p + d) % NPATCH),
            device_id_type=MESH,
        )

    for slot in range(STEPS):
        rows = ag.at[slot, pl.ds(0, (GROUP - 1) * SLOT)]
        pltpu.make_async_copy(rows, rows, rsem3.at[slot]).wait()
        step = fixed_step if slot == 0 else 1 - fixed_step
        red[slot, p] = packed(
            normal_part(slot, step, ag, ag_flat, cols, basis, col_ref, row_ref, sci_ref, svar_ref, bad_ref)
        )
        if slot == 0:
            pl.semaphore_wait(known.at[2], 2)
        for d in range(1, NPATCH):
            fourth_copy(slot, d).start()

    for i in range(len(PARTS)):

        @pl.when(sends(i))
        def _(i=i):
            first_copy(i).wait_send()

    @pl.when(from_fixed)
    def _():
        for d in range(1, NGROUPS):
            static_copy(d).wait_send()

    pltpu.make_async_copy(three, three, ssem2).wait()
    for slot in range(STEPS):
        rows = ag.at[slot, pl.ds(0, (GROUP - 1) * SLOT)]
        pltpu.make_async_copy(rows, rows, ssem3.at[slot]).wait()

    def coefs(slot):
        rows = red.at[slot, pl.ds(0, NPATCH - 1)]
        pltpu.make_async_copy(rows, rows, rsem4.at[slot]).wait()
        total = red[slot, 0]
        for q in range(1, NPATCH):
            total = total + red[slot, q]
        return solve([unpacked(total)])[0]

    def fit(slot, coef, b):
        sums = jnp.zeros((ROWS, 8, LANES), jnp.float32)
        for k in range(NPROF):
            d = basis[slot, b, :, k * LANES : (k + 1) * LANES].reshape(ROWS, 8, LANES)
            sums = sums + d * coef[k * 8 : k * 8 + 8][None]
        return -jnp.sum(sums, axis=1)

    coef0 = coefs(0)

    def fixed_block(b, carry):
        fitted[:, pl.ds(pl.multiple_of(b * LANES, LANES), LANES)] = fit(0, coef0, b)
        return carry

    lax.fori_loop(0, NBLOCKS, fixed_block, 0, unroll=4)
    coef1 = coefs(1)

    def other_block(b, carry):
        at = pl.multiple_of(b * LANES, LANES)
        ours, theirs = fitted[:, pl.ds(at, LANES)], fit(1, coef1, b)
        for step in range(STEPS):
            out_ref[step, 0, :, pl.ds(at, LANES)] = jnp.where(fixed_step == step, ours, theirs)
        return carry

    lax.fori_loop(0, NBLOCKS, other_block, 0, unroll=4)
    for slot in range(STEPS):
        rows = red.at[slot, pl.ds(0, NPATCH - 1)]
        pltpu.make_async_copy(rows, rows, ssem4.at[slot]).wait()


def shards(templates, owners, science, sci_var, bad_pixels):
    hbm = pl.BlockSpec(memory_space=pltpu.HBM)
    row_shape = (NBLOCKS, LANES)
    dma = pltpu.SemaphoreType.DMA
    col_table, rows_table = jnp.asarray(column_table()), jnp.asarray(row_table())
    operands = (templates, science, sci_var, bad_pixels, col_table, rows_table)
    return pl.pallas_call(
        kernel,
        out_shape=jax.ShapeDtypeStruct(science.shape, jnp.float32),
        in_specs=[pl.BlockSpec(memory_space=pltpu.SMEM)] + [hbm] * len(operands),
        out_specs=pl.BlockSpec(memory_space=pltpu.VMEM),
        scratch_shapes=[pltpu.VMEM(x.shape, x.dtype) for x in operands]
        + [
            dma((len(operands),)),
            pltpu.VMEM((2 * ROWS, *row_shape), jnp.float32),
            pltpu.VMEM((GROUP * SLOT, *row_shape), jnp.float32),
            pltpu.VMEM((SLOT, *row_shape), jnp.float32),
            pltpu.VMEM((NGROUPS * SLOT, *row_shape), jnp.float32),
            pltpu.VMEM((STEPS, GROUP * SLOT, *row_shape), jnp.float32),
            pltpu.VMEM((STEPS, NPATCH, 16, LANES), jnp.float32),
            pltpu.VMEM((NPROF * POSITIONS * NBLOCKS, LANES), jnp.float32),
            pltpu.VMEM((STEPS, NBLOCKS, ROWS * 8, NPROF * LANES), jnp.float32),
            pltpu.VMEM((ROWS, NBLOCKS * LANES), jnp.float32),
            dma((len(PARTS),)),
            dma,
            dma,
            dma,
            dma,
            dma((NGROUPS,)),
            dma,
            dma((STEPS,)),
            dma((STEPS,)),
            dma((STEPS,)),
            dma((STEPS,)),
            pltpu.SemaphoreType.REGULAR,
            pltpu.SemaphoreType.REGULAR((3,)),
        ],
        compiler_params=pltpu.CompilerParams(
            collective_id=0, has_side_effects=True, vmem_limit_bytes=60 * 1024 * 1024
        ),
        name="difference",
    )(owners, *operands)


def solution(mesh):
    return jax.shard_map(
        shards,
        mesh=mesh,
        in_specs=(
            P("visit", None, "patch", None),
            P(),
            P(None, "visit", "patch", None),
            P(None, "visit", "patch", None),
            P(None, "visit", "patch", None),
        ),
        out_specs=P(None, "visit", "patch", None),
        check_vma=False,
    )
```
